32 devices in a mesh: az: 8 (over z, core), el: 4 (over y, x).
Axes of the slice: x: 2, y: 2, z: 4, core: 2. Of those that a mesh axis runs over, the one named last changes fastest.
Arguments:
- points: bfloat16 [8, 2048, 256], P('el', 'az'), may hold values from -6 to 6
- skip: bfloat16 [8, 2048, 256], P('el', 'az'), may hold values from -6 to 6
- tokens: bfloat16 [8, 4, 128, 256], P('az', 'el')
- send_slots: int32 [8, 4, 5, 4, 16], P('az', 'el'), may hold values from 0 to 127
- recv_idx: int32 [8, 2048, 16], P('el', 'az'), may hold values from 0 to 319, as said below
- w_query: bfloat16 [256, 256], replicated, may hold values from -0.375 to 0.375
- w_key: bfloat16 [256, 256], replicated, may hold values from -0.375 to 0.375
- w_value: bfloat16 [256, 256], replicated, may hold values from -0.375 to 0.375
- w_out: bfloat16 [256, 256], replicated, may hold values from -0.375 to 0.375
- w_hid: bfloat16 [256, 1024], replicated, may hold values from -0.375 to 0.375
- w_skip: bfloat16 [256, 1024], replicated, may hold values from -0.375 to 0.375
- w_down: bfloat16 [1024, 256], replicated, may hold values from -0.1875 to 0.1875
- w_conv: bfloat16 [9, 256, 256], replicated, may hold values from -0.125 to 0.125
Outputs:
- refined: bfloat16 [8, 2048, 256], P('el', 'az')
The draws below stay inside these ranges and needn't reach their ends.
Inputs may be any that keep to these rules, and one draw needn't show every extreme that they name: send_slots[o, e, j, f, k] is the row of owner device (o, e)'s tokens sent as slot k to the device of azimuth block (o + j - 2) mod 8 and elevation block f. `recv_idx`: an entry (j * 4 + e) * 16 + k names slot k of what the device of elevation block e, 2 - j azimuth blocks away, sends to the point's device. For each requesting device and each such owner only the slots below a live count of 1 to 16 are named; each requesting device has its own block's slots from itself all live.
All inputs are finite; a program needn't handle non-finite values.
Results may differ from the reference program's by a relative error of at most 0.01.
Values may be sent and summed in bfloat16 or wider, within the bound.
No kernel may reach another device: no remote copies, remote signals or barrier semaphores. Data moves between devices by JAX's collectives and lax.ppermute only.
A program may use at most 64 MiB of HBM per device.

```python
import math
import jax
import jax.numpy as jnp
from jax import lax

D = 256
HEADS = 8
FF = 1024
NEAR = 16
REACH = 2
R_DEV = 2
C_DEV = 256
TOK_DEV = 128
CAP = 16
OFFSETS = 5
AZ_BLOCKS = 8
EL_BLOCKS = 4
ROWS = 8
COLS = 2048


def draw_tokens(key, part):
    shape = (AZ_BLOCKS, EL_BLOCKS, TOK_DEV, D)
    first = jax.random.fold_in(key, 0)
    return jax.random.normal(first, shape, jnp.float32).astype(jnp.bfloat16)


def draw_recv_idx(key, part):
    keys = jax.random.split(key, 4)
    live_counts = jax.random.randint(keys[0], (EL_BLOCKS, AZ_BLOCKS, OFFSETS, EL_BLOCKS), 1, CAP + 1)
    own_group = (jnp.arange(OFFSETS)[None, None, :, None] == REACH) & (jnp.arange(EL_BLOCKS)[:, None, None, None] == jnp.arange(EL_BLOCKS)[None, None, None, :])
    live_counts = jnp.where(own_group, CAP, live_counts)
    shape = (ROWS, COLS, NEAR)
    group = jax.random.randint(keys[1], shape, 0, OFFSETS)
    source_el = jax.random.randint(keys[2], shape, 0, EL_BLOCKS)
    raw_slot = jax.random.randint(keys[3], shape, 0, 1 << 20)
    target_el = (jnp.arange(ROWS) // R_DEV)[:, None, None]
    column_block = (jnp.arange(COLS) // C_DEV)[None, :, None]
    limit = live_counts[target_el, column_block, group, source_el]
    slot_number = raw_slot % limit
    return ((group * EL_BLOCKS + source_el) * CAP + slot_number).astype(jnp.int32)


def with_ends(array, own_key, least, top_value):
    place = [jax.random.randint(jax.random.fold_in(own_key, axis), (), 0, length) for axis, length in enumerate(array.shape)]
    main_axis = array.shape.index(max(array.shape))
    beside = place[:main_axis] + [(place[main_axis] + 1) % array.shape[main_axis]] + place[main_axis + 1:]
    return array.at[tuple(place)].set(least).at[tuple(beside)].set(top_value)


def steps_of(key, shape, cuts, smallest, top_value):
    level = 1.0
    for dim, parts in cuts:
        draws = jax.random.uniform(jax.random.fold_in(jax.random.fold_in(key, 6), dim), (parts,), jnp.float32, smallest / len(cuts), top_value / len(cuts))
        level = level * jnp.repeat(jnp.exp(draws), shape[dim] // parts).reshape((-1,) + (1,) * (len(shape) - 1 - dim))
    return level


def normal_values(key, extent, width, most, cuts=(), kind=jnp.bfloat16):
    entries = jax.random.normal(key, extent, jnp.float32) * width
    if len(cuts) > 0:
        entries = steps_of(key, extent, cuts, -0.22, 0.18) * entries
    return jnp.clip(entries, min=-most, max=most).astype(kind)


def setup_inputs(seed: int = 0) -> dict:
    seeds = jax.random.split(jax.random.key(seed), 14)
    points = normal_values(seeds[0], (ROWS, COLS, D), 1.0, 6.0, ((0, 4), (1, 8)))
    skip = normal_values(seeds[1], (ROWS, COLS, D), 1.0, 6.0, ((0, 4), (1, 8)))
    tokens = draw_tokens(jax.random.fold_in(seeds[13], 71), 0)
    send_slots = with_ends(jax.random.randint(seeds[3], (AZ_BLOCKS, EL_BLOCKS, OFFSETS, EL_BLOCKS, CAP), 0, TOK_DEV), jax.random.fold_in(seeds[3], 1), 0, TOK_DEV - 1).astype(jnp.int32)
    recv_idx = draw_recv_idx(jax.random.fold_in(seeds[13], 71), 0)
    w_query = normal_values(seeds[5], (D, D), D ** -0.5, 0.375)
    w_key = normal_values(seeds[6], (D, D), D ** -0.5, 0.375)
    w_value = normal_values(seeds[7], (D, D), D ** -0.5, 0.375)
    w_out = normal_values(seeds[8], (D, D), D ** -0.5, 0.375)
    w_hid = normal_values(seeds[9], (D, FF), D ** -0.5, 0.375)
    w_skip = normal_values(seeds[10], (D, FF), D ** -0.5, 0.375)
    w_down = normal_values(seeds[11], (FF, D), FF ** -0.5, 0.1875)
    w_conv = normal_values(seeds[12], (9, D, D), (9 * D) ** -0.5, 0.125)
    return dict(points=points, skip=skip, tokens=tokens, send_slots=send_slots, recv_idx=recv_idx, w_query=w_query, w_key=w_key, w_value=w_value, w_out=w_out, w_hid=w_hid, w_skip=w_skip, w_down=w_down, w_conv=w_conv)


def normalize(features):
    widened = features.astype(jnp.float32)
    return widened * lax.rsqrt(lax.optimization_barrier(jnp.mean(widened * widened, axis=-1, keepdims=True)) + 1e-06)

def reference(points, skip, tokens, send_slots, recv_idx, w_query, w_key, w_value, w_out, w_hid, w_skip, w_down, w_conv):
    flat_tokens = tokens.reshape(AZ_BLOCKS * EL_BLOCKS * TOK_DEV, D)
    key_rows = jnp.dot(flat_tokens, w_key, preferred_element_type=jnp.float32).astype(jnp.bfloat16)
    normed_tokens = normalize(flat_tokens).astype(jnp.bfloat16)
    value_rows = jnp.dot(normed_tokens, w_value, preferred_element_type=jnp.float32).astype(jnp.bfloat16)
    head_width = D // HEADS
    scale_factor = 1.0 / math.sqrt(head_width)
    column_block = jnp.arange(COLS, dtype=jnp.int32) // C_DEV

    def one_row(inputs):
        point_row, skip_row, index_row, row_number = inputs
        group = index_row // (EL_BLOCKS * CAP)
        source_el = index_row // CAP % EL_BLOCKS
        slot_number = index_row % CAP
        owner = (column_block[:, None] - group + REACH) % AZ_BLOCKS
        target_el = row_number // R_DEV
        local_row = send_slots[owner, source_el, group, target_el, slot_number]
        token_id = ((owner * EL_BLOCKS + source_el) * TOK_DEV + local_row).astype(jnp.int32)
        picked_keys = jnp.take(key_rows, token_id, axis=0).reshape(COLS, NEAR, HEADS, head_width)
        picked_values = jnp.take(value_rows, token_id, axis=0).reshape(COLS, NEAR, HEADS, head_width)
        query = jnp.dot(point_row, w_query, preferred_element_type=jnp.float32).astype(jnp.bfloat16)
        query = query.reshape(COLS, HEADS, head_width)
        scores = jnp.einsum('bhd,bkhd->bhk', query.astype(jnp.float32), picked_keys.astype(jnp.float32)) * scale_factor
        shifted = jnp.exp(scores - lax.optimization_barrier(jnp.max(scores, axis=-1, keepdims=True)))
        weights = (shifted / lax.optimization_barrier(jnp.sum(shifted, axis=-1, keepdims=True))).astype(jnp.bfloat16)
        combined = jnp.einsum('bhk,bkhd->bhd', weights.astype(jnp.float32), picked_values.astype(jnp.float32))
        attended = combined.reshape(COLS, D).astype(jnp.bfloat16)
        residual_sum = point_row.astype(jnp.float32) + jnp.dot(attended, w_out, preferred_element_type=jnp.float32)
        normed = normalize(residual_sum).astype(jnp.bfloat16)
        hidden_pre = jnp.dot(normed, w_hid, preferred_element_type=jnp.float32) + jnp.dot(skip_row, w_skip, preferred_element_type=jnp.float32)
        inner = jax.nn.gelu(hidden_pre, approximate=True).astype(jnp.bfloat16)
        return residual_sum + jnp.dot(inner, w_down, preferred_element_type=jnp.float32)
    joined = lax.map(one_row, (points, skip, recv_idx, jnp.arange(ROWS, dtype=jnp.int32)))
    conv_input = normalize(joined).astype(jnp.bfloat16)
    widened = jnp.concatenate([conv_input[:, -1:], conv_input, conv_input[:, :1]], axis=1)
    padded = jnp.pad(widened, ((1, 1), (0, 0), (0, 0)))
    refined = joined
    for tap_index in range(9):
        row_step = tap_index // 3
        col_step = tap_index % 3
        window = padded[row_step:row_step + ROWS, col_step:col_step + COLS].reshape(ROWS * COLS, D)
        refined = refined + jnp.dot(window, w_conv[tap_index], preferred_element_type=jnp.float32).reshape(ROWS, COLS, D)
    return refined.astype(jnp.bfloat16)
```

```python
import functools
import math

import jax
import jax.numpy as jnp
from jax import lax
from jax.experimental import pallas as pl
from jax.experimental.pallas import tpu as pltpu
from jax.sharding import PartitionSpec as P

HEADS = 8
REACH = 2
BF16 = jnp.bfloat16
F32 = jnp.float32
VMEM = pltpu.VMEM
SMEM = pltpu.SMEM


def ring(x, axis, by):
    length = lax.axis_size(axis)
    return lax.ppermute(x, axis, [(i, (i + by) % length) for i in range(length)])


def line(x, axis, by):
    length = lax.axis_size(axis)
    return lax.ppermute(
        x, axis, [(i, i + by) for i in range(length) if 0 <= i + by < length]
    )


def dot(a, b, contract=((1,), (0,))):
    return lax.dot_general(a, b, (contract, ((), ())), preferred_element_type=F32)


def rms(x):
    return x * lax.rsqrt(jnp.mean(x * x, axis=-1, keepdims=True) + 1e-06)


def call(body, outs, ins, name, cost, spaces=None, scratch=()):
    spaces = spaces or [VMEM] * len(ins)
    flops, transcendentals = cost
    moved = sum(x.size * x.dtype.itemsize for x in list(ins) + list(outs))
    return pl.pallas_call(
        body,
        out_shape=outs,
        in_specs=[pl.BlockSpec(memory_space=s) for s in spaces],
        out_specs=[pl.BlockSpec(memory_space=VMEM) for _ in outs],
        scratch_shapes=list(scratch),
        compiler_params=pltpu.CompilerParams(vmem_limit_bytes=32 * 1024 * 1024),
        cost_estimate=pl.CostEstimate(
            flops=flops, bytes_accessed=moved, transcendentals=transcendentals
        ),
        name=name,
    )(*ins)


def gather_body(me_ref, tokens_ref, slots_ref, *out_refs):
    groups = slots_ref.shape[1]
    offsets, capacity = slots_ref.shape[0], slots_ref.shape[2]
    rows = tokens_ref.shape[0]
    me = me_ref[0]
    tokens = tokens_ref[...]
    eye = (
        lax.broadcasted_iota(jnp.int32, (capacity, capacity), 0)
        == lax.broadcasted_iota(jnp.int32, (capacity, capacity), 1)
    )
    lane = lax.broadcasted_iota(jnp.int32, (capacity, rows), 1).astype(F32)
    for step in range(groups):
        target = lax.rem(me + step, groups)
        picks = []
        for offset in range(offsets):
            row = slots_ref[offset, pl.ds(target, 1), :].astype(F32)
            spread = jnp.broadcast_to(row, (capacity, capacity))
            column = jnp.sum(jnp.where(eye, spread, 0.0), axis=-1, keepdims=True)
            picks.append(jnp.where(column == lane, 1.0, 0.0))
        one_hot = jnp.concatenate(picks, axis=0).astype(BF16)
        chosen = dot(one_hot, tokens).astype(BF16)
        out_refs[step][...] = chosen.reshape(out_refs[step].shape)


def prepare_body(me_ref, points_ref, idx_ref, w_query_ref, q_ref, bias_ref, idx_t_ref, *, groups, capacity):
    count, width = q_ref.shape[1], q_ref.shape[0]
    me = me_ref[0]
    points = points_ref[...].reshape(count, width)
    scale = math.log2(math.e) / math.sqrt(width // HEADS)
    query = dot(points, w_query_ref[...]) * scale
    q_ref[...] = query.T.astype(BF16)
    near = idx_ref.shape[-1]
    idx_t_ref[...] = idx_ref[...].reshape(count, near).T
    lanes = 128
    for step in range(groups):
        source = lax.rem(me + groups - step, groups)
        for offset in range(bias_ref.shape[0] // (groups * capacity)):
            first = (offset * groups + source) * capacity
            slot = first + lax.broadcasted_iota(jnp.int32, (capacity, lanes), 0)
            place = (offset * groups + step) * capacity
            for start in range(0, count, lanes):
                total = jnp.zeros((capacity, lanes), F32)
                for n in range(near):
                    index = idx_t_ref[n : n + 1, start : start + lanes]
                    total = total + jnp.where(slot == index, 1.0, 0.0)
                bias_ref[place : place + capacity, start : start + lanes] = jnp.log2(total)


def main_body(
    *refs, pieces
):
    piece_refs = refs[:pieces]
    (
        q_ref,
        bias_ref,
        points_ref,
        skip_ref,
        w_key_ref,
        w_value_ref,
        w_out_ref,
        w_hid_ref,
        w_skip_ref,
        w_down_ref,
        joined_ref,
        first_ref,
        second_ref,
        left_ref,
        right_ref,
        att_ref,
    ) = refs[pieces:]
    width, count = q_ref.shape
    head_width = width // HEADS
    received = jnp.concatenate(
        [r[...].reshape(-1, width) for r in piece_refs], axis=0
    )
    table = received.shape[0]
    keys = dot(received, w_key_ref[...]).astype(BF16)
    normed_tokens = rms(received.astype(F32)).astype(BF16)
    values_t = dot(w_value_ref[...], normed_tokens, ((0,), (1,))).astype(BF16)
    ones = jnp.ones((16, table), BF16)
    for head in range(HEADS):
        low, high = head * head_width, (head + 1) * head_width
        scores = dot(keys[:, low:high], q_ref[low:high, :]) + bias_ref[...]
        top = jnp.max(scores, axis=0, keepdims=True)
        weights = jnp.exp2(scores - top).astype(BF16)
        lhs = jnp.concatenate([values_t[low:high, :], ones], axis=0)
        mixed = dot(lhs, weights)
        att_ref[low:high, :] = (mixed[:head_width] / mixed[head_width : head_width + 1]).astype(BF16)
    points = points_ref[...].reshape(count, width).astype(F32)
    residual = points + dot(att_ref[...], w_out_ref[...], ((0,), (0,)))
    normed = rms(residual).astype(BF16)
    skip = skip_ref[...].reshape(count, width)
    pre = dot(normed, w_hid_ref[...]) + dot(skip, w_skip_ref[...])
    c1 = math.sqrt(2.0 / math.pi)
    half = 0.5 * pre
    inner = (half + half * jnp.tanh(pre * (c1 + (c1 * 0.044715) * (pre * pre)))).astype(BF16)
    joined = residual + dot(inner, w_down_ref[...])
    conv = rms(joined).astype(BF16)
    joined_ref[...] = joined.reshape(joined_ref.shape)
    cols = count // 2
    first_ref[...] = conv[:cols]
    second_ref[...] = conv[cols:]
    left_ref[0:1, :] = conv[0:1]
    left_ref[1:2, :] = conv[cols : cols + 1]
    right_ref[0:1, :] = conv[cols - 1 : cols]
    right_ref[1:2, :] = conv[2 * cols - 1 : 2 * cols]


def shifted(x, by):
    rolled = pltpu.roll(x, by % x.shape[0], 0)
    row = lax.broadcasted_iota(jnp.int32, x.shape, 0)
    edge = 0 if by > 0 else x.shape[0] - 1
    return jnp.where(row == edge, 0.0, rolled)


def inside_body(first_ref, second_ref, joined_ref, w_conv_ref, out_ref):
    first, second = first_ref[...], second_ref[...]
    for r in range(2):
        taps = []
        for dc in range(3):
            taps.append(
                dot(first, w_conv_ref[3 * (1 - r) + dc])
                + dot(second, w_conv_ref[3 * (2 - r) + dc])
            )
        out_ref[r] = joined_ref[r] + taps[1] + shifted(taps[0], 1) + shifted(taps[2], -1)


def border_body(
    above_ref, below_ref, left_ref, right_ref, corner_up_ref, corner_down_ref, part_ref, w_conv_ref, out_ref
):
    cols, width = above_ref.shape
    row = lax.broadcasted_iota(jnp.int32, (cols, width), 0)
    sides = []
    for side, (ref, at) in enumerate(((left_ref, 0), (right_ref, 1))):
        ends = jnp.concatenate(
            [corner_up_ref[at : at + 1, :], ref[...], corner_down_ref[at : at + 1, :], jnp.zeros((12, width), BF16)],
            axis=0,
        )
        sides.append([dot(ends, w_conv_ref[3 * dr + 2 * side]) for dr in range(3)])
    for r, ref in enumerate((above_ref, below_ref)):
        x = ref[...]
        taps = [dot(x, w_conv_ref[6 * r + dc]) for dc in range(3)]
        total = part_ref[r] + taps[1] + shifted(taps[0], 1) + shifted(taps[2], -1)
        for side in range(2):
            e = sides[side]
            extra = e[0][r : r + 1] + e[1][r + 1 : r + 2] + e[2][r + 2 : r + 3]
            total = total + jnp.where(row == (0, cols - 1)[side], extra, 0.0)
        out_ref[r] = total.astype(BF16)


def per_device(
    points,
    skip,
    tokens,
    send_slots,
    recv_idx,
    w_query,
    w_key,
    w_value,
    w_out,
    w_hid,
    w_skip,
    w_down,
    w_conv,
):
    rows, cols, width = points.shape
    count = rows * cols
    own_tokens = tokens[0, 0]
    slots = send_slots[0, 0]
    offsets, groups, capacity = slots.shape
    table = offsets * groups * capacity
    me = lax.axis_index("el").astype(jnp.int32).reshape(1)
    shape = jax.ShapeDtypeStruct
    sent = call(
        gather_body,
        [shape((offsets, capacity, width), BF16)] * groups,
        [me, own_tokens, slots],
        "gather",
        (2 * table * own_tokens.shape[0] * width, 0),
        [SMEM, VMEM, VMEM],
    )
    got = [sent[0]] + [ring(sent[s], "el", s) for s in range(1, groups)]
    query_t, bias = call(
        functools.partial(prepare_body, groups=groups, capacity=capacity),
        [shape((width, count), BF16), shape((table, count), F32)],
        [me, points, recv_idx, w_query],
        "prepare",
        (table * count * 48, table * count),
        [SMEM, VMEM, VMEM, VMEM],
        [pltpu.VMEM((recv_idx.shape[-1], count), jnp.int32)],
    )
    pieces = []
    for offset in range(offsets):
        bundle = jnp.concatenate([g[offset] for g in got], axis=0)
        pieces.append(bundle if offset == REACH else ring(bundle, "az", offset - REACH))
    joined, first, second, left, right = call(
        functools.partial(main_body, pieces=len(pieces)),
        [
            shape((rows, cols, width), F32),
            shape((cols, width), BF16),
            shape((cols, width), BF16),
            shape((2, width), BF16),
            shape((2, width), BF16),
        ],
        pieces
        + [query_t, bias, points, skip, w_key, w_value, w_out, w_hid, w_skip, w_down],
        "main",
        (10 * table * count * width + 2 * count * width * 13 * width, table * count * HEADS),
        None,
        [pltpu.VMEM((width, count), BF16)],
    )
    from_left = ring(right, "az", 1)
    from_right = ring(left, "az", -1)
    above = line(second, "el", 1)
    below = line(first, "el", -1)
    ends = jnp.stack([from_left, from_right], axis=1)
    corner_up = line(ends[1], "el", 1)
    corner_down = line(ends[0], "el", -1)
    (partial,) = call(
        inside_body,
        [shape((rows, cols, width), F32)],
        [first, second, joined, w_conv],
        "inside",
        (2 * count * width * width * 6, 0),
    )
    (out,) = call(
        border_body,
        [shape((rows, cols, width), BF16)],
        [above, below, from_left, from_right, corner_up, corner_down, partial, w_conv],
        "border",
        (2 * count * width * width * 3, 0),
    )
    return out


def solution(mesh):
    return jax.shard_map(
        per_device,
        mesh=mesh,
        in_specs=(
            P("el", "az", None),
            P("el", "az", None),
            P("az", "el", None, None),
            P("az", "el", None, None, None),
            P("el", "az", None),
            P(),
            P(),
            P(),
            P(),
            P(),
            P(),
            P(),
            P(),
        ),
        out_specs=P("el", "az", None),
        check_vma=False,
    )
```

```python
import functools
import math

import jax
import jax.numpy as jnp
from jax import lax
from jax.experimental import pallas as pl
from jax.experimental.pallas import tpu as pltpu
from jax.sharding import PartitionSpec as P

HEADS = 8
REACH = 2
PAD = 16
BF16 = jnp.bfloat16
F32 = jnp.float32
VMEM = pltpu.VMEM
SMEM = pltpu.SMEM
HBM = pltpu.HBM


def same_chip(i, n):
    return i ^ 1


def next_chip(i, n):
    return (i + 1 if i % 2 else i - 1) % n


def two_on(i, n):
    return (i + 2 if i // 2 % 2 == 0 else i - 2) % n


def two_back(i, n):
    return (i - 2 if i // 2 % 2 == 0 else i + 2) % n


def inner_pair(i, n):
    return i if i in (0, n - 1) else next_chip(i, n)


def swap(x, axis, partner):
    n = lax.axis_size(axis)
    return lax.ppermute(x, axis, [(i, partner(i, n)) for i in range(n)])


def sent_offset(az, piece):
    odd, odd_chip = lax.rem(az, 2), lax.rem(lax.div(az, 2), 2)
    return (REACH, 3 - 2 * odd, 1 + 2 * odd, 4 - 4 * odd_chip, 4 * odd_chip)[piece]


MATCHES = (None, same_chip, next_chip, two_on, two_back)


def dot(a, b, contract=((1,), (0,))):
    return lax.dot_general(a, b, (contract, ((), ())), preferred_element_type=F32)


def rms(x):
    return x * lax.rsqrt(jnp.mean(x * x, axis=-1, keepdims=True) + 1e-06)


def call(body, outs, ins, name, cost, spaces=None, scratch=(), aliases=None):
    spaces = spaces or [VMEM] * len(ins)
    flops, transcendentals = cost
    moved = sum(x.size * x.dtype.itemsize for x in list(ins) + list(outs))
    ins = [
        pltpu.with_memory_space_constraint(x, HBM) if s == HBM else x
        for x, s in zip(ins, spaces)
    ]
    return pl.pallas_call(
        body,
        out_shape=outs,
        in_specs=[pl.BlockSpec(memory_space=s) for s in spaces],
        out_specs=[pl.BlockSpec(memory_space=VMEM) for _ in outs],
        scratch_shapes=list(scratch),
        input_output_aliases=aliases or {},
        compiler_params=pltpu.CompilerParams(vmem_limit_bytes=20 * 1024 * 1024),
        cost_estimate=pl.CostEstimate(
            flops=flops, bytes_accessed=moved, transcendentals=transcendentals
        ),
        name=name,
    )(*ins)


def gather_body(el_ref, az_ref, tokens_hbm, slots_hbm, *refs):
    out_refs, (tokens_ref, slots_ref, sems) = refs[:-3], refs[-3:]
    copies = [
        pltpu.make_async_copy(tokens_hbm, tokens_ref, sems.at[0]),
        pltpu.make_async_copy(slots_hbm, slots_ref, sems.at[1]),
    ]
    for c in copies:
        c.start()
    offsets, groups, capacity = slots_ref.shape
    rows = tokens_ref.shape[0]
    el, az = el_ref[0], az_ref[0]
    eye = lax.broadcasted_iota(jnp.int32, (capacity, capacity), 0) == lax.broadcasted_iota(
        jnp.int32, (capacity, capacity), 1
    )
    lane = lax.broadcasted_iota(jnp.int32, (capacity, rows), 1).astype(F32)
    for c in copies:
        c.wait()
    tokens = tokens_ref[...]
    for step in range(groups):
        target = lax.rem(el + step, groups)
        picks = []
        for piece in range(offsets):
            row = slots_ref[sent_offset(az, piece), pl.ds(target, 1), :].astype(F32)
            spread = jnp.broadcast_to(row, (capacity, capacity))
            column = jnp.sum(jnp.where(eye, spread, 0.0), axis=-1, keepdims=True)
            picks.append(jnp.where(column == lane, 1.0, 0.0))
        one_hot = jnp.concatenate(picks, axis=0).astype(BF16)
        chosen = dot(one_hot, tokens).astype(BF16)
        out_refs[step][...] = chosen.reshape(out_refs[step].shape)


def prepare_body(*refs, groups, capacity, weights):
    el_ref, az_ref, points_hbm, skip_hbm, idx_hbm, w_query_hbm = refs[:6]
    weight_hbm = refs[6 : 6 + weights]
    q_ref, bias_ref, points_ref, skip_ref = refs[6 + weights : 10 + weights]
    weight_refs = refs[10 + weights : 10 + 2 * weights]
    idx_ref, w_query_ref, sems = refs[10 + 2 * weights :]
    el, az = el_ref[0], az_ref[0]
    even = 1 - lax.rem(el, 2)
    cols = points_ref.shape[0] // 2
    first = [
        pltpu.make_async_copy(idx_hbm.at[even], idx_ref.at[0], sems.at[0]),
        pltpu.make_async_copy(idx_hbm.at[1 - even], idx_ref.at[1], sems.at[1]),
        pltpu.make_async_copy(w_query_hbm, w_query_ref, sems.at[2]),
        pltpu.make_async_copy(points_hbm.at[even], points_ref.at[pl.ds(0, cols)], sems.at[3]),
        pltpu.make_async_copy(points_hbm.at[1 - even], points_ref.at[pl.ds(cols, cols)], sems.at[4]),
    ]
    later = [
        pltpu.make_async_copy(skip_hbm.at[even], skip_ref.at[pl.ds(0, cols)], sems.at[5]),
        pltpu.make_async_copy(skip_hbm.at[1 - even], skip_ref.at[pl.ds(cols, cols)], sems.at[6]),
    ]
    for k in range(weights):
        later.append(pltpu.make_async_copy(weight_hbm[k], weight_refs[k], sems.at[7 + k]))
    for c in first + later:
        c.start()
    for c in first:
        c.wait()
    count, width = q_ref.shape[1], q_ref.shape[0]
    scale = math.log2(math.e) / math.sqrt(width // HEADS)
    query = dot(points_ref[...], w_query_ref[...]) * scale
    q_ref[...] = query.T.astype(BF16)
    near = idx_ref.shape[1]
    lanes = 128
    for piece in range(bias_ref.shape[0] // (groups * capacity)):
        offset = 2 * REACH - sent_offset(az, piece)
        for step in range(groups):
            source = lax.rem(el + groups - step, groups)
            low = (offset * groups + source) * capacity
            slot = low + lax.broadcasted_iota(jnp.int32, (capacity, lanes), 0)
            place = (piece * groups + step) * capacity
            for start in range(0, count, lanes):
                row, col = divmod(start, cols)
                total = jnp.zeros((capacity, lanes), F32)
                for n in range(near):
                    index = idx_ref[row, n : n + 1, col : col + lanes]
                    total = total + jnp.where(slot == index, 1.0, 0.0)
                bias_ref[place : place + capacity, start : start + lanes] = jnp.log2(total)
    for c in later:
        c.wait()


def main_body(az_ref, *refs, pieces):
    piece_refs = refs[:pieces]
    (
        q_ref,
        bias_ref,
        points_ref,
        skip_ref,
        w_key_ref,
        w_value_ref,
        w_out_ref,
        w_hid_ref,
        w_skip_ref,
        w_down_ref,
        joined_ref,
        near_ref,
        far_ref,
        inner_edge_ref,
        outer_edge_ref,
        att_ref,
    ) = refs[pieces:]
    width, count = q_ref.shape
    head_width = width // HEADS
    received = jnp.concatenate([r[...] for r in piece_refs], axis=0)
    table = received.shape[0]
    keys = dot(received, w_key_ref[...]).astype(BF16)
    normed_tokens = rms(received.astype(F32)).astype(BF16)
    values_t = dot(w_value_ref[...], normed_tokens, ((0,), (1,))).astype(BF16)
    ones = jnp.ones((16, table), BF16)
    for head in range(HEADS):
        low, high = head * head_width, (head + 1) * head_width
        scores = dot(keys[:, low:high], q_ref[low:high, :]) + bias_ref[...]
        top = jnp.max(scores, axis=0, keepdims=True)
        weights = jnp.exp2(scores - top).astype(BF16)
        lhs = jnp.concatenate([values_t[low:high, :], ones], axis=0)
        mixed = dot(lhs, weights)
        att_ref[low:high, :] = (mixed[:head_width] / mixed[head_width : head_width + 1]).astype(BF16)
    residual = points_ref[...].astype(F32) + dot(att_ref[...], w_out_ref[...], ((0,), (0,)))
    normed = rms(residual).astype(BF16)
    pre = dot(normed, w_hid_ref[...]) + dot(skip_ref[...], w_skip_ref[...])
    c1 = math.sqrt(2.0 / math.pi)
    half = 0.5 * pre
    inner = (half + half * jnp.tanh(pre * (c1 + (c1 * 0.044715) * (pre * pre)))).astype(BF16)
    joined = residual + dot(inner, w_down_ref[...])
    conv = rms(joined)
    joined_ref[...] = joined.reshape(joined_ref.shape)
    cols = count // 2
    near_ref[0:cols] = conv[:cols].astype(BF16)
    far_ref[0:cols] = conv[cols:].astype(BF16)
    left = jnp.concatenate([conv[0:1], conv[cols : cols + 1]], axis=0)
    right = jnp.concatenate([conv[cols - 1 : cols], conv[2 * cols - 1 :]], axis=0)
    odd = lax.rem(az_ref[0], 2) == 1
    inner_edge_ref[...] = jnp.where(odd, left, right).astype(BF16)
    outer_edge_ref[...] = jnp.where(odd, right, left).astype(BF16)


def pack_body(az_ref, inner_ref, outer_ref, near_in, far_in, near_ref, far_ref):
    del near_in, far_in
    odd = lax.rem(az_ref[0], 2) == 1
    inner, outer = inner_ref[...].astype(F32), outer_ref[...].astype(F32)
    right = jnp.where(odd, outer, inner)
    left = jnp.where(odd, inner, outer)
    cols, width = near_ref.shape[0] - PAD, near_ref.shape[1]
    row = lax.broadcasted_iota(jnp.int32, (PAD, width), 0)
    for at, ref in enumerate((near_ref, far_ref)):
        rows = jnp.where(row == 0, right[at : at + 1], 0.0)
        rows = jnp.where(row == PAD - 1, left[at : at + 1], rows)
        ref[cols:, :] = rows.astype(BF16)


def conv_rows(pairs, cols):
    taps = []
    for dc in range(3):
        total = None
        for x, w_ref, base in pairs:
            part = dot(x, w_ref[base + dc])
            total = part if total is None else total + part
        taps.append(total)
    length = taps[0].shape[0]
    shifted = taps[1] + pltpu.roll(taps[0], 1, 0) + pltpu.roll(taps[2], length - 1, 0)
    return shifted[:cols]


def inside_body(el_ref, near_ref, far_ref, joined_ref, w_ref, out_ref):
    odd = lax.rem(el_ref[0], 2)
    cols = joined_ref.shape[1]
    near, far = near_ref[...], far_ref[...]
    out_ref[0] = joined_ref[0] + conv_rows([(near, w_ref, 3), (far, w_ref, 6 * odd)], cols)
    out_ref[1] = joined_ref[1] + conv_rows([(far, w_ref, 3), (near, w_ref, 6 - 6 * odd)], cols)


def border_body(el_ref, near_ref, far_ref, part_ref, w_ref, out_ref, *, last):
    el = el_ref[0]
    odd = lax.rem(el, 2)
    cols = part_ref.shape[1]
    near = part_ref[0] + conv_rows([(near_ref[...], w_ref, 6 - 6 * odd)], cols)
    out_ref[1 - odd] = near.astype(BF16)
    far = conv_rows([(far_ref[...], w_ref, 6 * odd)], cols)
    ends = jnp.logical_or(el == 0, el == last)
    out_ref[odd] = (part_ref[1] + jnp.where(ends, 0.0, far)).astype(BF16)


def per_device(
    points,
    skip,
    tokens,
    send_slots,
    recv_idx,
    w_query,
    w_key,
    w_value,
    w_out,
    w_hid,
    w_skip,
    w_down,
    w_conv,
):
    rows, cols, width = points.shape
    count = rows * cols
    own_tokens = tokens[0, 0]
    slots = send_slots[0, 0]
    offsets, groups, capacity = slots.shape
    table = offsets * groups * capacity
    el = lax.axis_index("el").astype(jnp.int32).reshape(1)
    az = lax.axis_index("az").astype(jnp.int32).reshape(1)
    shape = jax.ShapeDtypeStruct
    dma = pltpu.SemaphoreType.DMA
    sent = call(
        gather_body,
        [shape((offsets, capacity, width), BF16)] * groups,
        [el, az, own_tokens, slots],
        "gather",
        (2 * table * own_tokens.shape[0] * width, 0),
        [SMEM, SMEM, HBM, HBM],
        [VMEM(own_tokens.shape, BF16), VMEM(slots.shape, jnp.int32), dma((2,))],
    )
    got = [sent[0]]
    for s in range(1, groups):
        got.append(swap(sent[s], "el", lambda i, n, s=s: (i + s) % n))
    pieces = []
    for piece in range(offsets):
        bundle = jnp.concatenate([g[piece] for g in got], axis=0)
        pieces.append(swap(bundle, "az", MATCHES[piece]) if piece else bundle)
    weights = [w_key, w_value, w_out, w_hid, w_skip, w_down, w_conv]
    idx = jnp.swapaxes(recv_idx, 1, 2)
    query_t, bias, points_v, skip_v, *held = call(
        functools.partial(prepare_body, groups=groups, capacity=capacity, weights=len(weights)),
        [
            shape((width, count), BF16),
            shape((table, count), F32),
            shape((count, width), BF16),
            shape((count, width), BF16),
        ]
        + [shape(w.shape, BF16) for w in weights],
        [el, az, points, skip, idx, w_query] + weights,
        "prepare",
        (table * count * 48, table * count),
        [SMEM, SMEM] + [HBM] * (4 + len(weights)),
        [VMEM(idx.shape, jnp.int32), VMEM(w_query.shape, BF16), dma((7 + len(weights),))],
    )
    joined, near, far, inner_edge, outer_edge = call(
        functools.partial(main_body, pieces=len(pieces)),
        [
            shape((rows, cols, width), F32),
            shape((cols + PAD, width), BF16),
            shape((cols + PAD, width), BF16),
            shape((2, width), BF16),
            shape((2, width), BF16),
        ],
        [az] + pieces + [query_t, bias, points_v, skip_v] + held[:-1],
        "main",
        (10 * table * count * width + 2 * count * width * 13 * width, table * count * HEADS),
        [SMEM] + [VMEM] * (len(pieces) + 10),
        [VMEM((width, count), BF16)],
    )
    outer_got = swap(outer_edge, "az", next_chip)
    inner_got = swap(inner_edge, "az", same_chip)
    near, far = call(
        pack_body,
        [shape((cols + PAD, width), BF16)] * 2,
        [az, inner_got, outer_got, near, far],
        "pack",
        (4 * PAD * width, 0),
        [SMEM] + [VMEM] * 4,
        (),
        {3: 0, 4: 1},
    )
    far_got = swap(far, "el", inner_pair)
    near_got = swap(near, "el", same_chip)
    (partial,) = call(
        inside_body,
        [shape((rows, cols, width), F32)],
        [el, near, far, joined, held[-1]],
        "inside",
        (2 * count * width * width * 6, 0),
        [SMEM] + [VMEM] * 4,
    )
    (out,) = call(
        functools.partial(border_body, last=lax.axis_size("el") - 1),
        [shape((rows, cols, width), BF16)],
        [el, near_got, far_got, partial, held[-1]],
        "border",
        (2 * count * width * width * 3, 0),
        [SMEM] + [VMEM] * 4,
    )
    return out


def solution(mesh):
    return jax.shard_map(
        per_device,
        mesh=mesh,
        in_specs=(
            P("el", "az", None),
            P("el", "az", None),
            P("az", "el", None, None),
            P("az", "el", None, None, None),
            P("el", "az", None),
            P(),
            P(),
            P(),
            P(),
            P(),
            P(),
            P(),
            P(),
        ),
        out_specs=P("el", "az", None),
        check_vma=False,
    )
```

```python
import functools
import math

import jax
import jax.numpy as jnp
from jax import lax
from jax.experimental import pallas as pl
from jax.experimental.pallas import tpu as pltpu
from jax.sharding import PartitionSpec as P

HEADS = 8
REACH = 2
PAD = 16
BF16 = jnp.bfloat16
F32 = jnp.float32
VMEM = pltpu.VMEM
SMEM = pltpu.SMEM
HBM = pltpu.HBM


def same_chip(i, n):
    return i ^ 1


def next_chip(i, n):
    return (i + 1 if i % 2 else i - 1) % n


def two_on(i, n):
    return (i + 2 if i // 2 % 2 == 0 else i - 2) % n


def two_back(i, n):
    return (i - 2 if i // 2 % 2 == 0 else i + 2) % n


def inner_pair(i, n):
    return i if i in (0, n - 1) else next_chip(i, n)


def swap(x, axis, partner):
    n = lax.axis_size(axis)
    return lax.ppermute(x, axis, [(i, partner(i, n)) for i in range(n)])


def sent_offset(az, piece):
    odd, odd_chip = lax.rem(az, 2), lax.rem(lax.div(az, 2), 2)
    return (REACH, 4 * odd_chip, 1 + 2 * odd, 4 - 4 * odd_chip, 3 - 2 * odd)[piece]


MATCHES = (None, two_back, next_chip, two_on, same_chip)


def dot(a, b, contract=((1,), (0,))):
    return lax.dot_general(a, b, (contract, ((), ())), preferred_element_type=F32)


def rms(x):
    return x * lax.rsqrt(jnp.mean(x * x, axis=-1, keepdims=True) + 1e-06)


def call(body, outs, ins, name, cost, spaces=None, scratch=(), aliases=None):
    spaces = spaces or [VMEM] * len(ins)
    flops, transcendentals = cost
    moved = sum(x.size * x.dtype.itemsize for x in list(ins) + list(outs))
    ins = [
        pltpu.with_memory_space_constraint(x, HBM) if s == HBM else x
        for x, s in zip(ins, spaces)
    ]
    return pl.pallas_call(
        body,
        out_shape=outs,
        in_specs=[pl.BlockSpec(memory_space=s) for s in spaces],
        out_specs=[pl.BlockSpec(memory_space=VMEM) for _ in outs],
        scratch_shapes=list(scratch),
        input_output_aliases=aliases or {},
        compiler_params=pltpu.CompilerParams(vmem_limit_bytes=20 * 1024 * 1024),
        cost_estimate=pl.CostEstimate(
            flops=flops, bytes_accessed=moved, transcendentals=transcendentals
        ),
        name=name,
    )(*ins)


def gather_body(el_ref, az_ref, tokens_hbm, slots_hbm, *refs):
    out_refs, (tokens_ref, slots_ref, sems) = refs[:-3], refs[-3:]
    copies = [
        pltpu.make_async_copy(tokens_hbm, tokens_ref, sems.at[0]),
        pltpu.make_async_copy(slots_hbm, slots_ref, sems.at[1]),
    ]
    for c in copies:
        c.start()
    offsets, groups, capacity = slots_ref.shape
    rows = tokens_ref.shape[0]
    el, az = el_ref[0], az_ref[0]
    eye = lax.broadcasted_iota(jnp.int32, (capacity, capacity), 0) == lax.broadcasted_iota(
        jnp.int32, (capacity, capacity), 1
    )
    lane = lax.broadcasted_iota(jnp.int32, (capacity, rows), 1).astype(F32)
    for c in copies:
        c.wait()
    tokens = tokens_ref[...]
    for step in range(groups):
        target = lax.rem(el + step, groups)
        picks = []
        for piece in range(offsets):
            row = slots_ref[sent_offset(az, piece), pl.ds(target, 1), :].astype(F32)
            spread = jnp.broadcast_to(row, (capacity, capacity))
            column = jnp.sum(jnp.where(eye, spread, 0.0), axis=-1, keepdims=True)
            picks.append(jnp.where(column == lane, 1.0, 0.0))
        one_hot = jnp.concatenate(picks, axis=0).astype(BF16)
        chosen = dot(one_hot, tokens).astype(BF16)
        out_refs[step][...] = chosen.reshape(out_refs[step].shape)


def prepare_body(*refs, groups, capacity, weights):
    el_ref, az_ref, points_hbm, skip_hbm, idx_hbm, w_query_hbm, w_skip_hbm = refs[:7]
    weight_hbm = refs[7 : 7 + weights]
    q_ref, bias_ref, points_ref, side_ref = refs[8 + weights : 12 + weights]
    weight_refs = refs[12 + weights : 12 + 2 * weights]
    idx_ref, w_query_ref, skip_ref, w_skip_ref, sems = refs[12 + 2 * weights :]
    el, az = el_ref[0], az_ref[0]
    even = 1 - lax.rem(el, 2)
    cols = points_ref.shape[0] // 2
    first = [
        pltpu.make_async_copy(idx_hbm.at[even], idx_ref.at[0], sems.at[0]),
        pltpu.make_async_copy(idx_hbm.at[1 - even], idx_ref.at[1], sems.at[1]),
        pltpu.make_async_copy(w_query_hbm, w_query_ref, sems.at[2]),
        pltpu.make_async_copy(points_hbm.at[even], points_ref.at[pl.ds(0, cols)], sems.at[3]),
        pltpu.make_async_copy(points_hbm.at[1 - even], points_ref.at[pl.ds(cols, cols)], sems.at[4]),
    ]
    later = [
        pltpu.make_async_copy(skip_hbm.at[even], skip_ref.at[pl.ds(0, cols)], sems.at[5]),
        pltpu.make_async_copy(skip_hbm.at[1 - even], skip_ref.at[pl.ds(cols, cols)], sems.at[6]),
        pltpu.make_async_copy(w_skip_hbm, w_skip_ref, sems.at[7]),
    ]
    for k in range(weights):
        later.append(pltpu.make_async_copy(weight_hbm[k], weight_refs[k], sems.at[8 + k]))
    for c in first + later:
        c.start()
    for c in first:
        c.wait()
    count, width = q_ref.shape[1], q_ref.shape[0]
    scale = math.log2(math.e) / math.sqrt(width // HEADS)
    query = dot(points_ref[...], w_query_ref[...]) * scale
    q_ref[...] = query.T.astype(BF16)
    near = idx_ref.shape[1]
    lanes = 128
    for piece in range(bias_ref.shape[0] // (groups * capacity)):
        offset = 2 * REACH - sent_offset(az, piece)
        for step in range(groups):
            source = lax.rem(el + groups - step, groups)
            low = (offset * groups + source) * capacity
            slot = low + lax.broadcasted_iota(jnp.int32, (capacity, lanes), 0)
            place = (piece * groups + step) * capacity
            for start in range(0, count, lanes):
                row, col = divmod(start, cols)
                total = jnp.zeros((capacity, lanes), F32)
                for n in range(near):
                    index = idx_ref[row, n : n + 1, col : col + lanes]
                    total = total + jnp.where(slot == index, 1.0, 0.0)
                bias_ref[place : place + capacity, start : start + lanes] = jnp.log2(total)
    for c in later:
        c.wait()
    side_ref[...] = dot(skip_ref[...], w_skip_ref[...])


def main_body(az_ref, *refs, pieces):
    piece_refs = refs[:pieces]
    (
        q_ref,
        bias_ref,
        points_ref,
        side_ref,
        w_key_ref,
        w_value_ref,
        w_out_ref,
        w_hid_ref,
        w_down_ref,
        joined_ref,
        near_ref,
        far_ref,
        inner_edge_ref,
        outer_edge_ref,
        att_ref,
    ) = refs[pieces:]
    width, count = q_ref.shape
    head_width = width // HEADS
    received = jnp.concatenate([r[...] for r in piece_refs], axis=0)
    table = received.shape[0]
    keys = dot(received, w_key_ref[...]).astype(BF16)
    normed_tokens = rms(received.astype(F32)).astype(BF16)
    values_t = dot(w_value_ref[...], normed_tokens, ((0,), (1,))).astype(BF16)
    ones = jnp.ones((16, table), BF16)
    for head in range(HEADS):
        low, high = head * head_width, (head + 1) * head_width
        scores = dot(keys[:, low:high], q_ref[low:high, :]) + bias_ref[...]
        top = jnp.max(scores, axis=0, keepdims=True)
        weights = jnp.exp2(scores - top).astype(BF16)
        lhs = jnp.concatenate([values_t[low:high, :], ones], axis=0)
        mixed = dot(lhs, weights)
        att_ref[low:high, :] = (mixed[:head_width] / mixed[head_width : head_width + 1]).astype(BF16)
    residual = points_ref[...].astype(F32) + dot(att_ref[...], w_out_ref[...], ((0,), (0,)))
    normed = rms(residual).astype(BF16)
    pre = dot(normed, w_hid_ref[...]) + side_ref[...]
    c1 = math.sqrt(2.0 / math.pi)
    half = 0.5 * pre
    inner = (half + half * jnp.tanh(pre * (c1 + (c1 * 0.044715) * (pre * pre)))).astype(BF16)
    joined = residual + dot(inner, w_down_ref[...])
    conv = rms(joined)
    joined_ref[...] = joined.reshape(joined_ref.shape)
    cols = count // 2
    near_ref[0:cols] = conv[:cols].astype(BF16)
    far_ref[0:cols] = conv[cols:].astype(BF16)
    left = jnp.concatenate([conv[0:1], conv[cols : cols + 1]], axis=0)
    right = jnp.concatenate([conv[cols - 1 : cols], conv[2 * cols - 1 :]], axis=0)
    odd = lax.rem(az_ref[0], 2) == 1
    inner_edge_ref[...] = jnp.where(odd, left, right).astype(BF16)
    outer_edge_ref[...] = jnp.where(odd, right, left).astype(BF16)


def pack_body(az_ref, inner_ref, outer_ref, near_in, far_in, near_ref, far_ref):
    del near_in, far_in
    odd = lax.rem(az_ref[0], 2) == 1
    inner, outer = inner_ref[...].astype(F32), outer_ref[...].astype(F32)
    right = jnp.where(odd, outer, inner)
    left = jnp.where(odd, inner, outer)
    cols, width = near_ref.shape[0] - PAD, near_ref.shape[1]
    row = lax.broadcasted_iota(jnp.int32, (PAD, width), 0)
    for at, ref in enumerate((near_ref, far_ref)):
        rows = jnp.where(row == 0, right[at : at + 1], 0.0)
        rows = jnp.where(row == PAD - 1, left[at : at + 1], rows)
        ref[cols:, :] = rows.astype(BF16)


def conv_rows(pairs, cols):
    taps = []
    for dc in range(3):
        total = None
        for x, w_ref, base in pairs:
            part = dot(x, w_ref[base + dc])
            total = part if total is None else total + part
        taps.append(total)
    length = taps[0].shape[0]
    shifted = taps[1] + pltpu.roll(taps[0], 1, 0) + pltpu.roll(taps[2], length - 1, 0)
    return shifted[:cols]


def inside_body(el_ref, near_ref, far_ref, joined_ref, w_ref, out_ref):
    odd = lax.rem(el_ref[0], 2)
    cols = joined_ref.shape[1]
    near, far = near_ref[...], far_ref[...]
    out_ref[0] = joined_ref[0] + conv_rows([(near, w_ref, 3), (far, w_ref, 6 * odd)], cols)
    out_ref[1] = joined_ref[1] + conv_rows([(far, w_ref, 3), (near, w_ref, 6 - 6 * odd)], cols)


def border_body(el_ref, near_ref, far_ref, part_ref, w_ref, out_ref, *, last):
    el = el_ref[0]
    odd = lax.rem(el, 2)
    cols = part_ref.shape[1]
    near = part_ref[0] + conv_rows([(near_ref[...], w_ref, 6 - 6 * odd)], cols)
    out_ref[1 - odd] = near.astype(BF16)
    far = conv_rows([(far_ref[...], w_ref, 6 * odd)], cols)
    ends = jnp.logical_or(el == 0, el == last)
    out_ref[odd] = (part_ref[1] + jnp.where(ends, 0.0, far)).astype(BF16)


def per_device(
    points,
    skip,
    tokens,
    send_slots,
    recv_idx,
    w_query,
    w_key,
    w_value,
    w_out,
    w_hid,
    w_skip,
    w_down,
    w_conv,
):
    rows, cols, width = points.shape
    count = rows * cols
    own_tokens = tokens[0, 0]
    slots = send_slots[0, 0]
    offsets, groups, capacity = slots.shape
    table = offsets * groups * capacity
    el = lax.axis_index("el").astype(jnp.int32).reshape(1)
    az = lax.axis_index("az").astype(jnp.int32).reshape(1)
    shape = jax.ShapeDtypeStruct
    dma = pltpu.SemaphoreType.DMA
    sent = call(
        gather_body,
        [shape((offsets, capacity, width), BF16)] * groups,
        [el, az, own_tokens, slots],
        "gather",
        (2 * table * own_tokens.shape[0] * width, 0),
        [SMEM, SMEM, HBM, HBM],
        [VMEM(own_tokens.shape, BF16), VMEM(slots.shape, jnp.int32), dma((2,))],
    )
    got = [sent[0]]
    for s in range(1, groups):
        got.append(swap(sent[s], "el", lambda i, n, s=s: (i + s) % n))
    pieces = []
    for piece in range(offsets):
        bundle = jnp.concatenate([g[piece] for g in got], axis=0)
        pieces.append(swap(bundle, "az", MATCHES[piece]) if piece else bundle)
    weights = [w_key, w_value, w_out, w_hid, w_down, w_conv]
    idx = jnp.swapaxes(recv_idx, 1, 2)
    query_t, bias, points_v, side, *held = call(
        functools.partial(prepare_body, groups=groups, capacity=capacity, weights=len(weights)),
        [
            shape((width, count), BF16),
            shape((table, count), F32),
            shape((count, width), BF16),
            shape((count, w_skip.shape[1]), F32),
        ]
        + [shape(w.shape, BF16) for w in weights],
        [el, az, points, skip, idx, w_query, w_skip] + weights + [pieces[0]],
        "prepare",
        (table * count * 48, table * count),
        [SMEM, SMEM] + [HBM] * (5 + len(weights)) + [VMEM],
        [
            VMEM(idx.shape, jnp.int32),
            VMEM(w_query.shape, BF16),
            VMEM((count, width), BF16),
            VMEM(w_skip.shape, BF16),
            dma((8 + len(weights),)),
        ],
    )
    joined, near, far, inner_edge, outer_edge = call(
        functools.partial(main_body, pieces=len(pieces)),
        [
            shape((rows, cols, width), F32),
            shape((cols + PAD, width), BF16),
            shape((cols + PAD, width), BF16),
            shape((2, width), BF16),
            shape((2, width), BF16),
        ],
        [az] + pieces + [query_t, bias, points_v, side] + held[:-1],
        "main",
        (10 * table * count * width + 2 * count * width * 13 * width, table * count * HEADS),
        [SMEM] + [VMEM] * (len(pieces) + 9),
        [VMEM((width, count), BF16)],
    )
    outer_got = swap(outer_edge, "az", next_chip)
    inner_got = swap(inner_edge, "az", same_chip)
    near, far = call(
        pack_body,
        [shape((cols + PAD, width), BF16)] * 2,
        [az, inner_got, outer_got, near, far],
        "pack",
        (4 * PAD * width, 0),
        [SMEM] + [VMEM] * 4,
        (),
        {3: 0, 4: 1},
    )
    far_got = swap(far, "el", inner_pair)
    near_got = swap(near, "el", same_chip)
    (partial,) = call(
        inside_body,
        [shape((rows, cols, width), F32)],
        [el, near, far, joined, held[-1]],
        "inside",
        (2 * count * width * width * 6, 0),
        [SMEM] + [VMEM] * 4,
    )
    (out,) = call(
        functools.partial(border_body, last=lax.axis_size("el") - 1),
        [shape((rows, cols, width), BF16)],
        [el, near_got, far_got, partial, held[-1]],
        "border",
        (2 * count * width * width * 3, 0),
        [SMEM] + [VMEM] * 4,
    )
    return out


def solution(mesh):
    return jax.shard_map(
        per_device,
        mesh=mesh,
        in_specs=(
            P("el", "az", None),
            P("el", "az", None),
            P("az", "el", None, None),
            P("az", "el", None, None, None),
            P("el", "az", None),
            P(),
            P(),
            P(),
            P(),
            P(),
            P(),
            P(),
            P(),
        ),
        out_specs=P("el", "az", None),
        check_vma=False,
    )
```

```python
import functools
import math

import jax
import jax.numpy as jnp
from jax import lax
from jax.experimental import pallas as pl
from jax.experimental.pallas import tpu as pltpu
from jax.sharding import PartitionSpec as P

HEADS = 8
REACH = 2
PAD = 16
BF16 = jnp.bfloat16
F32 = jnp.float32
VMEM = pltpu.VMEM
SMEM = pltpu.SMEM
HBM = pltpu.HBM


def same_chip(i, n):
    return i ^ 1


def next_chip(i, n):
    return (i + 1 if i % 2 else i - 1) % n


def two_on(i, n):
    return (i + 2 if i // 2 % 2 == 0 else i - 2) % n


def two_back(i, n):
    return (i - 2 if i // 2 % 2 == 0 else i + 2) % n


def inner_pair(i, n):
    return i if i in (0, n - 1) else next_chip(i, n)


def swap(x, axis, partner):
    n = lax.axis_size(axis)
    return lax.ppermute(x, axis, [(i, partner(i, n)) for i in range(n)])


def sent_offset(az, piece):
    odd, odd_chip = lax.rem(az, 2), lax.rem(lax.div(az, 2), 2)
    return (REACH, 4 * odd_chip, 1 + 2 * odd, 4 - 4 * odd_chip, 3 - 2 * odd)[piece]


MATCHES = (None, two_back, next_chip, two_on, same_chip)


def dot(a, b, contract=((1,), (0,))):
    return lax.dot_general(a, b, (contract, ((), ())), preferred_element_type=F32)


def rms(x):
    return x * lax.rsqrt(jnp.mean(x * x, axis=-1, keepdims=True) + 1e-06)


def call(body, outs, ins, name, cost, spaces=None, scratch=(), aliases=None):
    spaces = spaces or [VMEM] * len(ins)
    flops, transcendentals = cost
    moved = sum(x.size * x.dtype.itemsize for x in list(ins) + list(outs))
    ins = [
        pltpu.with_memory_space_constraint(x, HBM) if s == HBM else x
        for x, s in zip(ins, spaces)
    ]
    return pl.pallas_call(
        body,
        out_shape=outs,
        in_specs=[pl.BlockSpec(memory_space=s) for s in spaces],
        out_specs=[pl.BlockSpec(memory_space=VMEM) for _ in outs],
        scratch_shapes=list(scratch),
        input_output_aliases=aliases or {},
        compiler_params=pltpu.CompilerParams(vmem_limit_bytes=20 * 1024 * 1024),
        cost_estimate=pl.CostEstimate(
            flops=flops, bytes_accessed=moved, transcendentals=transcendentals
        ),
        name=name,
    )(*ins)


def gather_body(el_ref, az_ref, tokens_hbm, slots_hbm, *refs):
    out_refs, (tokens_ref, slots_ref, sems) = refs[:-3], refs[-3:]
    copies = [
        pltpu.make_async_copy(tokens_hbm, tokens_ref, sems.at[0]),
        pltpu.make_async_copy(slots_hbm, slots_ref, sems.at[1]),
    ]
    for c in copies:
        c.start()
    offsets, groups, capacity = slots_ref.shape
    rows = tokens_ref.shape[0]
    el, az = el_ref[0], az_ref[0]
    eye = lax.broadcasted_iota(jnp.int32, (capacity, capacity), 0) == lax.broadcasted_iota(
        jnp.int32, (capacity, capacity), 1
    )
    lane = lax.broadcasted_iota(jnp.int32, (capacity, rows), 1).astype(F32)
    for c in copies:
        c.wait()
    tokens = tokens_ref[...]
    for step in range(groups):
        target = lax.bitwise_xor(el, step)
        picks = []
        for piece in range(offsets):
            row = slots_ref[sent_offset(az, piece), pl.ds(target, 1), :].astype(F32)
            spread = jnp.broadcast_to(row, (capacity, capacity))
            column = jnp.sum(jnp.where(eye, spread, 0.0), axis=-1, keepdims=True)
            picks.append(jnp.where(column == lane, 1.0, 0.0))
        one_hot = jnp.concatenate(picks, axis=0).astype(BF16)
        chosen = dot(one_hot, tokens).astype(BF16)
        out_refs[step][...] = chosen.reshape(out_refs[step].shape)


def load_body(*refs, groups, capacity, held):
    el_ref, az_ref, points_hbm, skip_hbm, idx_hbm = refs[:5]
    held_hbm = refs[5 : 5 + held]
    bias_ref, points_ref, skip_ref = refs[5 + held : 8 + held]
    held_refs = refs[8 + held : 8 + 2 * held]
    idx_ref, sems = refs[8 + 2 * held :]
    el, az = el_ref[0], az_ref[0]
    even = 1 - lax.rem(el, 2)
    cols = points_ref.shape[0] // 2
    count = 2 * cols
    first, later = [], []
    for r, at in enumerate((even, 1 - even)):
        rows = pl.ds(r * cols, cols)
        first.append(pltpu.make_async_copy(idx_hbm.at[at], idx_ref.at[r], sems.at[r]))
        later.append(pltpu.make_async_copy(points_hbm.at[at], points_ref.at[rows], sems.at[2 + r]))
        later.append(pltpu.make_async_copy(skip_hbm.at[at], skip_ref.at[rows], sems.at[4 + r]))
    for k in range(held):
        later.append(pltpu.make_async_copy(held_hbm[k], held_refs[k], sems.at[6 + k]))
    for c in first + later:
        c.start()
    for c in first:
        c.wait()
    near = idx_ref.shape[1]
    lanes = 128
    for piece in range(bias_ref.shape[0] // (groups * capacity)):
        offset = 2 * REACH - sent_offset(az, piece)
        for step in range(groups):
            source = lax.bitwise_xor(el, step)
            low = (offset * groups + source) * capacity
            slot = low + lax.broadcasted_iota(jnp.int32, (capacity, lanes), 0)
            place = (piece * groups + step) * capacity
            for start in range(0, count, lanes):
                row, col = divmod(start, cols)
                total = jnp.zeros((capacity, lanes), F32)
                for n in range(near):
                    index = idx_ref[row, n : n + 1, col : col + lanes]
                    total = total + jnp.where(slot == index, 1.0, 0.0)
                bias_ref[place : place + capacity, start : start + lanes] = jnp.log2(total)
    for c in later:
        c.wait()


def query_body(points_ref, skip_ref, w_query_ref, w_skip_ref, after_ref, q_ref, side_ref):
    del after_ref
    scale = math.log2(math.e) / math.sqrt(q_ref.shape[0] // HEADS)
    query = dot(points_ref[...], w_query_ref[...]) * scale
    q_ref[...] = query.T.astype(BF16)
    side_ref[...] = dot(skip_ref[...], w_skip_ref[...])


def main_body(az_ref, *refs, pieces):
    piece_refs = refs[:pieces]
    (
        q_ref,
        bias_ref,
        points_ref,
        side_ref,
        w_key_ref,
        w_value_ref,
        w_out_ref,
        w_hid_ref,
        w_down_ref,
        joined_ref,
        near_ref,
        far_ref,
        inner_edge_ref,
        outer_edge_ref,
        att_ref,
    ) = refs[pieces:]
    width, count = q_ref.shape
    head_width = width // HEADS
    received = jnp.concatenate([r[...] for r in piece_refs], axis=0)
    table = received.shape[0]
    keys = dot(received, w_key_ref[...]).astype(BF16)
    normed_tokens = rms(received.astype(F32)).astype(BF16)
    values_t = dot(w_value_ref[...], normed_tokens, ((0,), (1,))).astype(BF16)
    ones = jnp.ones((16, table), BF16)
    for head in range(HEADS):
        low, high = head * head_width, (head + 1) * head_width
        scores = dot(keys[:, low:high], q_ref[low:high, :]) + bias_ref[...]
        top = jnp.max(scores, axis=0, keepdims=True)
        weights = jnp.exp2(scores - top).astype(BF16)
        lhs = jnp.concatenate([values_t[low:high, :], ones], axis=0)
        mixed = dot(lhs, weights)
        att_ref[low:high, :] = (mixed[:head_width] / mixed[head_width : head_width + 1]).astype(BF16)
    residual = points_ref[...].astype(F32) + dot(att_ref[...], w_out_ref[...], ((0,), (0,)))
    normed = rms(residual).astype(BF16)
    pre = dot(normed, w_hid_ref[...]) + side_ref[...]
    c1 = math.sqrt(2.0 / math.pi)
    half = 0.5 * pre
    inner = (half + half * jnp.tanh(pre * (c1 + (c1 * 0.044715) * (pre * pre)))).astype(BF16)
    joined = residual + dot(inner, w_down_ref[...])
    conv = rms(joined)
    joined_ref[...] = joined.reshape(joined_ref.shape)
    cols = count // 2
    near_ref[0:cols] = conv[:cols].astype(BF16)
    far_ref[0:cols] = conv[cols:].astype(BF16)
    left = jnp.concatenate([conv[0:1], conv[cols : cols + 1]], axis=0)
    right = jnp.concatenate([conv[cols - 1 : cols], conv[2 * cols - 1 :]], axis=0)
    odd = lax.rem(az_ref[0], 2) == 1
    inner_edge_ref[...] = jnp.where(odd, left, right).astype(BF16)
    outer_edge_ref[...] = jnp.where(odd, right, left).astype(BF16)


def pack_body(az_ref, inner_ref, outer_ref, near_in, far_in, near_ref, far_ref):
    del near_in, far_in
    odd = lax.rem(az_ref[0], 2) == 1
    inner, outer = inner_ref[...].astype(F32), outer_ref[...].astype(F32)
    right = jnp.where(odd, outer, inner)
    left = jnp.where(odd, inner, outer)
    cols, width = near_ref.shape[0] - PAD, near_ref.shape[1]
    row = lax.broadcasted_iota(jnp.int32, (PAD, width), 0)
    for at, ref in enumerate((near_ref, far_ref)):
        rows = jnp.where(row == 0, right[at : at + 1], 0.0)
        rows = jnp.where(row == PAD - 1, left[at : at + 1], rows)
        ref[cols:, :] = rows.astype(BF16)


def conv_rows(pairs, cols):
    taps = []
    for dc in range(3):
        total = None
        for x, w_ref, base in pairs:
            part = dot(x, w_ref[base + dc])
            total = part if total is None else total + part
        taps.append(total)
    length = taps[0].shape[0]
    shifted = taps[1] + pltpu.roll(taps[0], 1, 0) + pltpu.roll(taps[2], length - 1, 0)
    return shifted[:cols]


def inside_body(el_ref, near_ref, far_ref, joined_ref, w_ref, out_ref):
    odd = lax.rem(el_ref[0], 2)
    cols = joined_ref.shape[1]
    near, far = near_ref[...], far_ref[...]
    out_ref[0] = joined_ref[0] + conv_rows([(near, w_ref, 3), (far, w_ref, 6 * odd)], cols)
    out_ref[1] = joined_ref[1] + conv_rows([(far, w_ref, 3), (near, w_ref, 6 - 6 * odd)], cols)


def border_body(el_ref, near_ref, far_ref, part_ref, w_ref, out_ref, *, last):
    el = el_ref[0]
    odd = lax.rem(el, 2)
    cols = part_ref.shape[1]
    near = part_ref[0] + conv_rows([(near_ref[...], w_ref, 6 - 6 * odd)], cols)
    out_ref[1 - odd] = near.astype(BF16)
    far = conv_rows([(far_ref[...], w_ref, 6 * odd)], cols)
    ends = jnp.logical_or(el == 0, el == last)
    out_ref[odd] = (part_ref[1] + jnp.where(ends, 0.0, far)).astype(BF16)


def per_device(
    points,
    skip,
    tokens,
    send_slots,
    recv_idx,
    w_query,
    w_key,
    w_value,
    w_out,
    w_hid,
    w_skip,
    w_down,
    w_conv,
):
    rows, cols, width = points.shape
    count = rows * cols
    own_tokens = tokens[0, 0]
    slots = send_slots[0, 0]
    offsets, groups, capacity = slots.shape
    table = offsets * groups * capacity
    el = lax.axis_index("el").astype(jnp.int32).reshape(1)
    az = lax.axis_index("az").astype(jnp.int32).reshape(1)
    shape = jax.ShapeDtypeStruct
    dma = pltpu.SemaphoreType.DMA
    sent = call(
        gather_body,
        [shape((offsets, capacity, width), BF16)] * groups,
        [el, az, own_tokens, slots],
        "gather",
        (2 * table * own_tokens.shape[0] * width, 0),
        [SMEM, SMEM, HBM, HBM],
        [VMEM(own_tokens.shape, BF16), VMEM(slots.shape, jnp.int32), dma((2,))],
    )
    got = {0: sent[0]}
    for s in reversed(range(1, groups)):
        got[s] = swap(sent[s], "el", lambda i, n, s=s: i ^ s)
    pieces = []
    for piece in range(offsets):
        bundle = jnp.concatenate([got[s][piece] for s in range(groups)], axis=0)
        pieces.append(swap(bundle, "az", MATCHES[piece]) if piece else bundle)
    held = [w_query, w_skip, w_key, w_value, w_out, w_hid, w_down, w_conv]
    idx = jnp.swapaxes(recv_idx, 1, 2)
    bias, points_v, skip_v, *held = call(
        functools.partial(load_body, groups=groups, capacity=capacity, held=len(held)),
        [
            shape((table, count), F32),
            shape((count, width), BF16),
            shape((count, width), BF16),
        ]
        + [shape(w.shape, BF16) for w in held],
        [el, az, points, skip, idx] + held,
        "load",
        (table * count * 48, table * count),
        [SMEM, SMEM] + [HBM] * (3 + len(held)),
        [VMEM(idx.shape, jnp.int32), dma((6 + len(held),))],
    )
    query_t, side = call(
        query_body,
        [shape((width, count), BF16), shape((count, w_skip.shape[1]), F32)],
        [points_v, skip_v, held[0], held[1], pieces[0]],
        "query",
        (2 * count * width * 5 * width, 0),
    )
    joined, near, far, inner_edge, outer_edge = call(
        functools.partial(main_body, pieces=len(pieces)),
        [
            shape((rows, cols, width), F32),
            shape((cols + PAD, width), BF16),
            shape((cols + PAD, width), BF16),
            shape((2, width), BF16),
            shape((2, width), BF16),
        ],
        [az] + pieces + [query_t, bias, points_v, side] + held[2:-1],
        "main",
        (10 * table * count * width + 2 * count * width * 13 * width, table * count * HEADS),
        [SMEM] + [VMEM] * (len(pieces) + 9),
        [VMEM((width, count), BF16)],
    )
    outer_got = swap(outer_edge, "az", next_chip)
    inner_got = swap(inner_edge, "az", same_chip)
    near, far = call(
        pack_body,
        [shape((cols + PAD, width), BF16)] * 2,
        [az, inner_got, outer_got, near, far],
        "pack",
        (4 * PAD * width, 0),
        [SMEM] + [VMEM] * 4,
        (),
        {3: 0, 4: 1},
    )
    far_got = swap(far, "el", inner_pair)
    near_got = swap(near, "el", same_chip)
    (partial,) = call(
        inside_body,
        [shape((rows, cols, width), F32)],
        [el, near, far, joined, held[-1]],
        "inside",
        (2 * count * width * width * 6, 0),
        [SMEM] + [VMEM] * 4,
    )
    (out,) = call(
        functools.partial(border_body, last=lax.axis_size("el") - 1),
        [shape((rows, cols, width), BF16)],
        [el, near_got, far_got, partial, held[-1]],
        "border",
        (2 * count * width * width * 3, 0),
        [SMEM] + [VMEM] * 4,
    )
    return out


def solution(mesh):
    return jax.shard_map(
        per_device,
        mesh=mesh,
        in_specs=(
            P("el", "az", None),
            P("el", "az", None),
            P("az", "el", None, None),
            P("az", "el", None, None, None),
            P("el", "az", None),
            P(),
            P(),
            P(),
            P(),
            P(),
            P(),
            P(),
            P(),
        ),
        out_specs=P("el", "az", None),
        check_vma=False,
    )
```

```python
import functools
import math

import jax
import jax.numpy as jnp
from jax import lax
from jax.experimental import pallas as pl
from jax.experimental.pallas import tpu as pltpu
from jax.sharding import PartitionSpec as P

HEADS = 8
REACH = 2
PAD = 16
BF16 = jnp.bfloat16
F32 = jnp.float32
VMEM = pltpu.VMEM
SMEM = pltpu.SMEM
HBM = pltpu.HBM


def same_chip(i, n):
    return i ^ 1


def next_chip(i, n):
    return (i + 1 if i % 2 else i - 1) % n


def two_on(i, n):
    return (i + 2 if i // 2 % 2 == 0 else i - 2) % n


def two_back(i, n):
    return (i - 2 if i // 2 % 2 == 0 else i + 2) % n


def inner_pair(i, n):
    return i if i in (0, n - 1) else next_chip(i, n)


def swap(x, axis, partner):
    n = lax.axis_size(axis)
    return lax.ppermute(x, axis, [(i, partner(i, n)) for i in range(n)])


def sent_offset(az, piece):
    odd, odd_chip = lax.rem(az, 2), lax.rem(lax.div(az, 2), 2)
    return (REACH, 4 * odd_chip, 1 + 2 * odd, 4 - 4 * odd_chip, 3 - 2 * odd)[piece]


MATCHES = (None, two_back, next_chip, two_on, same_chip)


def dot(a, b, contract=((1,), (0,))):
    return lax.dot_general(a, b, (contract, ((), ())), preferred_element_type=F32)


def rms(x):
    return x * lax.rsqrt(jnp.mean(x * x, axis=-1, keepdims=True) + 1e-06)


def call(body, outs, ins, name, cost, spaces=None, scratch=(), aliases=None):
    spaces = spaces or [VMEM] * len(ins)
    flops, transcendentals = cost
    moved = sum(x.size * x.dtype.itemsize for x in list(ins) + list(outs))
    ins = [
        pltpu.with_memory_space_constraint(x, HBM) if s == HBM else x
        for x, s in zip(ins, spaces)
    ]
    return pl.pallas_call(
        body,
        out_shape=outs,
        in_specs=[pl.BlockSpec(memory_space=s) for s in spaces],
        out_specs=[pl.BlockSpec(memory_space=VMEM) for _ in outs],
        scratch_shapes=list(scratch),
        input_output_aliases=aliases or {},
        compiler_params=pltpu.CompilerParams(vmem_limit_bytes=20 * 1024 * 1024),
        cost_estimate=pl.CostEstimate(
            flops=flops, bytes_accessed=moved, transcendentals=transcendentals
        ),
        name=name,
    )(*ins)


def gather_body(el_ref, az_ref, tokens_hbm, slots_hbm, *refs):
    out_refs, (tokens_ref, slots_ref, sems) = refs[:-3], refs[-3:]
    copies = [
        pltpu.make_async_copy(tokens_hbm, tokens_ref, sems.at[0]),
        pltpu.make_async_copy(slots_hbm, slots_ref, sems.at[1]),
    ]
    for c in copies:
        c.start()
    offsets, groups, capacity = slots_ref.shape
    rows = tokens_ref.shape[0]
    el, az = el_ref[0], az_ref[0]
    eye = lax.broadcasted_iota(jnp.int32, (capacity, capacity), 0) == lax.broadcasted_iota(
        jnp.int32, (capacity, capacity), 1
    )
    lane = lax.broadcasted_iota(jnp.int32, (capacity, rows), 1).astype(F32)
    for c in copies:
        c.wait()
    tokens = tokens_ref[...]
    for step in range(groups):
        target = lax.bitwise_xor(el, step)
        picks = []
        for piece in range(offsets):
            row = slots_ref[sent_offset(az, piece), pl.ds(target, 1), :].astype(F32)
            spread = jnp.broadcast_to(row, (capacity, capacity))
            column = jnp.sum(jnp.where(eye, spread, 0.0), axis=-1, keepdims=True)
            picks.append(jnp.where(column == lane, 1.0, 0.0))
        one_hot = jnp.concatenate(picks, axis=0).astype(BF16)
        chosen = dot(one_hot, tokens).astype(BF16)
        out_refs[step][...] = chosen.reshape(out_refs[step].shape)


def load_body(*refs, groups, capacity, held):
    el_ref, az_ref, points_hbm, skip_hbm, idx_hbm = refs[:5]
    held_hbm = refs[5 : 5 + held]
    bias_ref, points_ref, skip_ref = refs[5 + held : 8 + held]
    held_refs = refs[8 + held : 8 + 2 * held]
    idx_ref, sems = refs[8 + 2 * held :]
    el, az = el_ref[0], az_ref[0]
    even = 1 - lax.rem(el, 2)
    cols = points_ref.shape[0] // 2
    count = 2 * cols
    first, later = [], []
    for r, at in enumerate((even, 1 - even)):
        rows = pl.ds(r * cols, cols)
        first.append(pltpu.make_async_copy(idx_hbm.at[at], idx_ref.at[r], sems.at[r]))
        later.append(pltpu.make_async_copy(points_hbm.at[at], points_ref.at[rows], sems.at[2 + r]))
        later.append(pltpu.make_async_copy(skip_hbm.at[at], skip_ref.at[rows], sems.at[4 + r]))
    for k in range(held):
        later.append(pltpu.make_async_copy(held_hbm[k], held_refs[k], sems.at[6 + k]))
    for c in first + later:
        c.start()
    for c in first:
        c.wait()
    near = idx_ref.shape[1]
    lanes = 128
    for piece in range(bias_ref.shape[0] // (groups * capacity)):
        offset = 2 * REACH - sent_offset(az, piece)
        for step in range(groups):
            source = lax.bitwise_xor(el, step)
            low = (offset * groups + source) * capacity
            slot = low + lax.broadcasted_iota(jnp.int32, (capacity, lanes), 0)
            place = (piece * groups + step) * capacity
            for start in range(0, count, lanes):
                row, col = divmod(start, cols)
                total = jnp.zeros((capacity, lanes), F32)
                for n in range(near):
                    index = idx_ref[row, n : n + 1, col : col + lanes]
                    total = total + jnp.where(slot == index, 1.0, 0.0)
                bias_ref[place : place + capacity, start : start + lanes] = jnp.log2(total)
    for c in later:
        c.wait()


def query_body(points_ref, skip_ref, w_query_ref, w_skip_ref, after_ref, q_ref, side_ref):
    del after_ref
    scale = math.log2(math.e) / math.sqrt(q_ref.shape[0] // HEADS)
    query = dot(points_ref[...], w_query_ref[...]) * scale
    q_ref[...] = query.T.astype(BF16)
    side_ref[...] = dot(skip_ref[...], w_skip_ref[...])


def table_body(*refs, pieces):
    (
        w_key_ref,
        w_value_ref,
        *rest,
        keys_ref,
        values_ref,
        att_ref,
    ) = refs[pieces:]
    received = jnp.concatenate([r[...] for r in refs[:pieces]], axis=0)
    keys_ref[...] = dot(received, w_key_ref[...]).astype(BF16)
    normed_tokens = rms(received.astype(F32)).astype(BF16)
    values_ref[...] = dot(w_value_ref[...], normed_tokens, ((0,), (1,))).astype(BF16)
    row_body(keys_ref, values_ref, *rest, att_ref, row=1)


def row_body(
    keys_ref,
    values_ref,
    q_ref,
    bias_ref,
    points_ref,
    side_ref,
    w_out_ref,
    w_hid_ref,
    w_down_ref,
    joined_ref,
    conv_ref,
    *refs,
    row,
):
    att_ref = refs[-1]
    width, cols = att_ref.shape
    lanes = slice(row * cols, (row + 1) * cols)
    head_width = width // HEADS
    keys = keys_ref[...]
    ones = jnp.ones((16, keys.shape[0]), BF16)
    for head in range(HEADS):
        low, high = head * head_width, (head + 1) * head_width
        scores = dot(keys[:, low:high], q_ref[low:high, lanes]) + bias_ref[:, lanes]
        top = jnp.max(scores, axis=0, keepdims=True)
        weights = jnp.exp2(scores - top).astype(BF16)
        lhs = jnp.concatenate([values_ref[low:high, :], ones], axis=0)
        mixed = dot(lhs, weights)
        att_ref[low:high, :] = (mixed[:head_width] / mixed[head_width : head_width + 1]).astype(BF16)
    residual = points_ref[lanes].astype(F32) + dot(att_ref[...], w_out_ref[...], ((0,), (0,)))
    normed = rms(residual).astype(BF16)
    pre = dot(normed, w_hid_ref[...]) + side_ref[lanes]
    c1 = math.sqrt(2.0 / math.pi)
    half = 0.5 * pre
    inner = (half + half * jnp.tanh(pre * (c1 + (c1 * 0.044715) * (pre * pre)))).astype(BF16)
    joined = residual + dot(inner, w_down_ref[...])
    conv = rms(joined)
    joined_ref[...] = joined
    conv_ref[...] = conv.astype(BF16)
    if len(refs) == 2:
        refs[0][...] = jnp.concatenate([conv[:1], conv[cols - 1 :]], axis=0).astype(BF16)


def ends_of(ref):
    cols = ref.shape[0]
    if cols == 2:
        both = ref[...].astype(F32)
        return both[:1], both[1:]
    return ref[:PAD].astype(F32)[:1], ref[cols - PAD :].astype(F32)[PAD - 1 :]


def edges_body(az_ref, halo_ends_ref, near_ref, far_ref, far_halo_ref, inner_ref, outer_ref):
    both = [ends_of(r) for r in (halo_ends_ref, near_ref, far_ref, far_halo_ref)]
    left = jnp.concatenate([x[0] for x in both], axis=0)
    right = jnp.concatenate([x[1] for x in both], axis=0)
    odd = lax.rem(az_ref[0], 2) == 1
    inner_ref[...] = jnp.where(odd, left, right).astype(BF16)
    outer_ref[...] = jnp.where(odd, right, left).astype(BF16)


def conv_rows(pairs, w_ref, left=0.0, right=0.0):
    taps = []
    for dc in range(3):
        total = None
        for x, base in pairs:
            part = dot(x, w_ref[base + dc])
            total = part if total is None else total + part
        taps.append(total)
    cols = taps[0].shape[0]
    row = lax.broadcasted_iota(jnp.int32, taps[0].shape, 0)
    before = jnp.where(row == 0, left, pltpu.roll(taps[0], 1, 0))
    after = jnp.where(row == cols - 1, right, pltpu.roll(taps[2], cols - 1, 0))
    return taps[1] + before + after


def inside_body(el_ref, near_ref, far_ref, joined_near_ref, joined_far_ref, w_ref, near_out, far_out):
    odd = lax.rem(el_ref[0], 2)
    near, far = near_ref[...], far_ref[...]
    near_out[...] = joined_near_ref[...] + conv_rows([(near, 3), (far, 6 * odd)], w_ref)
    far_out[...] = joined_far_ref[...] + conv_rows([(far, 3), (near, 6 - 6 * odd)], w_ref)


def border_body(
    el_ref,
    az_ref,
    near_ref,
    far_ref,
    inner_ref,
    outer_ref,
    near_part_ref,
    far_part_ref,
    w_ref,
    out_ref,
    *,
    last,
):
    el = el_ref[0]
    odd = lax.rem(el, 2)
    to_near, to_far = 6 - 6 * odd, 6 * odd
    outside = jnp.logical_or(el == 0, el == last)
    inner, outer = inner_ref[...].astype(F32), outer_ref[...].astype(F32)
    odd_az = lax.rem(az_ref[0], 2) == 1
    near_ends, far_ends = [], []
    for side, x in enumerate((jnp.where(odd_az, inner, outer), jnp.where(odd_az, outer, inner))):
        line = lax.broadcasted_iota(jnp.int32, x.shape, 0)
        x = jnp.where(jnp.logical_and(outside, line == 3), 0.0, x)
        x = jnp.concatenate([x, jnp.zeros((PAD - 4, x.shape[1]), F32)], axis=0).astype(BF16)
        a, m, b = (dot(x, w_ref[base + 2 * side]) for base in (to_near, 3, to_far))
        near_ends.append(a[0:1] + m[1:2] + b[2:3])
        far_ends.append(a[1:2] + m[2:3] + b[3:4])
    far = far_ref[...]
    far = jnp.where(outside, jnp.zeros_like(far), far)
    out_ref[odd] = (far_part_ref[...] + conv_rows([(far, to_far)], w_ref, *far_ends)).astype(BF16)
    near = conv_rows([(near_ref[...], to_near)], w_ref, *near_ends)
    out_ref[1 - odd] = (near_part_ref[...] + near).astype(BF16)


def per_device(
    points,
    skip,
    tokens,
    send_slots,
    recv_idx,
    w_query,
    w_key,
    w_value,
    w_out,
    w_hid,
    w_skip,
    w_down,
    w_conv,
):
    rows, cols, width = points.shape
    count = rows * cols
    own_tokens = tokens[0, 0]
    slots = send_slots[0, 0]
    offsets, groups, capacity = slots.shape
    table = offsets * groups * capacity
    el = lax.axis_index("el").astype(jnp.int32).reshape(1)
    az = lax.axis_index("az").astype(jnp.int32).reshape(1)
    shape = jax.ShapeDtypeStruct
    dma = pltpu.SemaphoreType.DMA
    sent = call(
        gather_body,
        [shape((offsets, capacity, width), BF16)] * groups,
        [el, az, own_tokens, slots],
        "gather",
        (2 * table * own_tokens.shape[0] * width, 0),
        [SMEM, SMEM, HBM, HBM],
        [VMEM(own_tokens.shape, BF16), VMEM(slots.shape, jnp.int32), dma((2,))],
    )
    got = {0: sent[0]}
    for s in reversed(range(1, groups)):
        got[s] = swap(sent[s], "el", lambda i, n, s=s: i ^ s)
    pieces = []
    for piece in range(offsets):
        bundle = jnp.concatenate([got[s][piece] for s in range(groups)], axis=0)
        pieces.append(swap(bundle, "az", MATCHES[piece]) if piece else bundle)
    held = [w_query, w_skip, w_key, w_value, w_out, w_hid, w_down, w_conv]
    idx = jnp.swapaxes(recv_idx, 1, 2)
    bias, points_v, skip_v, *held = call(
        functools.partial(load_body, groups=groups, capacity=capacity, held=len(held)),
        [
            shape((table, count), F32),
            shape((count, width), BF16),
            shape((count, width), BF16),
        ]
        + [shape(w.shape, BF16) for w in held],
        [el, az, points, skip, idx] + held,
        "load",
        (table * count * 48, table * count),
        [SMEM, SMEM] + [HBM] * (3 + len(held)),
        [VMEM(idx.shape, jnp.int32), dma((6 + len(held),))],
    )
    query_t, side = call(
        query_body,
        [shape((width, count), BF16), shape((count, w_skip.shape[1]), F32)],
        [points_v, skip_v, held[0], held[1], pieces[0]],
        "query",
        (2 * count * width * 5 * width, 0),
    )
    w_key, w_value, w_out, w_hid, w_down, w_conv = held[2:]
    row_f32, row_bf16 = shape((cols, width), F32), shape((cols, width), BF16)
    work = (5 * table * count * width + count * width * 9 * width, table * cols * HEADS)
    shared = [query_t, bias, points_v, side, w_out, w_hid, w_down]
    joined_far, far, keys, values = call(
        functools.partial(table_body, pieces=len(pieces)),
        [row_f32, row_bf16, shape((table, width), BF16), shape((width, table), BF16)],
        pieces + [w_key, w_value] + shared,
        "far_row",
        work,
        None,
        [VMEM((width, cols), BF16)],
    )
    far_got = swap(far, "el", inner_pair)
    joined_near, near, near_ends = call(
        functools.partial(row_body, row=0),
        [row_f32, row_bf16, shape((2, width), BF16)],
        [keys, values] + shared,
        "near_row",
        work,
        None,
        [VMEM((width, cols), BF16)],
    )
    halo_ends = swap(near_ends, "el", same_chip)
    near_got = swap(near, "el", same_chip)
    inner_edge, outer_edge = call(
        edges_body,
        [shape((4, width), BF16)] * 2,
        [az, halo_ends, near, far, far_got],
        "edges",
        (16 * width, 0),
        [SMEM] + [VMEM] * 4,
    )
    outer_got = swap(outer_edge, "az", next_chip)
    inner_got = swap(inner_edge, "az", same_chip)
    near_part, far_part = call(
        inside_body,
        [row_f32, row_f32],
        [el, near, far, joined_near, joined_far, w_conv],
        "inside",
        (2 * count * width * width * 6, 0),
        [SMEM] + [VMEM] * 5,
    )
    (out,) = call(
        functools.partial(border_body, last=lax.axis_size("el") - 1),
        [shape((rows, cols, width), BF16)],
        [el, az, near_got, far_got, inner_got, outer_got, near_part, far_part, w_conv],
        "border",
        (2 * count * width * width * 3, 0),
        [SMEM, SMEM] + [VMEM] * 7,
    )
    return out


def solution(mesh):
    return jax.shard_map(
        per_device,
        mesh=mesh,
        in_specs=(
            P("el", "az", None),
            P("el", "az", None),
            P("az", "el", None, None),
            P("az", "el", None, None, None),
            P("el", "az", None),
            P(),
            P(),
            P(),
            P(),
            P(),
            P(),
            P(),
            P(),
        ),
        out_specs=P("el", "az", None),
        check_vma=False,
    )
```

```python
import functools
import math

import jax
import jax.numpy as jnp
from jax import lax
from jax.experimental import pallas as pl
from jax.experimental.pallas import tpu as pltpu
from jax.sharding import PartitionSpec as P

HEADS = 8
REACH = 2
PAD = 16
BF16 = jnp.bfloat16
F32 = jnp.float32
VMEM = pltpu.VMEM
SMEM = pltpu.SMEM
HBM = pltpu.HBM


def same_chip(i, n):
    return i ^ 1


def next_chip(i, n):
    return (i + 1 if i % 2 else i - 1) % n


def two_on(i, n):
    return (i + 2 if i // 2 % 2 == 0 else i - 2) % n


def two_back(i, n):
    return (i - 2 if i // 2 % 2 == 0 else i + 2) % n


def inner_pair(i, n):
    return i if i in (0, n - 1) else next_chip(i, n)


def swap(x, axis, partner):
    n = lax.axis_size(axis)
    return lax.ppermute(x, axis, [(i, partner(i, n)) for i in range(n)])


def sent_offset(az, piece):
    odd, odd_chip = lax.rem(az, 2), lax.rem(lax.div(az, 2), 2)
    return (REACH, 4 * odd_chip, 1 + 2 * odd, 4 - 4 * odd_chip, 3 - 2 * odd)[piece]


MATCHES = (None, two_back, next_chip, two_on, same_chip)


def dot(a, b, contract=((1,), (0,))):
    return lax.dot_general(a, b, (contract, ((), ())), preferred_element_type=F32)


def rms(x):
    return x * lax.rsqrt(jnp.mean(x * x, axis=-1, keepdims=True) + 1e-06)


def call(body, outs, ins, name, cost, spaces=None, scratch=(), aliases=None):
    spaces = spaces or [VMEM] * len(ins)
    flops, transcendentals = cost
    moved = sum(x.size * x.dtype.itemsize for x in list(ins) + list(outs))
    ins = [
        pltpu.with_memory_space_constraint(x, HBM) if s == HBM else x
        for x, s in zip(ins, spaces)
    ]
    return pl.pallas_call(
        body,
        out_shape=outs,
        in_specs=[pl.BlockSpec(memory_space=s) for s in spaces],
        out_specs=[pl.BlockSpec(memory_space=VMEM) for _ in outs],
        scratch_shapes=list(scratch),
        input_output_aliases=aliases or {},
        compiler_params=pltpu.CompilerParams(vmem_limit_bytes=32 * 1024 * 1024),
        cost_estimate=pl.CostEstimate(
            flops=flops, bytes_accessed=moved, transcendentals=transcendentals
        ),
        name=name,
    )(*ins)


def gather_body(el_ref, az_ref, tokens_hbm, slots_hbm, *refs):
    out_refs, (tokens_ref, slots_ref, sems) = refs[:-3], refs[-3:]
    copies = [
        pltpu.make_async_copy(tokens_hbm, tokens_ref, sems.at[0]),
        pltpu.make_async_copy(slots_hbm, slots_ref, sems.at[1]),
    ]
    for c in copies:
        c.start()
    offsets, groups, capacity = slots_ref.shape
    rows = tokens_ref.shape[0]
    el, az = el_ref[0], az_ref[0]
    eye = lax.broadcasted_iota(jnp.int32, (capacity, capacity), 0) == lax.broadcasted_iota(
        jnp.int32, (capacity, capacity), 1
    )
    lane = lax.broadcasted_iota(jnp.int32, (capacity, rows), 1).astype(F32)
    for c in copies:
        c.wait()
    tokens = tokens_ref[...]
    for step in range(groups):
        target = lax.bitwise_xor(el, step)
        picks = []
        for piece in range(offsets):
            row = slots_ref[sent_offset(az, piece), pl.ds(target, 1), :].astype(F32)
            spread = jnp.broadcast_to(row, (capacity, capacity))
            column = jnp.sum(jnp.where(eye, spread, 0.0), axis=-1, keepdims=True)
            picks.append(jnp.where(column == lane, 1.0, 0.0))
        one_hot = jnp.concatenate(picks, axis=0).astype(BF16)
        chosen = dot(one_hot, tokens).astype(BF16)
        out_refs[step][...] = chosen.reshape(out_refs[step].shape)


def load_body(*refs, groups, capacity, held):
    el_ref, az_ref, points_hbm, skip_hbm, idx_hbm = refs[:5]
    held_hbm = refs[5 : 5 + held]
    bias_ref, points_ref, skip_ref = refs[5 + held : 8 + held]
    held_refs = refs[8 + held : 8 + 2 * held]
    idx_ref, sems = refs[8 + 2 * held :]
    el, az = el_ref[0], az_ref[0]
    even = 1 - lax.rem(el, 2)
    cols = points_ref.shape[0] // 2
    count = 2 * cols
    first, later = [], []
    for r, at in enumerate((even, 1 - even)):
        rows = pl.ds(r * cols, cols)
        first.append(pltpu.make_async_copy(idx_hbm.at[at], idx_ref.at[r], sems.at[r]))
        later.append(pltpu.make_async_copy(points_hbm.at[at], points_ref.at[rows], sems.at[2 + r]))
        later.append(pltpu.make_async_copy(skip_hbm.at[at], skip_ref.at[rows], sems.at[4 + r]))
    for k in range(held):
        later.append(pltpu.make_async_copy(held_hbm[k], held_refs[k], sems.at[6 + k]))
    for c in first + later:
        c.start()
    for c in first:
        c.wait()
    near = idx_ref.shape[1]
    lanes = 128
    for piece in range(bias_ref.shape[0] // (groups * capacity)):
        offset = 2 * REACH - sent_offset(az, piece)
        for step in range(groups):
            source = lax.bitwise_xor(el, step)
            low = (offset * groups + source) * capacity
            slot = low + lax.broadcasted_iota(jnp.int32, (capacity, lanes), 0)
            place = (piece * groups + step) * capacity
            for start in range(0, count, lanes):
                row, col = divmod(start, cols)
                total = jnp.zeros((capacity, lanes), F32)
                for n in range(near):
                    index = idx_ref[row, n : n + 1, col : col + lanes]
                    total = total + jnp.where(slot == index, 1.0, 0.0)
                bias_ref[place : place + capacity, start : start + lanes] = jnp.log2(total)
    for c in later:
        c.wait()


def query_body(points_ref, skip_ref, w_query_ref, w_skip_ref, after_ref, q_ref, side_ref):
    del after_ref
    scale = math.log2(math.e) / math.sqrt(q_ref.shape[0] // HEADS)
    query = dot(points_ref[...], w_query_ref[...]) * scale
    q_ref[...] = query.T.astype(BF16)
    side_ref[...] = dot(skip_ref[...], w_skip_ref[...])


def attend(keys, values_t, q_ref, bias_ref, score_ref, weight_ref, att_ref):
    table, width = keys.shape
    count = q_ref.shape[1]
    head_width = width // HEADS
    lanes = 128
    for head in range(HEADS):
        low, high = head * head_width, (head + 1) * head_width
        score_ref[head] = dot(keys[:, low:high], q_ref[low:high, :]) + bias_ref[...]
    for head in range(HEADS):
        for start in range(0, count, lanes):
            x = score_ref[head, :, start : start + lanes]
            top = jnp.max(jnp.max(x.reshape(table // 64, 8, 8, lanes), axis=0), axis=0)
            top = jnp.max(top, axis=0, keepdims=True)
            weight_ref[head, :, start : start + lanes] = jnp.exp2(x - top).astype(BF16)
    ones = jnp.ones((16, table), BF16)
    for head in range(HEADS):
        low, high = head * head_width, (head + 1) * head_width
        lhs = jnp.concatenate([values_t[low:high, :], ones], axis=0)
        mixed = dot(lhs, weight_ref[head])
        scale = 1.0 / mixed[head_width : head_width + 1]
        att_ref[low:high, :] = (mixed[:head_width] * scale).astype(BF16)


def join(points_ref, side_ref, att_ref, w_out_ref, w_hid_ref, w_down_ref):
    count = points_ref.shape[0]
    size = count // 2
    c1 = math.sqrt(2.0 / math.pi)
    residuals, pres, out = [], [], []
    for start in range(0, count, size):
        part = slice(start, start + size)
        residuals.append(
            points_ref[part].astype(F32) + dot(att_ref[:, part], w_out_ref[...], ((0,), (0,)))
        )
    for at, residual in enumerate(residuals):
        part = slice(at * size, (at + 1) * size)
        pres.append(dot(rms(residual).astype(BF16), w_hid_ref[...]) + side_ref[part])
    for residual, pre in zip(residuals, pres):
        half = 0.5 * pre
        inner = half + half * jnp.tanh(pre * (c1 + (c1 * 0.044715) * (pre * pre)))
        out.append(residual + dot(inner.astype(BF16), w_down_ref[...]))
    return out


def main_body(az_ref, *refs, pieces):
    piece_refs = refs[:pieces]
    (
        q_ref,
        bias_ref,
        points_ref,
        side_ref,
        w_key_ref,
        w_value_ref,
        w_out_ref,
        w_hid_ref,
        w_down_ref,
        joined_ref,
        near_ref,
        far_ref,
        inner_edge_ref,
        outer_edge_ref,
        score_ref,
        weight_ref,
        att_ref,
    ) = refs[pieces:]
    width, count = q_ref.shape
    received = jnp.concatenate([r[...] for r in piece_refs], axis=0)
    keys = dot(received, w_key_ref[...]).astype(BF16)
    normed_tokens = rms(received.astype(F32)).astype(BF16)
    values_t = dot(w_value_ref[...], normed_tokens, ((0,), (1,))).astype(BF16)
    attend(keys, values_t, q_ref, bias_ref, score_ref, weight_ref, att_ref)
    joined = join(points_ref, side_ref, att_ref, w_out_ref, w_hid_ref, w_down_ref)
    conv = []
    for at, x in enumerate(joined):
        joined_ref[at] = x
        conv.append(rms(x))
    cols = count // 2
    near_ref[0:cols] = conv[0].astype(BF16)
    far_ref[0:cols] = conv[1].astype(BF16)
    left = jnp.concatenate([x[:1] for x in conv], axis=0)
    right = jnp.concatenate([x[cols - 1 :] for x in conv], axis=0)
    odd = lax.rem(az_ref[0], 2) == 1
    inner_edge_ref[...] = jnp.where(odd, left, right).astype(BF16)
    outer_edge_ref[...] = jnp.where(odd, right, left).astype(BF16)


def pack_body(az_ref, inner_ref, outer_ref, near_in, far_in, near_ref, far_ref):
    del near_in, far_in
    odd = lax.rem(az_ref[0], 2) == 1
    inner, outer = inner_ref[...].astype(F32), outer_ref[...].astype(F32)
    right = jnp.where(odd, outer, inner)
    left = jnp.where(odd, inner, outer)
    cols, width = near_ref.shape[0] - PAD, near_ref.shape[1]
    row = lax.broadcasted_iota(jnp.int32, (PAD, width), 0)
    for at, ref in enumerate((near_ref, far_ref)):
        rows = jnp.where(row == 0, right[at : at + 1], 0.0)
        rows = jnp.where(row == PAD - 1, left[at : at + 1], rows)
        ref[cols:, :] = rows.astype(BF16)


def conv_rows(pairs, cols):
    taps = []
    for dc in range(3):
        total = None
        for x, w_ref, base in pairs:
            part = dot(x, w_ref[base + dc])
            total = part if total is None else total + part
        taps.append(total)
    length = taps[0].shape[0]
    shifted = taps[1] + pltpu.roll(taps[0], 1, 0) + pltpu.roll(taps[2], length - 1, 0)
    return shifted[:cols]


def inside_body(el_ref, near_ref, far_ref, joined_ref, w_ref, out_ref):
    odd = lax.rem(el_ref[0], 2)
    cols = joined_ref.shape[1]
    near, far = near_ref[...], far_ref[...]
    out_ref[0] = joined_ref[0] + conv_rows([(near, w_ref, 3), (far, w_ref, 6 * odd)], cols)
    out_ref[1] = joined_ref[1] + conv_rows([(far, w_ref, 3), (near, w_ref, 6 - 6 * odd)], cols)


def border_body(el_ref, near_ref, far_ref, part_ref, w_ref, out_ref, *, last):
    el = el_ref[0]
    odd = lax.rem(el, 2)
    cols = part_ref.shape[1]
    near = part_ref[0] + conv_rows([(near_ref[...], w_ref, 6 - 6 * odd)], cols)
    out_ref[1 - odd] = near.astype(BF16)
    far = conv_rows([(far_ref[...], w_ref, 6 * odd)], cols)
    ends = jnp.logical_or(el == 0, el == last)
    out_ref[odd] = (part_ref[1] + jnp.where(ends, 0.0, far)).astype(BF16)


def per_device(
    points,
    skip,
    tokens,
    send_slots,
    recv_idx,
    w_query,
    w_key,
    w_value,
    w_out,
    w_hid,
    w_skip,
    w_down,
    w_conv,
):
    rows, cols, width = points.shape
    count = rows * cols
    own_tokens = tokens[0, 0]
    slots = send_slots[0, 0]
    offsets, groups, capacity = slots.shape
    table = offsets * groups * capacity
    el = lax.axis_index("el").astype(jnp.int32).reshape(1)
    az = lax.axis_index("az").astype(jnp.int32).reshape(1)
    shape = jax.ShapeDtypeStruct
    dma = pltpu.SemaphoreType.DMA
    sent = call(
        gather_body,
        [shape((offsets, capacity, width), BF16)] * groups,
        [el, az, own_tokens, slots],
        "gather",
        (2 * table * own_tokens.shape[0] * width, 0),
        [SMEM, SMEM, HBM, HBM],
        [VMEM(own_tokens.shape, BF16), VMEM(slots.shape, jnp.int32), dma((2,))],
    )
    got = {0: sent[0]}
    for s in reversed(range(1, groups)):
        got[s] = swap(sent[s], "el", lambda i, n, s=s: i ^ s)
    pieces = []
    for piece in range(offsets):
        bundle = jnp.concatenate([got[s][piece] for s in range(groups)], axis=0)
        pieces.append(swap(bundle, "az", MATCHES[piece]) if piece else bundle)
    held = [w_query, w_skip, w_key, w_value, w_out, w_hid, w_down, w_conv]
    idx = jnp.swapaxes(recv_idx, 1, 2)
    bias, points_v, skip_v, *held = call(
        functools.partial(load_body, groups=groups, capacity=capacity, held=len(held)),
        [
            shape((table, count), F32),
            shape((count, width), BF16),
            shape((count, width), BF16),
        ]
        + [shape(w.shape, BF16) for w in held],
        [el, az, points, skip, idx] + held,
        "load",
        (table * count * 48, table * count),
        [SMEM, SMEM] + [HBM] * (3 + len(held)),
        [VMEM(idx.shape, jnp.int32), dma((6 + len(held),))],
    )
    query_t, side = call(
        query_body,
        [shape((width, count), BF16), shape((count, w_skip.shape[1]), F32)],
        [points_v, skip_v, held[0], held[1], pieces[0]],
        "query",
        (2 * count * width * 5 * width, 0),
    )
    joined, near, far, inner_edge, outer_edge = call(
        functools.partial(main_body, pieces=len(pieces)),
        [
            shape((rows, cols, width), F32),
            shape((cols + PAD, width), BF16),
            shape((cols + PAD, width), BF16),
            shape((2, width), BF16),
            shape((2, width), BF16),
        ],
        [az] + pieces + [query_t, bias, points_v, side] + held[2:-1],
        "main",
        (10 * table * count * width + 2 * count * width * 13 * width, table * count * HEADS),
        [SMEM] + [VMEM] * (len(pieces) + 9),
        [
            VMEM((HEADS, table, count), F32),
            VMEM((HEADS, table, count), BF16),
            VMEM((width, count), BF16),
        ],
    )
    outer_got = swap(outer_edge, "az", next_chip)
    inner_got = swap(inner_edge, "az", same_chip)
    near, far = call(
        pack_body,
        [shape((cols + PAD, width), BF16)] * 2,
        [az, inner_got, outer_got, near, far],
        "pack",
        (4 * PAD * width, 0),
        [SMEM] + [VMEM] * 4,
        (),
        {3: 0, 4: 1},
    )
    far_got = swap(far, "el", inner_pair)
    near_got = swap(near, "el", same_chip)
    (partial,) = call(
        inside_body,
        [shape((rows, cols, width), F32)],
        [el, near, far, joined, held[-1]],
        "inside",
        (2 * count * width * width * 6, 0),
        [SMEM] + [VMEM] * 4,
    )
    (out,) = call(
        functools.partial(border_body, last=lax.axis_size("el") - 1),
        [shape((rows, cols, width), BF16)],
        [el, near_got, far_got, partial, held[-1]],
        "border",
        (2 * count * width * width * 3, 0),
        [SMEM] + [VMEM] * 4,
    )
    return out


def solution(mesh):
    return jax.shard_map(
        per_device,
        mesh=mesh,
        in_specs=(
            P("el", "az", None),
            P("el", "az", None),
            P("az", "el", None, None),
            P("az", "el", None, None, None),
            P("el", "az", None),
            P(),
            P(),
            P(),
            P(),
            P(),
            P(),
            P(),
            P(),
        ),
        out_specs=P("el", "az", None),
        check_vma=False,
    )
```

```python
import functools
import math

import jax
import jax.numpy as jnp
from jax import lax
from jax.experimental import pallas as pl
from jax.experimental.pallas import tpu as pltpu
from jax.sharding import PartitionSpec as P

HEADS = 8
REACH = 2
PAD = 16
BF16 = jnp.bfloat16
F32 = jnp.float32
VMEM = pltpu.VMEM
SMEM = pltpu.SMEM
HBM = pltpu.HBM


def same_chip(i, n):
    return i ^ 1


def next_chip(i, n):
    return (i + 1 if i % 2 else i - 1) % n


def two_on(i, n):
    return (i + 2 if i // 2 % 2 == 0 else i - 2) % n


def two_back(i, n):
    return (i - 2 if i // 2 % 2 == 0 else i + 2) % n


def inner_pair(i, n):
    return i if i in (0, n - 1) else next_chip(i, n)


def swap(x, axis, partner):
    n = lax.axis_size(axis)
    return lax.ppermute(x, axis, [(i, partner(i, n)) for i in range(n)])


def sent_offset(az, piece):
    odd, odd_chip = lax.rem(az, 2), lax.rem(lax.div(az, 2), 2)
    return (REACH, 4 * odd_chip, 1 + 2 * odd, 4 - 4 * odd_chip, 3 - 2 * odd)[piece]


MATCHES = (None, two_back, next_chip, two_on, same_chip)


def dot(a, b, contract=((1,), (0,))):
    return lax.dot_general(a, b, (contract, ((), ())), preferred_element_type=F32)


def rms(x):
    return x * lax.rsqrt(jnp.mean(x * x, axis=-1, keepdims=True) + 1e-06)


def call(body, outs, ins, name, cost, spaces=None, scratch=(), aliases=None):
    spaces = spaces or [VMEM] * len(ins)
    flops, transcendentals = cost
    moved = sum(x.size * x.dtype.itemsize for x in list(ins) + list(outs))
    ins = [
        pltpu.with_memory_space_constraint(x, HBM) if s == HBM else x
        for x, s in zip(ins, spaces)
    ]
    return pl.pallas_call(
        body,
        out_shape=outs,
        in_specs=[pl.BlockSpec(memory_space=s) for s in spaces],
        out_specs=[pl.BlockSpec(memory_space=VMEM) for _ in outs],
        scratch_shapes=list(scratch),
        input_output_aliases=aliases or {},
        compiler_params=pltpu.CompilerParams(vmem_limit_bytes=32 * 1024 * 1024),
        cost_estimate=pl.CostEstimate(
            flops=flops, bytes_accessed=moved, transcendentals=transcendentals
        ),
        name=name,
    )(*ins)


def gather_body(el_ref, az_ref, tokens_hbm, slots_hbm, *refs):
    out_refs, (tokens_ref, slots_ref, sems) = refs[:-3], refs[-3:]
    copies = [
        pltpu.make_async_copy(tokens_hbm, tokens_ref, sems.at[0]),
        pltpu.make_async_copy(slots_hbm, slots_ref, sems.at[1]),
    ]
    for c in copies:
        c.start()
    offsets, groups, capacity = slots_ref.shape
    rows = tokens_ref.shape[0]
    el, az = el_ref[0], az_ref[0]
    eye = lax.broadcasted_iota(jnp.int32, (capacity, capacity), 0) == lax.broadcasted_iota(
        jnp.int32, (capacity, capacity), 1
    )
    lane = lax.broadcasted_iota(jnp.int32, (capacity, rows), 1).astype(F32)
    for c in copies:
        c.wait()
    tokens = tokens_ref[...]
    for step in range(groups):
        target = lax.bitwise_xor(el, step)
        picks = []
        for piece in range(offsets):
            row = slots_ref[sent_offset(az, piece), pl.ds(target, 1), :].astype(F32)
            spread = jnp.broadcast_to(row, (capacity, capacity))
            column = jnp.sum(jnp.where(eye, spread, 0.0), axis=-1, keepdims=True)
            picks.append(jnp.where(column == lane, 1.0, 0.0))
        one_hot = jnp.concatenate(picks, axis=0).astype(BF16)
        chosen = dot(one_hot, tokens).astype(BF16)
        out_refs[step][...] = chosen.reshape(out_refs[step].shape)


def load_body(*refs, groups, capacity, held):
    el_ref, az_ref, points_hbm, skip_hbm, idx_hbm = refs[:5]
    held_hbm = refs[5 : 5 + held]
    bias_ref, points_ref, skip_ref = refs[5 + held : 8 + held]
    held_refs = refs[8 + held : 8 + 2 * held]
    idx_ref, sems = refs[8 + 2 * held :]
    el, az = el_ref[0], az_ref[0]
    even = 1 - lax.rem(el, 2)
    cols = points_ref.shape[0] // 2
    count = 2 * cols
    first, later = [], []
    turn = cols // 4
    spans = [
        (even, turn, 0, 2 * turn),
        (even, 3 * turn, 2 * turn, turn),
        (even, 0, 3 * turn, turn),
        (1 - even, 0, cols, cols),
    ]
    for r, at in enumerate((even, 1 - even)):
        first.append(pltpu.make_async_copy(idx_hbm.at[at], idx_ref.at[r], sems.at[r]))
    for r, (at, low, to, size) in enumerate(spans):
        rows, place = pl.ds(low, size), pl.ds(to, size)
        later.append(
            pltpu.make_async_copy(points_hbm.at[at, rows], points_ref.at[place], sems.at[2 + r])
        )
        later.append(
            pltpu.make_async_copy(skip_hbm.at[at, rows], skip_ref.at[place], sems.at[6 + r])
        )
    for k in range(held):
        later.append(pltpu.make_async_copy(held_hbm[k], held_refs[k], sems.at[10 + k]))
    for c in first + later:
        c.start()
    for c in first:
        c.wait()
    idx_ref[0] = pltpu.roll(idx_ref[0], cols - turn, 1)
    near = idx_ref.shape[1]
    lanes = 128
    for piece in range(bias_ref.shape[0] // (groups * capacity)):
        offset = 2 * REACH - sent_offset(az, piece)
        for step in range(groups):
            source = lax.bitwise_xor(el, step)
            low = (offset * groups + source) * capacity
            slot = low + lax.broadcasted_iota(jnp.int32, (capacity, lanes), 0)
            place = (piece * groups + step) * capacity
            for start in range(0, count, lanes):
                row, col = divmod(start, cols)
                total = jnp.zeros((capacity, lanes), F32)
                for n in range(near):
                    index = idx_ref[row, n : n + 1, col : col + lanes]
                    total = total + jnp.where(slot == index, 1.0, 0.0)
                bias_ref[place : place + capacity, start : start + lanes] = jnp.log2(total)
    for c in later:
        c.wait()


def query_body(points_ref, skip_ref, w_query_ref, w_skip_ref, after_ref, q_ref, side_ref):
    del after_ref
    scale = math.log2(math.e) / math.sqrt(q_ref.shape[0] // HEADS)
    query = dot(points_ref[...], w_query_ref[...]) * scale
    q_ref[...] = query.T.astype(BF16)
    side_ref[...] = dot(skip_ref[...], w_skip_ref[...])


def attend(keys, values_t, q_ref, bias_ref, score_ref, weight_ref, att_ref, first):
    table, width = keys.shape
    count = att_ref.shape[1]
    part = slice(first, first + count)
    head_width = width // HEADS
    lanes = 128
    for head in range(HEADS):
        low, high = head * head_width, (head + 1) * head_width
        score_ref[head] = dot(keys[:, low:high], q_ref[low:high, part]) + bias_ref[:, part]
    for head in range(HEADS):
        for start in range(0, count, lanes):
            x = score_ref[head, :, start : start + lanes]
            top = jnp.max(jnp.max(x.reshape(table // 64, 8, 8, lanes), axis=0), axis=0)
            top = jnp.max(top, axis=0, keepdims=True)
            weight_ref[head, :, start : start + lanes] = jnp.exp2(x - top).astype(BF16)
    ones = jnp.ones((16, table), BF16)
    for head in range(HEADS):
        low, high = head * head_width, (head + 1) * head_width
        lhs = jnp.concatenate([values_t[low:high, :], ones], axis=0)
        mixed = dot(lhs, weight_ref[head])
        scale = 1.0 / mixed[head_width : head_width + 1]
        att_ref[low:high, :] = (mixed[:head_width] * scale).astype(BF16)


def join(points_ref, side_ref, att_ref, w_out_ref, w_hid_ref, w_down_ref, first, sizes):
    c1 = math.sqrt(2.0 / math.pi)
    residuals, pres, out = [], [], []
    starts = [sum(sizes[:k]) for k in range(len(sizes))]
    for start, size in zip(starts, sizes):
        rows = slice(first + start, first + start + size)
        mixed = att_ref[:, start : start + size]
        residuals.append(
            points_ref[rows].astype(F32) + dot(mixed, w_out_ref[...], ((0,), (0,)))
        )
    for start, size, residual in zip(starts, sizes, residuals):
        rows = slice(first + start, first + start + size)
        pres.append(dot(rms(residual).astype(BF16), w_hid_ref[...]) + side_ref[rows])
    for residual, pre in zip(residuals, pres):
        half = 0.5 * pre
        inner = half + half * jnp.tanh(pre * (c1 + (c1 * 0.044715) * (pre * pre)))
        out.append(residual + dot(inner.astype(BF16), w_down_ref[...]))
    return out


def block_body(*refs, pieces, first):
    (
        w_key_ref,
        w_value_ref,
        q_ref,
        bias_ref,
        points_ref,
        side_ref,
        w_out_ref,
        w_hid_ref,
        w_down_ref,
        joined_ref,
        block_ref,
        ends_ref,
        keys_ref,
        values_ref,
        score_ref,
        weight_ref,
        att_ref,
    ) = refs[pieces:]
    received = jnp.concatenate([r[...] for r in refs[:pieces]], axis=0)
    keys = dot(received, w_key_ref[...]).astype(BF16)
    normed_tokens = rms(received.astype(F32)).astype(BF16)
    values_t = dot(w_value_ref[...], normed_tokens, ((0,), (1,))).astype(BF16)
    keys_ref[...], values_ref[...] = keys, values_t
    attend(keys, values_t, q_ref, bias_ref, score_ref, weight_ref, att_ref, first)
    size = block_ref.shape[0]
    (joined,) = join(
        points_ref, side_ref, att_ref, w_out_ref, w_hid_ref, w_down_ref, first, (size,)
    )
    joined_ref[...] = joined
    block = rms(joined)
    block_ref[...] = block.astype(BF16)
    turn = size // 2
    ends = jnp.concatenate([block[turn : turn + 1], block[turn - 1 : turn]], axis=0)
    ends_ref[...] = ends.astype(BF16)


def far_body(
    keys_ref,
    values_ref,
    q_ref,
    bias_ref,
    points_ref,
    side_ref,
    w_out_ref,
    w_hid_ref,
    w_down_ref,
    joined_ref,
    far_ref,
    score_ref,
    weight_ref,
    att_ref,
):
    cols = far_ref.shape[0]
    attend(
        keys_ref[...], values_ref[...], q_ref, bias_ref, score_ref, weight_ref, att_ref, cols
    )
    half = cols // 2
    parts = join(
        points_ref, side_ref, att_ref, w_out_ref, w_hid_ref, w_down_ref, cols, (half, half)
    )
    for at, part in enumerate(parts):
        joined_ref[at * half : (at + 1) * half] = part
        far_ref[at * half : (at + 1) * half] = rms(part).astype(BF16)


def near_body(
    keys_ref,
    values_ref,
    joined_ends_ref,
    block_ref,
    q_ref,
    bias_ref,
    points_ref,
    side_ref,
    w_out_ref,
    w_hid_ref,
    w_down_ref,
    joined_ref,
    near_ref,
    score_ref,
    weight_ref,
    att_ref,
):
    attend(
        keys_ref[...], values_ref[...], q_ref, bias_ref, score_ref, weight_ref, att_ref, 0
    )
    size = block_ref.shape[0]
    turn = size // 2
    (middle,) = join(
        points_ref, side_ref, att_ref, w_out_ref, w_hid_ref, w_down_ref, 0, (size,)
    )
    for ref, inner, ends_ref in (
        (joined_ref, middle, joined_ends_ref),
        (near_ref, rms(middle).astype(BF16), block_ref),
    ):
        ref[turn : turn + size] = inner
        ref[turn + size :] = ends_ref[:turn]
        ref[:turn] = ends_ref[turn:]


def ends_of(ref):
    cols = ref.shape[0]
    if cols == 2:
        both = ref[...].astype(F32)
        return both[:1], both[1:]
    return ref[:PAD].astype(F32)[:1], ref[cols - PAD :].astype(F32)[PAD - 1 :]


def edges_body(az_ref, halo_ends_ref, near_ref, far_ref, far_halo_ref, inner_ref, outer_ref):
    both = [ends_of(r) for r in (halo_ends_ref, near_ref, far_ref, far_halo_ref)]
    left = jnp.concatenate([x[0] for x in both], axis=0)
    right = jnp.concatenate([x[1] for x in both], axis=0)
    odd = lax.rem(az_ref[0], 2) == 1
    inner_ref[...] = jnp.where(odd, left, right).astype(BF16)
    outer_ref[...] = jnp.where(odd, right, left).astype(BF16)


def conv_rows(pairs, w_ref, left=0.0, right=0.0):
    taps = []
    for dc in range(3):
        total = None
        for x, base in pairs:
            part = dot(x, w_ref[base + dc])
            total = part if total is None else total + part
        taps.append(total)
    cols = taps[0].shape[0]
    row = lax.broadcasted_iota(jnp.int32, taps[0].shape, 0)
    before = jnp.where(row == 0, left, pltpu.roll(taps[0], 1, 0))
    after = jnp.where(row == cols - 1, right, pltpu.roll(taps[2], cols - 1, 0))
    return taps[1] + before + after


def inside_body(el_ref, near_ref, far_ref, joined_near_ref, joined_far_ref, w_ref, near_out, far_out):
    odd = lax.rem(el_ref[0], 2)
    near, far = near_ref[...], far_ref[...]
    near_out[...] = joined_near_ref[...] + conv_rows([(near, 3), (far, 6 * odd)], w_ref)
    far_out[...] = joined_far_ref[...] + conv_rows([(far, 3), (near, 6 - 6 * odd)], w_ref)


def border_body(
    el_ref,
    az_ref,
    near_ref,
    far_ref,
    inner_ref,
    outer_ref,
    near_part_ref,
    far_part_ref,
    w_ref,
    out_ref,
    *,
    last,
):
    el = el_ref[0]
    odd = lax.rem(el, 2)
    to_near, to_far = 6 - 6 * odd, 6 * odd
    outside = jnp.logical_or(el == 0, el == last)
    inner, outer = inner_ref[...].astype(F32), outer_ref[...].astype(F32)
    odd_az = lax.rem(az_ref[0], 2) == 1
    near_ends, far_ends = [], []
    for side, x in enumerate((jnp.where(odd_az, inner, outer), jnp.where(odd_az, outer, inner))):
        line = lax.broadcasted_iota(jnp.int32, x.shape, 0)
        x = jnp.where(jnp.logical_and(outside, line == 3), 0.0, x)
        x = jnp.concatenate([x, jnp.zeros((PAD - 4, x.shape[1]), F32)], axis=0).astype(BF16)
        a, m, b = (dot(x, w_ref[base + 2 * side]) for base in (to_near, 3, to_far))
        near_ends.append(a[0:1] + m[1:2] + b[2:3])
        far_ends.append(a[1:2] + m[2:3] + b[3:4])
    far = far_ref[...]
    far = jnp.where(outside, jnp.zeros_like(far), far)
    out_ref[odd] = (far_part_ref[...] + conv_rows([(far, to_far)], w_ref, *far_ends)).astype(BF16)
    near = conv_rows([(near_ref[...], to_near)], w_ref, *near_ends)
    out_ref[1 - odd] = (near_part_ref[...] + near).astype(BF16)


def per_device(
    points,
    skip,
    tokens,
    send_slots,
    recv_idx,
    w_query,
    w_key,
    w_value,
    w_out,
    w_hid,
    w_skip,
    w_down,
    w_conv,
):
    rows, cols, width = points.shape
    count = rows * cols
    own_tokens = tokens[0, 0]
    slots = send_slots[0, 0]
    offsets, groups, capacity = slots.shape
    table = offsets * groups * capacity
    el = lax.axis_index("el").astype(jnp.int32).reshape(1)
    az = lax.axis_index("az").astype(jnp.int32).reshape(1)
    shape = jax.ShapeDtypeStruct
    dma = pltpu.SemaphoreType.DMA
    sent = call(
        gather_body,
        [shape((offsets, capacity, width), BF16)] * groups,
        [el, az, own_tokens, slots],
        "gather",
        (2 * table * own_tokens.shape[0] * width, 0),
        [SMEM, SMEM, HBM, HBM],
        [VMEM(own_tokens.shape, BF16), VMEM(slots.shape, jnp.int32), dma((2,))],
    )
    got = {0: sent[0]}
    for s in reversed(range(1, groups)):
        got[s] = swap(sent[s], "el", lambda i, n, s=s: i ^ s)
    pieces = []
    for piece in range(offsets):
        bundle = jnp.concatenate([got[s][piece] for s in range(groups)], axis=0)
        pieces.append(swap(bundle, "az", MATCHES[piece]) if piece else bundle)
    held = [w_query, w_skip, w_key, w_value, w_out, w_hid, w_down, w_conv]
    idx = jnp.swapaxes(recv_idx, 1, 2)
    bias, points_v, skip_v, *held = call(
        functools.partial(load_body, groups=groups, capacity=capacity, held=len(held)),
        [
            shape((table, count), F32),
            shape((count, width), BF16),
            shape((count, width), BF16),
        ]
        + [shape(w.shape, BF16) for w in held],
        [el, az, points, skip, idx] + held,
        "load",
        (table * count * 48, table * count),
        [SMEM, SMEM] + [HBM] * (3 + len(held)),
        [VMEM(idx.shape, jnp.int32), dma((10 + len(held),))],
    )
    query_t, side = call(
        query_body,
        [shape((width, count), BF16), shape((count, w_skip.shape[1]), F32)],
        [points_v, skip_v, held[0], held[1], pieces[0]],
        "query",
        (2 * count * width * 5 * width, 0),
    )
    w_key, w_value, w_out, w_hid, w_down, w_conv = held[2:]
    half = cols // 2
    row_f32, row_bf16 = shape((cols, width), F32), shape((cols, width), BF16)

    def work(points):
        return (10 * table * points * width + 18 * points * width * width, table * points * HEADS)

    def room(points):
        return [
            VMEM((HEADS, table, points), F32),
            VMEM((HEADS, table, points), BF16),
            VMEM((width, points), BF16),
        ]

    shared = [query_t, bias, points_v, side, w_out, w_hid, w_down]
    joined_block, block, near_ends, keys, values = call(
        functools.partial(block_body, pieces=len(pieces), first=half),
        [
            shape((half, width), F32),
            shape((half, width), BF16),
            shape((2, width), BF16),
            shape((table, width), BF16),
            shape((width, table), BF16),
        ],
        pieces + [w_key, w_value] + shared,
        "near_ends",
        work(half),
        None,
        room(half),
    )
    halo_ends = swap(near_ends, "el", same_chip)
    joined_far, far = call(
        far_body,
        [row_f32, row_bf16],
        [keys, values] + shared,
        "far_row",
        work(cols),
        None,
        room(cols),
    )
    far, halo_ends = lax.optimization_barrier((far, halo_ends))
    far_got = swap(far, "el", inner_pair)
    joined_near, near = call(
        near_body,
        [row_f32, row_bf16],
        [keys, values, joined_block, block] + shared,
        "near_row",
        work(half),
        None,
        room(half),
    )
    near_got = swap(near, "el", same_chip)
    inner_edge, outer_edge = call(
        edges_body,
        [shape((4, width), BF16)] * 2,
        [az, halo_ends, near, far, far_got],
        "edges",
        (16 * width, 0),
        [SMEM] + [VMEM] * 4,
    )
    outer_got = swap(outer_edge, "az", next_chip)
    inner_got = swap(inner_edge, "az", same_chip)
    near_part, far_part = call(
        inside_body,
        [row_f32, row_f32],
        [el, near, far, joined_near, joined_far, w_conv],
        "inside",
        (2 * count * width * width * 6, 0),
        [SMEM] + [VMEM] * 5,
    )
    (out,) = call(
        functools.partial(border_body, last=lax.axis_size("el") - 1),
        [shape((rows, cols, width), BF16)],
        [el, az, near_got, far_got, inner_got, outer_got, near_part, far_part, w_conv],
        "border",
        (2 * count * width * width * 3, 0),
        [SMEM, SMEM] + [VMEM] * 7,
    )
    return out


def solution(mesh):
    return jax.shard_map(
        per_device,
        mesh=mesh,
        in_specs=(
            P("el", "az", None),
            P("el", "az", None),
            P("az", "el", None, None),
            P("az", "el", None, None, None),
            P("el", "az", None),
            P(),
            P(),
            P(),
            P(),
            P(),
            P(),
            P(),
            P(),
        ),
        out_specs=P("el", "az", None),
        check_vma=False,
    )
```

```python
import functools
import math

import jax
import jax.numpy as jnp
from jax import lax
from jax.experimental import pallas as pl
from jax.experimental.pallas import tpu as pltpu
from jax.sharding import PartitionSpec as P

HEADS = 8
REACH = 2
PAD = 16
BF16 = jnp.bfloat16
F32 = jnp.float32
VMEM = pltpu.VMEM
SMEM = pltpu.SMEM
HBM = pltpu.HBM


def same_chip(i, n):
    return i ^ 1


def next_chip(i, n):
    return (i + 1 if i % 2 else i - 1) % n


def two_on(i, n):
    return (i + 2 if i // 2 % 2 == 0 else i - 2) % n


def two_back(i, n):
    return (i - 2 if i // 2 % 2 == 0 else i + 2) % n


def inner_pair(i, n):
    return i if i in (0, n - 1) else next_chip(i, n)


def swap(x, axis, partner):
    n = lax.axis_size(axis)
    return lax.ppermute(x, axis, [(i, partner(i, n)) for i in range(n)])


def sent_offset(az, piece):
    odd, odd_chip = lax.rem(az, 2), lax.rem(lax.div(az, 2), 2)
    return (REACH, 4 * odd_chip, 1 + 2 * odd, 4 - 4 * odd_chip, 3 - 2 * odd)[piece]


MATCHES = (None, two_back, next_chip, two_on, same_chip)


def dot(a, b, contract=((1,), (0,))):
    return lax.dot_general(a, b, (contract, ((), ())), preferred_element_type=F32)


def rms(x):
    return x * lax.rsqrt(jnp.mean(x * x, axis=-1, keepdims=True) + 1e-06)


def call(body, outs, ins, name, cost, spaces=None, scratch=(), aliases=None):
    spaces = spaces or [VMEM] * len(ins)
    flops, transcendentals = cost
    moved = sum(x.size * x.dtype.itemsize for x in list(ins) + list(outs))
    ins = [
        pltpu.with_memory_space_constraint(x, HBM) if s == HBM else x
        for x, s in zip(ins, spaces)
    ]
    return pl.pallas_call(
        body,
        out_shape=outs,
        in_specs=[pl.BlockSpec(memory_space=s) for s in spaces],
        out_specs=[pl.BlockSpec(memory_space=VMEM) for _ in outs],
        scratch_shapes=list(scratch),
        input_output_aliases=aliases or {},
        compiler_params=pltpu.CompilerParams(vmem_limit_bytes=32 * 1024 * 1024),
        cost_estimate=pl.CostEstimate(
            flops=flops, bytes_accessed=moved, transcendentals=transcendentals
        ),
        name=name,
    )(*ins)


def gather_body(el_ref, az_ref, tokens_hbm, slots_hbm, *refs):
    out_refs, (tokens_ref, slots_ref, sems) = refs[:-3], refs[-3:]
    copies = [
        pltpu.make_async_copy(tokens_hbm, tokens_ref, sems.at[0]),
        pltpu.make_async_copy(slots_hbm, slots_ref, sems.at[1]),
    ]
    for c in copies:
        c.start()
    offsets, groups, capacity = slots_ref.shape
    rows = tokens_ref.shape[0]
    el, az = el_ref[0], az_ref[0]
    eye = lax.broadcasted_iota(jnp.int32, (capacity, capacity), 0) == lax.broadcasted_iota(
        jnp.int32, (capacity, capacity), 1
    )
    lane = lax.broadcasted_iota(jnp.int32, (capacity, rows), 1).astype(F32)
    for c in copies:
        c.wait()
    tokens = tokens_ref[...]
    for step in range(groups):
        target = lax.bitwise_xor(el, step)
        picks = []
        for piece in range(offsets):
            row = slots_ref[sent_offset(az, piece), pl.ds(target, 1), :].astype(F32)
            spread = jnp.broadcast_to(row, (capacity, capacity))
            column = jnp.sum(jnp.where(eye, spread, 0.0), axis=-1, keepdims=True)
            picks.append(jnp.where(column == lane, 1.0, 0.0))
        one_hot = jnp.concatenate(picks, axis=0).astype(BF16)
        chosen = dot(one_hot, tokens).astype(BF16)
        out_refs[step][...] = chosen.reshape(out_refs[step].shape)


def load_body(*refs, groups, capacity, held):
    el_ref, az_ref, points_hbm, skip_hbm, idx_hbm = refs[:5]
    held_hbm = refs[5 : 5 + held]
    bias_ref, points_ref, skip_ref = refs[5 + held : 8 + held]
    held_refs = refs[8 + held : 8 + 2 * held]
    idx_ref, sems = refs[8 + 2 * held :]
    el, az = el_ref[0], az_ref[0]
    even = 1 - lax.rem(el, 2)
    cols = points_ref.shape[0] // 2
    count = 2 * cols
    first, later = [], []
    turn, half = cols // 4, cols // 2
    spans = []
    for r, at in enumerate((even, 1 - even)):
        spans.append((at, turn, r * half, half))
        spans.append((at, 3 * turn, (2 + r) * half, turn))
        spans.append((at, 0, (2 + r) * half + turn, turn))
    for r, at in enumerate((even, 1 - even)):
        first.append(pltpu.make_async_copy(idx_hbm.at[at], idx_ref.at[r], sems.at[r]))
    for r, (at, low, to, size) in enumerate(spans):
        rows, place = pl.ds(low, size), pl.ds(to, size)
        later.append(
            pltpu.make_async_copy(points_hbm.at[at, rows], points_ref.at[place], sems.at[2 + r])
        )
        later.append(
            pltpu.make_async_copy(skip_hbm.at[at, rows], skip_ref.at[place], sems.at[8 + r])
        )
    for k in range(held):
        later.append(pltpu.make_async_copy(held_hbm[k], held_refs[k], sems.at[14 + k]))
    for c in first + later:
        c.start()
    for c in first:
        c.wait()
    for r in range(2):
        idx_ref[r] = pltpu.roll(idx_ref[r], cols - turn, 1)
    near = idx_ref.shape[1]
    lanes = half
    for piece in range(bias_ref.shape[0] // (groups * capacity)):
        offset = 2 * REACH - sent_offset(az, piece)
        for step in range(groups):
            source = lax.bitwise_xor(el, step)
            low = (offset * groups + source) * capacity
            slot = low + lax.broadcasted_iota(jnp.int32, (capacity, lanes), 0)
            place = (piece * groups + step) * capacity
            for start in range(0, count, lanes):
                row, col = start // half % 2, start // cols * half
                total = jnp.zeros((capacity, lanes), F32)
                for n in range(near):
                    index = idx_ref[row, n : n + 1, col : col + lanes]
                    total = total + jnp.where(slot == index, 1.0, 0.0)
                bias_ref[place : place + capacity, start : start + lanes] = jnp.log2(total)
    for c in later:
        c.wait()


def query_body(points_ref, skip_ref, w_query_ref, w_skip_ref, after_ref, q_ref, side_ref):
    del after_ref
    scale = math.log2(math.e) / math.sqrt(q_ref.shape[0] // HEADS)
    query = dot(points_ref[...], w_query_ref[...]) * scale
    q_ref[...] = query.T.astype(BF16)
    side_ref[...] = dot(skip_ref[...], w_skip_ref[...])


def attend(keys, values_t, q_ref, bias_ref, score_ref, weight_ref, att_ref, first):
    table, width = keys.shape
    count = att_ref.shape[1]
    part = slice(first, first + count)
    head_width = width // HEADS
    lanes = 128
    for head in range(HEADS):
        low, high = head * head_width, (head + 1) * head_width
        score_ref[head] = dot(keys[:, low:high], q_ref[low:high, part]) + bias_ref[:, part]
    for head in range(HEADS):
        for start in range(0, count, lanes):
            x = score_ref[head, :, start : start + lanes]
            top = jnp.max(jnp.max(x.reshape(table // 64, 8, 8, lanes), axis=0), axis=0)
            top = jnp.max(top, axis=0, keepdims=True)
            weight_ref[head, :, start : start + lanes] = jnp.exp2(x - top).astype(BF16)
    ones = jnp.ones((16, table), BF16)
    for head in range(HEADS):
        low, high = head * head_width, (head + 1) * head_width
        lhs = jnp.concatenate([values_t[low:high, :], ones], axis=0)
        mixed = dot(lhs, weight_ref[head])
        scale = 1.0 / mixed[head_width : head_width + 1]
        att_ref[low:high, :] = (mixed[:head_width] * scale).astype(BF16)


def join(points_ref, side_ref, att_ref, w_out_ref, w_hid_ref, w_down_ref, first, sizes):
    c1 = math.sqrt(2.0 / math.pi)
    residuals, pres, out = [], [], []
    starts = [sum(sizes[:k]) for k in range(len(sizes))]
    for start, size in zip(starts, sizes):
        rows = slice(first + start, first + start + size)
        mixed = att_ref[:, start : start + size]
        residuals.append(
            points_ref[rows].astype(F32) + dot(mixed, w_out_ref[...], ((0,), (0,)))
        )
    for start, size, residual in zip(starts, sizes, residuals):
        rows = slice(first + start, first + start + size)
        pres.append(dot(rms(residual).astype(BF16), w_hid_ref[...]) + side_ref[rows])
    for residual, pre in zip(residuals, pres):
        half = 0.5 * pre
        inner = half + half * jnp.tanh(pre * (c1 + (c1 * 0.044715) * (pre * pre)))
        out.append(residual + dot(inner.astype(BF16), w_down_ref[...]))
    return out


def ends_body(az_ref, *refs, pieces):
    (
        w_key_ref,
        w_value_ref,
        q_ref,
        bias_ref,
        points_ref,
        side_ref,
        w_out_ref,
        w_hid_ref,
        w_down_ref,
        joined_ref,
        block_ref,
        inner_edge_ref,
        outer_edge_ref,
        keys_ref,
        values_ref,
        score_ref,
        weight_ref,
        att_ref,
    ) = refs[pieces:]
    received = jnp.concatenate([r[...] for r in refs[:pieces]], axis=0)
    keys = dot(received, w_key_ref[...]).astype(BF16)
    normed_tokens = rms(received.astype(F32)).astype(BF16)
    values_t = dot(w_value_ref[...], normed_tokens, ((0,), (1,))).astype(BF16)
    keys_ref[...], values_ref[...] = keys, values_t
    half = block_ref.shape[1]
    first = 2 * half
    attend(keys, values_t, q_ref, bias_ref, score_ref, weight_ref, att_ref, first)
    joined = join(
        points_ref, side_ref, att_ref, w_out_ref, w_hid_ref, w_down_ref, first, (half, half)
    )
    blocks = [rms(x) for x in joined]
    for at in range(2):
        joined_ref[at] = joined[at]
        block_ref[at] = blocks[at].astype(BF16)
    turn = half // 2
    left = jnp.concatenate([x[turn : turn + 1] for x in blocks], axis=0)
    right = jnp.concatenate([x[turn - 1 : turn] for x in blocks], axis=0)
    odd = lax.rem(az_ref[0], 2) == 1
    inner_edge_ref[...] = jnp.where(odd, left, right).astype(BF16)
    outer_edge_ref[...] = jnp.where(odd, right, left).astype(BF16)


def middle_body(
    keys_ref,
    values_ref,
    joined_ends_ref,
    block_ref,
    q_ref,
    bias_ref,
    points_ref,
    side_ref,
    w_out_ref,
    w_hid_ref,
    w_down_ref,
    joined_ref,
    near_ref,
    far_ref,
    score_ref,
    weight_ref,
    att_ref,
):
    attend(
        keys_ref[...], values_ref[...], q_ref, bias_ref, score_ref, weight_ref, att_ref, 0
    )
    half = block_ref.shape[1]
    turn = half // 2
    joined = join(
        points_ref, side_ref, att_ref, w_out_ref, w_hid_ref, w_down_ref, 0, (half, half)
    )
    for at, (x, ref) in enumerate(zip(joined, (near_ref, far_ref))):
        joined_ref[at, turn : turn + half] = x
        joined_ref[at, turn + half :] = joined_ends_ref[at, :turn]
        joined_ref[at, :turn] = joined_ends_ref[at, turn:]
        ref[turn : turn + half] = rms(x).astype(BF16)
        ref[turn + half : 2 * half] = block_ref[at, :turn]
        ref[:turn] = block_ref[at, turn:]


def pack_body(az_ref, inner_ref, outer_ref, near_in, far_in, near_ref, far_ref):
    del near_in, far_in
    odd = lax.rem(az_ref[0], 2) == 1
    inner, outer = inner_ref[...].astype(F32), outer_ref[...].astype(F32)
    right = jnp.where(odd, outer, inner)
    left = jnp.where(odd, inner, outer)
    cols, width = near_ref.shape[0] - PAD, near_ref.shape[1]
    row = lax.broadcasted_iota(jnp.int32, (PAD, width), 0)
    for at, ref in enumerate((near_ref, far_ref)):
        rows = jnp.where(row == 0, right[at : at + 1], 0.0)
        rows = jnp.where(row == PAD - 1, left[at : at + 1], rows)
        ref[cols:, :] = rows.astype(BF16)


def conv_rows(pairs, cols):
    taps = []
    for dc in range(3):
        total = None
        for x, w_ref, base in pairs:
            part = dot(x, w_ref[base + dc])
            total = part if total is None else total + part
        taps.append(total)
    length = taps[0].shape[0]
    shifted = taps[1] + pltpu.roll(taps[0], 1, 0) + pltpu.roll(taps[2], length - 1, 0)
    return shifted[:cols]


def inside_body(el_ref, near_ref, far_ref, joined_ref, w_ref, out_ref):
    odd = lax.rem(el_ref[0], 2)
    cols = joined_ref.shape[1]
    near, far = near_ref[...], far_ref[...]
    out_ref[0] = joined_ref[0] + conv_rows([(near, w_ref, 3), (far, w_ref, 6 * odd)], cols)
    out_ref[1] = joined_ref[1] + conv_rows([(far, w_ref, 3), (near, w_ref, 6 - 6 * odd)], cols)


def border_body(el_ref, near_ref, far_ref, part_ref, w_ref, out_ref, *, last):
    el = el_ref[0]
    odd = lax.rem(el, 2)
    cols = part_ref.shape[1]
    near = part_ref[0] + conv_rows([(near_ref[...], w_ref, 6 - 6 * odd)], cols)
    out_ref[1 - odd] = near.astype(BF16)
    far = conv_rows([(far_ref[...], w_ref, 6 * odd)], cols)
    ends = jnp.logical_or(el == 0, el == last)
    out_ref[odd] = (part_ref[1] + jnp.where(ends, 0.0, far)).astype(BF16)


def per_device(
    points,
    skip,
    tokens,
    send_slots,
    recv_idx,
    w_query,
    w_key,
    w_value,
    w_out,
    w_hid,
    w_skip,
    w_down,
    w_conv,
):
    rows, cols, width = points.shape
    count = rows * cols
    own_tokens = tokens[0, 0]
    slots = send_slots[0, 0]
    offsets, groups, capacity = slots.shape
    table = offsets * groups * capacity
    el = lax.axis_index("el").astype(jnp.int32).reshape(1)
    az = lax.axis_index("az").astype(jnp.int32).reshape(1)
    shape = jax.ShapeDtypeStruct
    dma = pltpu.SemaphoreType.DMA
    sent = call(
        gather_body,
        [shape((offsets, capacity, width), BF16)] * groups,
        [el, az, own_tokens, slots],
        "gather",
        (2 * table * own_tokens.shape[0] * width, 0),
        [SMEM, SMEM, HBM, HBM],
        [VMEM(own_tokens.shape, BF16), VMEM(slots.shape, jnp.int32), dma((2,))],
    )
    got = {0: sent[0]}
    for s in reversed(range(1, groups)):
        got[s] = swap(sent[s], "el", lambda i, n, s=s: i ^ s)
    pieces = []
    for piece in range(offsets):
        bundle = jnp.concatenate([got[s][piece] for s in range(groups)], axis=0)
        pieces.append(swap(bundle, "az", MATCHES[piece]) if piece else bundle)
    held = [w_query, w_skip, w_key, w_value, w_out, w_hid, w_down, w_conv]
    idx = jnp.swapaxes(recv_idx, 1, 2)
    bias, points_v, skip_v, *held = call(
        functools.partial(load_body, groups=groups, capacity=capacity, held=len(held)),
        [
            shape((table, count), F32),
            shape((count, width), BF16),
            shape((count, width), BF16),
        ]
        + [shape(w.shape, BF16) for w in held],
        [el, az, points, skip, idx] + held,
        "load",
        (table * count * 48, table * count),
        [SMEM, SMEM] + [HBM] * (3 + len(held)),
        [VMEM(idx.shape, jnp.int32), dma((14 + len(held),))],
    )
    query_t, side = call(
        query_body,
        [shape((width, count), BF16), shape((count, w_skip.shape[1]), F32)],
        [points_v, skip_v, held[0], held[1], pieces[0]],
        "query",
        (2 * count * width * 5 * width, 0),
    )
    w_key, w_value, w_out, w_hid, w_down, w_conv = held[2:]
    half = cols // 2
    work = (10 * table * cols * width + 18 * cols * width * width, table * cols * HEADS)
    room = [
        VMEM((HEADS, table, cols), F32),
        VMEM((HEADS, table, cols), BF16),
        VMEM((width, cols), BF16),
    ]
    shared = [query_t, bias, points_v, side, w_out, w_hid, w_down]
    joined_ends, blocks, inner_edge, outer_edge, keys, values = call(
        functools.partial(ends_body, pieces=len(pieces)),
        [
            shape((rows, half, width), F32),
            shape((rows, half, width), BF16),
            shape((2, width), BF16),
            shape((2, width), BF16),
            shape((table, width), BF16),
            shape((width, table), BF16),
        ],
        [az] + pieces + [w_key, w_value] + shared,
        "ends",
        work,
        [SMEM] + [VMEM] * (len(pieces) + 2 + len(shared)),
        room,
    )
    outer_got = swap(outer_edge, "az", next_chip)
    inner_got = swap(inner_edge, "az", same_chip)
    joined, near, far = call(
        middle_body,
        [
            shape((rows, cols, width), F32),
            shape((cols + PAD, width), BF16),
            shape((cols + PAD, width), BF16),
        ],
        [keys, values, joined_ends, blocks] + shared,
        "middle",
        work,
        None,
        room,
    )
    near, far = call(
        pack_body,
        [shape((cols + PAD, width), BF16)] * 2,
        [az, inner_got, outer_got, near, far],
        "pack",
        (4 * PAD * width, 0),
        [SMEM] + [VMEM] * 4,
        (),
        {3: 0, 4: 1},
    )
    far_got = swap(far, "el", inner_pair)
    near_got = swap(near, "el", same_chip)
    (partial,) = call(
        inside_body,
        [shape((rows, cols, width), F32)],
        [el, near, far, joined, w_conv],
        "inside",
        (2 * count * width * width * 6, 0),
        [SMEM] + [VMEM] * 4,
    )
    (out,) = call(
        functools.partial(border_body, last=lax.axis_size("el") - 1),
        [shape((rows, cols, width), BF16)],
        [el, near_got, far_got, partial, w_conv],
        "border",
        (2 * count * width * width * 3, 0),
        [SMEM] + [VMEM] * 4,
    )
    return out


def solution(mesh):
    return jax.shard_map(
        per_device,
        mesh=mesh,
        in_specs=(
            P("el", "az", None),
            P("el", "az", None),
            P("az", "el", None, None),
            P("az", "el", None, None, None),
            P("el", "az", None),
            P(),
            P(),
            P(),
            P(),
            P(),
            P(),
            P(),
            P(),
        ),
        out_specs=P("el", "az", None),
        check_vma=False,
    )
```

```python
import functools
import math

import jax
import jax.numpy as jnp
from jax import lax
from jax.experimental import pallas as pl
from jax.experimental.pallas import tpu as pltpu
from jax.sharding import PartitionSpec as P

HEADS = 8
REACH = 2
PAD = 16
BF16 = jnp.bfloat16
F32 = jnp.float32
VMEM = pltpu.VMEM
SMEM = pltpu.SMEM
HBM = pltpu.HBM


def same_chip(i, n):
    return i ^ 1


def next_chip(i, n):
    return (i + 1 if i % 2 else i - 1) % n


def two_on(i, n):
    return (i + 2 if i // 2 % 2 == 0 else i - 2) % n


def two_back(i, n):
    return (i - 2 if i // 2 % 2 == 0 else i + 2) % n


def inner_pair(i, n):
    return i if i in (0, n - 1) else next_chip(i, n)


def swap(x, axis, partner):
    n = lax.axis_size(axis)
    return lax.ppermute(x, axis, [(i, partner(i, n)) for i in range(n)])


def sent_offset(az, piece):
    odd, odd_chip = lax.rem(az, 2), lax.rem(lax.div(az, 2), 2)
    return (REACH, 4 * odd_chip, 1 + 2 * odd, 4 - 4 * odd_chip, 3 - 2 * odd)[piece]


MATCHES = (None, two_back, next_chip, two_on, same_chip)


def dot(a, b, contract=((1,), (0,))):
    return lax.dot_general(a, b, (contract, ((), ())), preferred_element_type=F32)


def rms(x):
    return x * lax.rsqrt(jnp.mean(x * x, axis=-1, keepdims=True) + 1e-06)


def call(body, outs, ins, name, cost, spaces=None, scratch=(), aliases=None, out_space=VMEM):
    spaces = spaces or [VMEM] * len(ins)
    flops, transcendentals = cost
    moved = sum(x.size * x.dtype.itemsize for x in list(ins) + list(outs))
    ins = [
        pltpu.with_memory_space_constraint(x, HBM) if s == HBM else x
        for x, s in zip(ins, spaces)
    ]
    return pl.pallas_call(
        body,
        out_shape=outs,
        in_specs=[pl.BlockSpec(memory_space=s) for s in spaces],
        out_specs=[pl.BlockSpec(memory_space=out_space) for _ in outs],
        scratch_shapes=list(scratch),
        input_output_aliases=aliases or {},
        compiler_params=pltpu.CompilerParams(vmem_limit_bytes=32 * 1024 * 1024),
        cost_estimate=pl.CostEstimate(
            flops=flops, bytes_accessed=moved, transcendentals=transcendentals
        ),
        name=name,
    )(*ins)


def swap_order(groups):
    return sorted(range(groups), key=lambda s: (s > 0, -s.bit_count(), s))


def gather_body(el_ref, az_ref, tokens_hbm, slots_hbm, *refs):
    out_refs, (tokens_ref, slots_ref, sems) = refs[:-3], refs[-3:]
    copies = [
        pltpu.make_async_copy(tokens_hbm, tokens_ref, sems.at[0]),
        pltpu.make_async_copy(slots_hbm, slots_ref, sems.at[1]),
    ]
    for c in copies:
        c.start()
    offsets, groups, capacity = slots_ref.shape
    rows = tokens_ref.shape[0]
    el, az = el_ref[0], az_ref[0]
    eye = lax.broadcasted_iota(jnp.int32, (capacity, capacity), 0) == lax.broadcasted_iota(
        jnp.int32, (capacity, capacity), 1
    )
    lane = lax.broadcasted_iota(jnp.int32, (capacity, rows), 1).astype(F32)
    for c in copies:
        c.wait()
    tokens = tokens_ref[...]
    for place, step in enumerate(swap_order(groups)):
        target = lax.bitwise_xor(el, step)
        picks = []
        for piece in range(offsets):
            row = slots_ref[sent_offset(az, piece), pl.ds(target, 1), :].astype(F32)
            spread = jnp.broadcast_to(row, (capacity, capacity))
            column = jnp.sum(jnp.where(eye, spread, 0.0), axis=-1, keepdims=True)
            picks.append(jnp.where(column == lane, 1.0, 0.0))
        one_hot = jnp.concatenate(picks, axis=0).astype(BF16)
        chosen = dot(one_hot, tokens).astype(BF16)
        out_refs[place][...] = chosen.reshape(out_refs[place].shape)


def load_body(*refs, groups, capacity, held):
    el_ref, az_ref, points_hbm, skip_hbm, idx_hbm = refs[:5]
    held_hbm = refs[5 : 5 + held]
    bias_ref, points_ref, skip_ref = refs[5 + held : 8 + held]
    held_refs = refs[8 + held : 8 + 2 * held]
    idx_ref, sems = refs[8 + 2 * held :]
    el, az = el_ref[0], az_ref[0]
    even = 1 - lax.rem(el, 2)
    cols = points_ref.shape[0] // 2
    count = 2 * cols
    first, later = [], []
    turn, half = cols // 4, cols // 2
    spans = []
    for r, at in enumerate((even, 1 - even)):
        spans.append((at, turn, r * half, half))
        spans.append((at, 3 * turn, (2 + r) * half, turn))
        spans.append((at, 0, (2 + r) * half + turn, turn))
    for r, at in enumerate((even, 1 - even)):
        first.append(pltpu.make_async_copy(idx_hbm.at[at], idx_ref.at[r], sems.at[r]))
    for r, (at, low, to, size) in enumerate(spans):
        rows, place = pl.ds(low, size), pl.ds(to, size)
        later.append(
            pltpu.make_async_copy(points_hbm.at[at, rows], points_ref.at[place], sems.at[2 + r])
        )
        later.append(
            pltpu.make_async_copy(skip_hbm.at[at, rows], skip_ref.at[place], sems.at[8 + r])
        )
    for k in range(held):
        later.append(pltpu.make_async_copy(held_hbm[k], held_refs[k], sems.at[14 + k]))
    for c in first + later:
        c.start()
    for c in first:
        c.wait()
    for r in range(2):
        idx_ref[r] = pltpu.roll(idx_ref[r], cols - turn, 1)
    near = idx_ref.shape[1]
    lanes = half
    for piece in range(bias_ref.shape[0] // (groups * capacity)):
        offset = 2 * REACH - sent_offset(az, piece)
        for block, step in enumerate(swap_order(groups)):
            source = lax.bitwise_xor(el, step)
            low = (offset * groups + source) * capacity
            slot = low + lax.broadcasted_iota(jnp.int32, (capacity, lanes), 0)
            place = (piece * groups + block) * capacity
            for start in range(0, count, lanes):
                row, col = start // half % 2, start // cols * half
                total = jnp.zeros((capacity, lanes), F32)
                for n in range(near):
                    index = idx_ref[row, n : n + 1, col : col + lanes]
                    total = total + jnp.where(slot == index, 1.0, 0.0)
                bias_ref[place : place + capacity, start : start + lanes] = jnp.log2(total)
    for c in later:
        c.wait()


def query_body(points_ref, skip_ref, w_query_ref, w_skip_ref, after_ref, q_ref, side_ref):
    del after_ref
    scale = math.log2(math.e) / math.sqrt(q_ref.shape[0] // HEADS)
    query = dot(points_ref[...], w_query_ref[...]) * scale
    q_ref[...] = query.T.astype(BF16)
    side_ref[...] = dot(skip_ref[...], w_skip_ref[...])


def attend(keys, values_t, q_ref, bias_ref, score_ref, weight_ref, att_ref, first):
    table, width = keys.shape
    count = att_ref.shape[1]
    part = slice(first, first + count)
    head_width = width // HEADS
    lanes = 128
    for head in range(HEADS):
        low, high = head * head_width, (head + 1) * head_width
        score_ref[head] = dot(keys[:, low:high], q_ref[low:high, part]) + bias_ref[:, part]
    for head in range(HEADS):
        for start in range(0, count, lanes):
            x = score_ref[head, :, start : start + lanes]
            top = jnp.max(jnp.max(x.reshape(table // 64, 8, 8, lanes), axis=0), axis=0)
            top = jnp.max(top, axis=0, keepdims=True)
            weight_ref[head, :, start : start + lanes] = jnp.exp2(x - top).astype(BF16)
    ones = jnp.ones((16, table), BF16)
    for head in range(HEADS):
        low, high = head * head_width, (head + 1) * head_width
        lhs = jnp.concatenate([values_t[low:high, :], ones], axis=0)
        mixed = dot(lhs, weight_ref[head])
        scale = 1.0 / mixed[head_width : head_width + 1]
        att_ref[low:high, :] = (mixed[:head_width] * scale).astype(BF16)


def join(points_ref, side_ref, att_ref, w_out_ref, w_hid_ref, w_down_ref, first, sizes):
    c1 = math.sqrt(2.0 / math.pi)
    residuals, pres, out = [], [], []
    starts = [sum(sizes[:k]) for k in range(len(sizes))]
    for start, size in zip(starts, sizes):
        rows = slice(first + start, first + start + size)
        mixed = att_ref[:, start : start + size]
        residuals.append(
            points_ref[rows].astype(F32) + dot(mixed, w_out_ref[...], ((0,), (0,)))
        )
    for start, size, residual in zip(starts, sizes, residuals):
        rows = slice(first + start, first + start + size)
        pres.append(dot(rms(residual).astype(BF16), w_hid_ref[...]) + side_ref[rows])
    for residual, pre in zip(residuals, pres):
        half = 0.5 * pre
        inner = half + half * jnp.tanh(pre * (c1 + (c1 * 0.044715) * (pre * pre)))
        out.append(residual + dot(inner.astype(BF16), w_down_ref[...]))
    return out


def ends_body(az_ref, *refs, pieces):
    (
        w_key_ref,
        w_value_ref,
        q_ref,
        bias_ref,
        points_ref,
        side_ref,
        w_out_ref,
        w_hid_ref,
        w_down_ref,
        joined_ref,
        block_ref,
        inner_edge_ref,
        outer_edge_ref,
        keys_ref,
        values_ref,
        score_ref,
        weight_ref,
        att_ref,
    ) = refs[pieces:]
    received = jnp.concatenate([r[...] for r in refs[:pieces]], axis=0)
    keys = dot(received, w_key_ref[...]).astype(BF16)
    normed_tokens = rms(received.astype(F32)).astype(BF16)
    values_t = dot(w_value_ref[...], normed_tokens, ((0,), (1,))).astype(BF16)
    keys_ref[...], values_ref[...] = keys, values_t
    half = block_ref.shape[1]
    first = 2 * half
    attend(keys, values_t, q_ref, bias_ref, score_ref, weight_ref, att_ref, first)
    joined = join(
        points_ref, side_ref, att_ref, w_out_ref, w_hid_ref, w_down_ref, first, (half, half)
    )
    blocks = [rms(x) for x in joined]
    for at in range(2):
        joined_ref[at] = joined[at]
        block_ref[at] = blocks[at].astype(BF16)
    turn = half // 2
    left = jnp.concatenate([x[turn : turn + 1] for x in blocks], axis=0)
    right = jnp.concatenate([x[turn - 1 : turn] for x in blocks], axis=0)
    odd = lax.rem(az_ref[0], 2) == 1
    inner_edge_ref[...] = jnp.where(odd, left, right).astype(BF16)
    outer_edge_ref[...] = jnp.where(odd, right, left).astype(BF16)


def middle_body(
    keys_ref,
    values_ref,
    joined_ends_ref,
    block_ref,
    q_ref,
    bias_ref,
    points_ref,
    side_ref,
    w_out_ref,
    w_hid_ref,
    w_down_ref,
    joined_ref,
    near_ref,
    far_ref,
    score_ref,
    weight_ref,
    att_ref,
):
    attend(
        keys_ref[...], values_ref[...], q_ref, bias_ref, score_ref, weight_ref, att_ref, 0
    )
    half = block_ref.shape[1]
    turn = half // 2
    joined = join(
        points_ref, side_ref, att_ref, w_out_ref, w_hid_ref, w_down_ref, 0, (half, half)
    )
    for at, (x, ref) in enumerate(zip(joined, (near_ref, far_ref))):
        joined_ref[at, turn : turn + half] = x
        joined_ref[at, turn + half :] = joined_ends_ref[at, :turn]
        joined_ref[at, :turn] = joined_ends_ref[at, turn:]
        ref[turn : turn + half] = rms(x).astype(BF16)
        ref[turn + half : 2 * half] = block_ref[at, :turn]
        ref[:turn] = block_ref[at, turn:]


def pack_body(az_ref, inner_ref, outer_ref, near_in, far_in, near_ref, far_ref):
    del near_in, far_in
    odd = lax.rem(az_ref[0], 2) == 1
    inner, outer = inner_ref[...].astype(F32), outer_ref[...].astype(F32)
    right = jnp.where(odd, outer, inner)
    left = jnp.where(odd, inner, outer)
    cols, width = near_ref.shape[0] - PAD, near_ref.shape[1]
    row = lax.broadcasted_iota(jnp.int32, (PAD, width), 0)
    for at, ref in enumerate((near_ref, far_ref)):
        rows = jnp.where(row == 0, right[at : at + 1], 0.0)
        rows = jnp.where(row == PAD - 1, left[at : at + 1], rows)
        ref[cols:, :] = rows.astype(BF16)


def conv_rows(pairs, cols):
    taps = []
    for dc in range(3):
        total = None
        for x, w_ref, base in pairs:
            part = dot(x, w_ref[base + dc])
            total = part if total is None else total + part
        taps.append(total)
    length = taps[0].shape[0]
    shifted = taps[1] + pltpu.roll(taps[0], 1, 0) + pltpu.roll(taps[2], length - 1, 0)
    return shifted[:cols]


def inside_body(el_ref, near_ref, far_ref, joined_ref, w_ref, out_ref):
    odd = lax.rem(el_ref[0], 2)
    cols = joined_ref.shape[1]
    near, far = near_ref[...], far_ref[...]
    out_ref[0] = joined_ref[0] + conv_rows([(near, w_ref, 3), (far, w_ref, 6 * odd)], cols)
    out_ref[1] = joined_ref[1] + conv_rows([(far, w_ref, 3), (near, w_ref, 6 - 6 * odd)], cols)


def near_border_body(el_ref, near_ref, part_ref, w_ref, out_ref):
    odd = lax.rem(el_ref[0], 2)
    near = part_ref[0] + conv_rows([(near_ref[...], w_ref, 6 - 6 * odd)], part_ref.shape[1])
    out_ref[...] = near.astype(BF16)


def far_border_body(el_ref, near_ref, far_ref, part_ref, w_ref, out_hbm, row_ref, sems, *, last):
    el = el_ref[0]
    odd = lax.rem(el, 2)
    first = pltpu.make_async_copy(near_ref, out_hbm.at[1 - odd], sems.at[0])
    first.start()
    far = conv_rows([(far_ref[...], w_ref, 6 * odd)], part_ref.shape[1])
    ends = jnp.logical_or(el == 0, el == last)
    row_ref[...] = (part_ref[1] + jnp.where(ends, 0.0, far)).astype(BF16)
    second = pltpu.make_async_copy(row_ref, out_hbm.at[odd], sems.at[1])
    second.start()
    first.wait()
    second.wait()


def per_device(
    points,
    skip,
    tokens,
    send_slots,
    recv_idx,
    w_query,
    w_key,
    w_value,
    w_out,
    w_hid,
    w_skip,
    w_down,
    w_conv,
):
    rows, cols, width = points.shape
    count = rows * cols
    own_tokens = tokens[0, 0]
    slots = send_slots[0, 0]
    offsets, groups, capacity = slots.shape
    table = offsets * groups * capacity
    el = lax.axis_index("el").astype(jnp.int32).reshape(1)
    az = lax.axis_index("az").astype(jnp.int32).reshape(1)
    shape = jax.ShapeDtypeStruct
    dma = pltpu.SemaphoreType.DMA
    sent = call(
        gather_body,
        [shape((offsets, capacity, width), BF16)] * groups,
        [el, az, own_tokens, slots],
        "gather",
        (2 * table * own_tokens.shape[0] * width, 0),
        [SMEM, SMEM, HBM, HBM],
        [VMEM(own_tokens.shape, BF16), VMEM(slots.shape, jnp.int32), dma((2,))],
    )
    got = []
    for block, step in zip(sent, swap_order(groups)):
        got.append(swap(block, "el", lambda i, n, step=step: i ^ step) if step else block)
    pieces = []
    for piece in range(offsets):
        bundle = jnp.concatenate([block[piece] for block in got], axis=0)
        pieces.append(swap(bundle, "az", MATCHES[piece]) if piece else bundle)
    held = [w_query, w_skip, w_key, w_value, w_out, w_hid, w_down, w_conv]
    idx = jnp.swapaxes(recv_idx, 1, 2)
    bias, points_v, skip_v, *held = call(
        functools.partial(load_body, groups=groups, capacity=capacity, held=len(held)),
        [
            shape((table, count), F32),
            shape((count, width), BF16),
            shape((count, width), BF16),
        ]
        + [shape(w.shape, BF16) for w in held],
        [el, az, points, skip, idx] + held,
        "load",
        (table * count * 48, table * count),
        [SMEM, SMEM] + [HBM] * (3 + len(held)),
        [VMEM(idx.shape, jnp.int32), dma((14 + len(held),))],
    )
    query_t, side = call(
        query_body,
        [shape((width, count), BF16), shape((count, w_skip.shape[1]), F32)],
        [points_v, skip_v, held[0], held[1], pieces[0]],
        "query",
        (2 * count * width * 5 * width, 0),
    )
    w_key, w_value, w_out, w_hid, w_down, w_conv = held[2:]
    half = cols // 2
    work = (10 * table * cols * width + 18 * cols * width * width, table * cols * HEADS)
    room = [
        VMEM((HEADS, table, cols), F32),
        VMEM((HEADS, table, cols), BF16),
        VMEM((width, cols), BF16),
    ]
    shared = [query_t, bias, points_v, side, w_out, w_hid, w_down]
    joined_ends, blocks, inner_edge, outer_edge, keys, values = call(
        functools.partial(ends_body, pieces=len(pieces)),
        [
            shape((rows, half, width), F32),
            shape((rows, half, width), BF16),
            shape((2, width), BF16),
            shape((2, width), BF16),
            shape((table, width), BF16),
            shape((width, table), BF16),
        ],
        [az] + pieces + [w_key, w_value] + shared,
        "ends",
        work,
        [SMEM] + [VMEM] * (len(pieces) + 2 + len(shared)),
        room,
    )
    outer_got = swap(outer_edge, "az", next_chip)
    inner_got = swap(inner_edge, "az", same_chip)
    joined, near, far = call(
        middle_body,
        [
            shape((rows, cols, width), F32),
            shape((cols + PAD, width), BF16),
            shape((cols + PAD, width), BF16),
        ],
        [keys, values, joined_ends, blocks] + shared,
        "middle",
        work,
        None,
        room,
    )
    near, far = call(
        pack_body,
        [shape((cols + PAD, width), BF16)] * 2,
        [az, inner_got, outer_got, near, far],
        "pack",
        (4 * PAD * width, 0),
        [SMEM] + [VMEM] * 4,
        (),
        {3: 0, 4: 1},
    )
    far_got = swap(far, "el", inner_pair)
    near_got = swap(near, "el", same_chip)
    (partial,) = call(
        inside_body,
        [shape((rows, cols, width), F32)],
        [el, near, far, joined, w_conv],
        "inside",
        (2 * count * width * width * 6, 0),
        [SMEM] + [VMEM] * 4,
    )
    (near_row,) = call(
        near_border_body,
        [shape((cols, width), BF16)],
        [el, near_got, partial, w_conv],
        "near_border",
        (cols * width * width * 6, 0),
        [SMEM] + [VMEM] * 3,
    )
    (out,) = call(
        functools.partial(far_border_body, last=lax.axis_size("el") - 1),
        [shape((rows, cols, width), BF16)],
        [el, near_row, far_got, partial, w_conv],
        "far_border",
        (cols * width * width * 6, 0),
        [SMEM] + [VMEM] * 4,
        [VMEM((cols, width), BF16), dma((2,))],
        out_space=HBM,
    )
    return out


def solution(mesh):
    return jax.shard_map(
        per_device,
        mesh=mesh,
        in_specs=(
            P("el", "az", None),
            P("el", "az", None),
            P("az", "el", None, None),
            P("az", "el", None, None, None),
            P("el", "az", None),
            P(),
            P(),
            P(),
            P(),
            P(),
            P(),
            P(),
            P(),
        ),
        out_specs=P("el", "az", None),
        check_vma=False,
    )
```

```python
import functools
import math

import jax
import jax.numpy as jnp
from jax import lax
from jax.experimental import pallas as pl
from jax.experimental.pallas import tpu as pltpu
from jax.sharding import PartitionSpec as P

HEADS = 8
REACH = 2
PAD = 16
BF16 = jnp.bfloat16
F32 = jnp.float32
VMEM = pltpu.VMEM
SMEM = pltpu.SMEM
HBM = pltpu.HBM


def same_chip(i, n):
    return i ^ 1


def next_chip(i, n):
    return (i + 1 if i % 2 else i - 1) % n


def two_on(i, n):
    return (i + 2 if i // 2 % 2 == 0 else i - 2) % n


def two_back(i, n):
    return (i - 2 if i // 2 % 2 == 0 else i + 2) % n


def inner_pair(i, n):
    return i if i in (0, n - 1) else next_chip(i, n)


def swap(x, axis, partner):
    n = lax.axis_size(axis)
    return lax.ppermute(x, axis, [(i, partner(i, n)) for i in range(n)])


def sent_offset(az, piece):
    odd, odd_chip = lax.rem(az, 2), lax.rem(lax.div(az, 2), 2)
    return (REACH, 4 * odd_chip, 1 + 2 * odd, 4 - 4 * odd_chip, 3 - 2 * odd)[piece]


MATCHES = (None, two_back, next_chip, two_on, same_chip)


def dot(a, b, contract=((1,), (0,))):
    return lax.dot_general(a, b, (contract, ((), ())), preferred_element_type=F32)


def rms(x):
    return x * lax.rsqrt(jnp.mean(x * x, axis=-1, keepdims=True) + 1e-06)


def call(body, outs, ins, name, cost, spaces=None, scratch=(), aliases=None, out_space=VMEM):
    spaces = spaces or [VMEM] * len(ins)
    flops, transcendentals = cost
    moved = sum(x.size * x.dtype.itemsize for x in list(ins) + list(outs))
    ins = [
        pltpu.with_memory_space_constraint(x, HBM) if s == HBM else x
        for x, s in zip(ins, spaces)
    ]
    return pl.pallas_call(
        body,
        out_shape=outs,
        in_specs=[pl.BlockSpec(memory_space=s) for s in spaces],
        out_specs=[pl.BlockSpec(memory_space=out_space) for _ in outs],
        scratch_shapes=list(scratch),
        input_output_aliases=aliases or {},
        compiler_params=pltpu.CompilerParams(vmem_limit_bytes=32 * 1024 * 1024),
        cost_estimate=pl.CostEstimate(
            flops=flops, bytes_accessed=moved, transcendentals=transcendentals
        ),
        name=name,
    )(*ins)


def swap_order(groups):
    return sorted(range(groups), key=lambda s: (s > 0, -s.bit_count(), s))


def gather_body(el_ref, az_ref, tokens_hbm, slots_hbm, *refs):
    out_refs, (tokens_ref, slots_ref, sems) = refs[:-3], refs[-3:]
    copies = [
        pltpu.make_async_copy(tokens_hbm, tokens_ref, sems.at[0]),
        pltpu.make_async_copy(slots_hbm, slots_ref, sems.at[1]),
    ]
    for c in copies:
        c.start()
    offsets, groups, capacity = slots_ref.shape
    rows = tokens_ref.shape[0]
    el, az = el_ref[0], az_ref[0]
    eye = lax.broadcasted_iota(jnp.int32, (capacity, capacity), 0) == lax.broadcasted_iota(
        jnp.int32, (capacity, capacity), 1
    )
    lane = lax.broadcasted_iota(jnp.int32, (capacity, rows), 1).astype(F32)
    for c in copies:
        c.wait()
    tokens = tokens_ref[...]
    for place, step in enumerate(swap_order(groups)):
        target = lax.bitwise_xor(el, step)
        picks = []
        for piece in range(offsets):
            row = slots_ref[sent_offset(az, piece), pl.ds(target, 1), :].astype(F32)
            spread = jnp.broadcast_to(row, (capacity, capacity))
            column = jnp.sum(jnp.where(eye, spread, 0.0), axis=-1, keepdims=True)
            picks.append(jnp.where(column == lane, 1.0, 0.0))
        one_hot = jnp.concatenate(picks, axis=0).astype(BF16)
        chosen = dot(one_hot, tokens).astype(BF16)
        out_refs[place][...] = chosen.reshape(out_refs[place].shape)


def load_body(*refs, groups, capacity, held):
    el_ref, az_ref, points_hbm, skip_hbm, idx_hbm = refs[:5]
    held_hbm = refs[5 : 5 + held]
    bias_ref, points_ref, skip_ref = refs[5 + held : 8 + held]
    held_refs = refs[8 + held : 8 + 2 * held]
    idx_ref, sems = refs[8 + 2 * held :]
    el, az = el_ref[0], az_ref[0]
    even = 1 - lax.rem(el, 2)
    cols = points_ref.shape[0] // 2
    count = 2 * cols
    first, later = [], []
    turn, half = cols // 4, cols // 2
    spans = []
    for r, at in enumerate((even, 1 - even)):
        spans.append((at, turn, r * half, half))
        spans.append((at, 3 * turn, (2 + r) * half, turn))
        spans.append((at, 0, (2 + r) * half + turn, turn))
    for r, at in enumerate((even, 1 - even)):
        first.append(pltpu.make_async_copy(idx_hbm.at[at], idx_ref.at[r], sems.at[r]))
    for r, (at, low, to, size) in enumerate(spans):
        rows, place = pl.ds(low, size), pl.ds(to, size)
        later.append(
            pltpu.make_async_copy(points_hbm.at[at, rows], points_ref.at[place], sems.at[2 + r])
        )
        later.append(
            pltpu.make_async_copy(skip_hbm.at[at, rows], skip_ref.at[place], sems.at[8 + r])
        )
    for k in range(held):
        later.append(pltpu.make_async_copy(held_hbm[k], held_refs[k], sems.at[14 + k]))
    for c in first + later:
        c.start()
    for c in first:
        c.wait()
    for r in range(2):
        idx_ref[r] = pltpu.roll(idx_ref[r], cols - turn, 1)
    near = idx_ref.shape[1]
    lanes = half
    for piece in range(bias_ref.shape[0] // (groups * capacity)):
        offset = 2 * REACH - sent_offset(az, piece)
        for block, step in enumerate(swap_order(groups)):
            source = lax.bitwise_xor(el, step)
            low = (offset * groups + source) * capacity
            slot = low + lax.broadcasted_iota(jnp.int32, (capacity, lanes), 0)
            place = (piece * groups + block) * capacity
            for start in range(0, count, lanes):
                row, col = start // half % 2, start // cols * half
                total = jnp.zeros((capacity, lanes), F32)
                for n in range(near):
                    index = idx_ref[row, n : n + 1, col : col + lanes]
                    total = total + jnp.where(slot == index, 1.0, 0.0)
                bias_ref[place : place + capacity, start : start + lanes] = jnp.log2(total)
    for c in later:
        c.wait()


def query_body(points_ref, skip_ref, w_query_ref, w_skip_ref, after_ref, q_ref, side_ref):
    del after_ref
    scale = math.log2(math.e) / math.sqrt(q_ref.shape[0] // HEADS)
    query = dot(points_ref[...], w_query_ref[...]) * scale
    q_ref[...] = query.T.astype(BF16)
    side_ref[...] = dot(skip_ref[...], w_skip_ref[...])


def attend(keys, values_t, q_ref, bias_ref, score_ref, weight_ref, att_ref, first):
    table, width = keys.shape
    count = att_ref.shape[1]
    part = slice(first, first + count)
    head_width = width // HEADS
    lanes = 128
    for head in range(HEADS):
        low, high = head * head_width, (head + 1) * head_width
        score_ref[head] = dot(keys[:, low:high], q_ref[low:high, part]) + bias_ref[:, part]
    for head in range(HEADS):
        for start in range(0, count, lanes):
            x = score_ref[head, :, start : start + lanes]
            top = jnp.max(jnp.max(x.reshape(table // 64, 8, 8, lanes), axis=0), axis=0)
            top = jnp.max(top, axis=0, keepdims=True)
            weight_ref[head, :, start : start + lanes] = jnp.exp2(x - top).astype(BF16)
    ones = jnp.ones((16, table), BF16)
    for head in range(HEADS):
        low, high = head * head_width, (head + 1) * head_width
        lhs = jnp.concatenate([values_t[low:high, :], ones], axis=0)
        mixed = dot(lhs, weight_ref[head])
        scale = 1.0 / mixed[head_width : head_width + 1]
        att_ref[low:high, :] = (mixed[:head_width] * scale).astype(BF16)


def join(points_ref, side_ref, att_ref, w_out_ref, w_hid_ref, w_down_ref, first, sizes):
    c1 = math.sqrt(2.0 / math.pi)
    residuals, pres, out = [], [], []
    starts = [sum(sizes[:k]) for k in range(len(sizes))]
    for start, size in zip(starts, sizes):
        rows = slice(first + start, first + start + size)
        mixed = att_ref[:, start : start + size]
        residuals.append(
            points_ref[rows].astype(F32) + dot(mixed, w_out_ref[...], ((0,), (0,)))
        )
    for start, size, residual in zip(starts, sizes, residuals):
        rows = slice(first + start, first + start + size)
        pres.append(dot(rms(residual).astype(BF16), w_hid_ref[...]) + side_ref[rows])
    for residual, pre in zip(residuals, pres):
        half = 0.5 * pre
        inner = half + half * jnp.tanh(pre * (c1 + (c1 * 0.044715) * (pre * pre)))
        out.append(residual + dot(inner.astype(BF16), w_down_ref[...]))
    return out


def ends_body(az_ref, *refs, pieces):
    (
        w_key_ref,
        w_value_ref,
        q_ref,
        bias_ref,
        points_ref,
        side_ref,
        w_out_ref,
        w_hid_ref,
        w_down_ref,
        joined_ref,
        block_ref,
        inner_edge_ref,
        outer_edge_ref,
        keys_ref,
        values_ref,
        score_ref,
        weight_ref,
        att_ref,
    ) = refs[pieces:]
    received = jnp.concatenate([r[...] for r in refs[:pieces]], axis=0)
    keys = dot(received, w_key_ref[...]).astype(BF16)
    normed_tokens = rms(received.astype(F32)).astype(BF16)
    values_t = dot(w_value_ref[...], normed_tokens, ((0,), (1,))).astype(BF16)
    keys_ref[...], values_ref[...] = keys, values_t
    half = block_ref.shape[1]
    first = 2 * half
    attend(keys, values_t, q_ref, bias_ref, score_ref, weight_ref, att_ref, first)
    joined = join(
        points_ref, side_ref, att_ref, w_out_ref, w_hid_ref, w_down_ref, first, (half, half)
    )
    blocks = [rms(x) for x in joined]
    for at in range(2):
        joined_ref[at] = joined[at]
        block_ref[at] = blocks[at].astype(BF16)
    turn = half // 2
    left = jnp.concatenate([x[turn : turn + 1] for x in blocks], axis=0)
    right = jnp.concatenate([x[turn - 1 : turn] for x in blocks], axis=0)
    odd = lax.rem(az_ref[0], 2) == 1
    inner_edge_ref[...] = jnp.where(odd, left, right).astype(BF16)
    outer_edge_ref[...] = jnp.where(odd, right, left).astype(BF16)


def middle_body(
    keys_ref,
    values_ref,
    joined_ends_ref,
    block_ref,
    q_ref,
    bias_ref,
    points_ref,
    side_ref,
    w_out_ref,
    w_hid_ref,
    w_down_ref,
    joined_ref,
    near_ref,
    far_ref,
    score_ref,
    weight_ref,
    att_ref,
):
    attend(
        keys_ref[...], values_ref[...], q_ref, bias_ref, score_ref, weight_ref, att_ref, 0
    )
    half = block_ref.shape[1]
    turn = half // 2
    joined = join(
        points_ref, side_ref, att_ref, w_out_ref, w_hid_ref, w_down_ref, 0, (half, half)
    )
    for at, (x, ref) in enumerate(zip(joined, (near_ref, far_ref))):
        joined_ref[at, turn : turn + half] = x
        joined_ref[at, turn + half :] = joined_ends_ref[at, :turn]
        joined_ref[at, :turn] = joined_ends_ref[at, turn:]
        ref[turn : turn + half] = rms(x).astype(BF16)
        ref[turn + half : 2 * half] = block_ref[at, :turn]
        ref[:turn] = block_ref[at, turn:]


def pack_body(az_ref, inner_ref, outer_ref, near_in, far_in, near_ref, far_ref):
    del near_in, far_in
    odd = lax.rem(az_ref[0], 2) == 1
    inner, outer = inner_ref[...].astype(F32), outer_ref[...].astype(F32)
    right = jnp.where(odd, outer, inner)
    left = jnp.where(odd, inner, outer)
    cols, width = near_ref.shape[0] - PAD, near_ref.shape[1]
    row = lax.broadcasted_iota(jnp.int32, (PAD, width), 0)
    for at, ref in enumerate((near_ref, far_ref)):
        rows = jnp.where(row == 0, right[at : at + 1], 0.0)
        rows = jnp.where(row == PAD - 1, left[at : at + 1], rows)
        ref[cols:, :] = rows.astype(BF16)


def conv_rows(pairs, cols):
    taps = []
    for dc in range(3):
        total = None
        for x, w_ref, base in pairs:
            part = dot(x, w_ref[base + dc])
            total = part if total is None else total + part
        taps.append(total)
    length = taps[0].shape[0]
    shifted = taps[1] + pltpu.roll(taps[0], 1, 0) + pltpu.roll(taps[2], length - 1, 0)
    return shifted[:cols]


def inside_body(el_ref, near_ref, far_ref, joined_ref, w_ref, out_ref):
    odd = lax.rem(el_ref[0], 2)
    cols = joined_ref.shape[1]
    near, far = near_ref[...], far_ref[...]
    out_ref[0] = joined_ref[0] + conv_rows([(near, w_ref, 3), (far, w_ref, 6 * odd)], cols)
    out_ref[1] = joined_ref[1] + conv_rows([(far, w_ref, 3), (near, w_ref, 6 - 6 * odd)], cols)


def far_border_body(el_ref, far_ref, part_ref, w_ref, out_ref, *, last):
    el = el_ref[0]
    far = conv_rows([(far_ref[...], w_ref, 6 * lax.rem(el, 2))], part_ref.shape[1])
    ends = jnp.logical_or(el == 0, el == last)
    out_ref[...] = (part_ref[1] + jnp.where(ends, 0.0, far)).astype(BF16)


def near_border_body(el_ref, far_row_ref, near_ref, part_ref, w_ref, out_hbm, row_ref, sems):
    odd = lax.rem(el_ref[0], 2)
    first = pltpu.make_async_copy(far_row_ref, out_hbm.at[odd], sems.at[0])
    first.start()
    near = conv_rows([(near_ref[...], w_ref, 6 - 6 * odd)], part_ref.shape[1])
    row_ref[...] = (part_ref[0] + near).astype(BF16)
    second = pltpu.make_async_copy(row_ref, out_hbm.at[1 - odd], sems.at[1])
    second.start()
    first.wait()
    second.wait()


def per_device(
    points,
    skip,
    tokens,
    send_slots,
    recv_idx,
    w_query,
    w_key,
    w_value,
    w_out,
    w_hid,
    w_skip,
    w_down,
    w_conv,
):
    rows, cols, width = points.shape
    count = rows * cols
    own_tokens = tokens[0, 0]
    slots = send_slots[0, 0]
    offsets, groups, capacity = slots.shape
    table = offsets * groups * capacity
    el = lax.axis_index("el").astype(jnp.int32).reshape(1)
    az = lax.axis_index("az").astype(jnp.int32).reshape(1)
    shape = jax.ShapeDtypeStruct
    dma = pltpu.SemaphoreType.DMA
    sent = call(
        gather_body,
        [shape((offsets, capacity, width), BF16)] * groups,
        [el, az, own_tokens, slots],
        "gather",
        (2 * table * own_tokens.shape[0] * width, 0),
        [SMEM, SMEM, HBM, HBM],
        [VMEM(own_tokens.shape, BF16), VMEM(slots.shape, jnp.int32), dma((2,))],
    )
    got = []
    for block, step in zip(sent, swap_order(groups)):
        got.append(swap(block, "el", lambda i, n, step=step: i ^ step) if step else block)
    pieces = []
    for piece in range(offsets):
        bundle = jnp.concatenate([block[piece] for block in got], axis=0)
        pieces.append(swap(bundle, "az", MATCHES[piece]) if piece else bundle)
    held = [w_query, w_skip, w_key, w_value, w_out, w_hid, w_down, w_conv]
    idx = jnp.swapaxes(recv_idx, 1, 2)
    bias, points_v, skip_v, *held = call(
        functools.partial(load_body, groups=groups, capacity=capacity, held=len(held)),
        [
            shape((table, count), F32),
            shape((count, width), BF16),
            shape((count, width), BF16),
        ]
        + [shape(w.shape, BF16) for w in held],
        [el, az, points, skip, idx] + held,
        "load",
        (table * count * 48, table * count),
        [SMEM, SMEM] + [HBM] * (3 + len(held)),
        [VMEM(idx.shape, jnp.int32), dma((14 + len(held),))],
    )
    query_t, side = call(
        query_body,
        [shape((width, count), BF16), shape((count, w_skip.shape[1]), F32)],
        [points_v, skip_v, held[0], held[1], pieces[0]],
        "query",
        (2 * count * width * 5 * width, 0),
    )
    w_key, w_value, w_out, w_hid, w_down, w_conv = held[2:]
    half = cols // 2
    work = (10 * table * cols * width + 18 * cols * width * width, table * cols * HEADS)
    room = [
        VMEM((HEADS, table, cols), F32),
        VMEM((HEADS, table, cols), BF16),
        VMEM((width, cols), BF16),
    ]
    shared = [query_t, bias, points_v, side, w_out, w_hid, w_down]
    joined_ends, blocks, inner_edge, outer_edge, keys, values = call(
        functools.partial(ends_body, pieces=len(pieces)),
        [
            shape((rows, half, width), F32),
            shape((rows, half, width), BF16),
            shape((2, width), BF16),
            shape((2, width), BF16),
            shape((table, width), BF16),
            shape((width, table), BF16),
        ],
        [az] + pieces + [w_key, w_value] + shared,
        "ends",
        work,
        [SMEM] + [VMEM] * (len(pieces) + 2 + len(shared)),
        room,
    )
    outer_got = swap(outer_edge, "az", next_chip)
    inner_got = swap(inner_edge, "az", same_chip)
    joined, near, far = call(
        middle_body,
        [
            shape((rows, cols, width), F32),
            shape((cols + PAD, width), BF16),
            shape((cols + PAD, width), BF16),
        ],
        [keys, values, joined_ends, blocks] + shared,
        "middle",
        work,
        None,
        room,
    )
    near, far = call(
        pack_body,
        [shape((cols + PAD, width), BF16)] * 2,
        [az, inner_got, outer_got, near, far],
        "pack",
        (4 * PAD * width, 0),
        [SMEM] + [VMEM] * 4,
        (),
        {3: 0, 4: 1},
    )
    far_got = swap(far, "el", inner_pair)
    near_got = swap(near, "el", same_chip)
    (partial,) = call(
        inside_body,
        [shape((rows, cols, width), F32)],
        [el, near, far, joined, w_conv],
        "inside",
        (2 * count * width * width * 6, 0),
        [SMEM] + [VMEM] * 4,
    )
    (far_row,) = call(
        functools.partial(far_border_body, last=lax.axis_size("el") - 1),
        [shape((cols, width), BF16)],
        [el, far_got, partial, w_conv],
        "far_border",
        (cols * width * width * 6, 0),
        [SMEM] + [VMEM] * 3,
    )
    (out,) = call(
        near_border_body,
        [shape((rows, cols, width), BF16)],
        [el, far_row, near_got, partial, w_conv],
        "near_border",
        (cols * width * width * 6, 0),
        [SMEM] + [VMEM] * 4,
        [VMEM((cols, width), BF16), dma((2,))],
        out_space=HBM,
    )
    return out


def solution(mesh):
    return jax.shard_map(
        per_device,
        mesh=mesh,
        in_specs=(
            P("el", "az", None),
            P("el", "az", None),
            P("az", "el", None, None),
            P("az", "el", None, None, None),
            P("el", "az", None),
            P(),
            P(),
            P(),
            P(),
            P(),
            P(),
            P(),
            P(),
        ),
        out_specs=P("el", "az", None),
        check_vma=False,
    )
```

```python
import functools
import math

import jax
import jax.numpy as jnp
from jax import lax
from jax.experimental import pallas as pl
from jax.experimental.pallas import tpu as pltpu
from jax.sharding import PartitionSpec as P

HEADS = 8
REACH = 2
PAD = 16
BF16 = jnp.bfloat16
F32 = jnp.float32
VMEM = pltpu.VMEM
SMEM = pltpu.SMEM
HBM = pltpu.HBM


def same_chip(i, n):
    return i ^ 1


def next_chip(i, n):
    return (i + 1 if i % 2 else i - 1) % n


def two_on(i, n):
    return (i + 2 if i // 2 % 2 == 0 else i - 2) % n


def two_back(i, n):
    return (i - 2 if i // 2 % 2 == 0 else i + 2) % n


def swap(x, axis, partner):
    n = lax.axis_size(axis)
    return lax.ppermute(x, axis, [(i, partner(i, n)) for i in range(n)])


def sent_offset(az, piece):
    odd, odd_chip = lax.rem(az, 2), lax.rem(lax.div(az, 2), 2)
    return (REACH, 4 * odd_chip, 1 + 2 * odd, 4 - 4 * odd_chip, 3 - 2 * odd)[piece]


MATCHES = (None, two_back, next_chip, two_on, same_chip)


def dot(a, b, contract=((1,), (0,))):
    return lax.dot_general(a, b, (contract, ((), ())), preferred_element_type=F32)


def rms(x):
    return x * lax.rsqrt(jnp.mean(x * x, axis=-1, keepdims=True) + 1e-06)


def call(body, outs, ins, name, cost, spaces=None, scratch=(), aliases=None, out_space=VMEM):
    spaces = spaces or [VMEM] * len(ins)
    flops, transcendentals = cost
    moved = sum(x.size * x.dtype.itemsize for x in list(ins) + list(outs))
    ins = [
        pltpu.with_memory_space_constraint(x, HBM) if s == HBM else x
        for x, s in zip(ins, spaces)
    ]
    return pl.pallas_call(
        body,
        out_shape=outs,
        in_specs=[pl.BlockSpec(memory_space=s) for s in spaces],
        out_specs=[pl.BlockSpec(memory_space=out_space) for _ in outs],
        scratch_shapes=list(scratch),
        input_output_aliases=aliases or {},
        compiler_params=pltpu.CompilerParams(vmem_limit_bytes=32 * 1024 * 1024),
        cost_estimate=pl.CostEstimate(
            flops=flops, bytes_accessed=moved, transcendentals=transcendentals
        ),
        name=name,
    )(*ins)


def swap_order(groups):
    return sorted(range(groups), key=lambda s: (s > 0, -s.bit_count(), s))


def gather_body(el_ref, az_ref, tokens_hbm, slots_hbm, *refs):
    out_refs, (tokens_ref, slots_ref, sems) = refs[:-3], refs[-3:]
    copies = [
        pltpu.make_async_copy(tokens_hbm, tokens_ref, sems.at[0]),
        pltpu.make_async_copy(slots_hbm, slots_ref, sems.at[1]),
    ]
    for c in copies:
        c.start()
    offsets, groups, capacity = slots_ref.shape
    rows = tokens_ref.shape[0]
    el, az = el_ref[0], az_ref[0]
    eye = lax.broadcasted_iota(jnp.int32, (capacity, capacity), 0) == lax.broadcasted_iota(
        jnp.int32, (capacity, capacity), 1
    )
    lane = lax.broadcasted_iota(jnp.int32, (capacity, rows), 1).astype(F32)
    for c in copies:
        c.wait()
    tokens = tokens_ref[...]
    for place, step in enumerate(swap_order(groups)):
        target = lax.bitwise_xor(el, step)
        picks = []
        for piece in range(offsets):
            row = slots_ref[sent_offset(az, piece), pl.ds(target, 1), :].astype(F32)
            spread = jnp.broadcast_to(row, (capacity, capacity))
            column = jnp.sum(jnp.where(eye, spread, 0.0), axis=-1, keepdims=True)
            picks.append(jnp.where(column == lane, 1.0, 0.0))
        one_hot = jnp.concatenate(picks, axis=0).astype(BF16)
        chosen = dot(one_hot, tokens).astype(BF16)
        out_refs[place][...] = chosen.reshape(out_refs[place].shape)


def load_body(*refs, groups, capacity, held):
    el_ref, az_ref, points_hbm, skip_hbm, idx_hbm = refs[:5]
    held_hbm = refs[5 : 5 + held]
    bias_ref, points_ref, skip_ref = refs[5 + held : 8 + held]
    held_refs = refs[8 + held : 8 + 2 * held]
    idx_ref, sems = refs[8 + 2 * held :]
    el, az = el_ref[0], az_ref[0]
    even = 1 - lax.rem(el, 2)
    cols = points_ref.shape[0] // 2
    count = 2 * cols
    first, later = [], []
    turn, half = cols // 4, cols // 2
    spans = []
    for r, at in enumerate((even, 1 - even)):
        spans.append((at, turn, r * half, half))
        spans.append((at, 3 * turn, (2 + r) * half, turn))
        spans.append((at, 0, (2 + r) * half + turn, turn))
    for r, at in enumerate((even, 1 - even)):
        first.append(pltpu.make_async_copy(idx_hbm.at[at], idx_ref.at[r], sems.at[r]))
    for r, (at, low, to, size) in enumerate(spans):
        rows, place = pl.ds(low, size), pl.ds(to, size)
        later.append(
            pltpu.make_async_copy(points_hbm.at[at, rows], points_ref.at[place], sems.at[2 + r])
        )
        later.append(
            pltpu.make_async_copy(skip_hbm.at[at, rows], skip_ref.at[place], sems.at[8 + r])
        )
    for k in range(held):
        later.append(pltpu.make_async_copy(held_hbm[k], held_refs[k], sems.at[14 + k]))
    for c in first + later:
        c.start()
    for c in first:
        c.wait()
    for r in range(2):
        idx_ref[r] = pltpu.roll(idx_ref[r], cols - turn, 1)
    near = idx_ref.shape[1]
    lanes = half
    for piece in range(bias_ref.shape[0] // (groups * capacity)):
        offset = 2 * REACH - sent_offset(az, piece)
        for block, step in enumerate(swap_order(groups)):
            source = lax.bitwise_xor(el, step)
            low = (offset * groups + source) * capacity
            slot = low + lax.broadcasted_iota(jnp.int32, (capacity, lanes), 0)
            place = (piece * groups + block) * capacity
            for start in range(0, count, lanes):
                row, col = start // half % 2, start // cols * half
                total = jnp.zeros((capacity, lanes), F32)
                for n in range(near):
                    index = idx_ref[row, n : n + 1, col : col + lanes]
                    total = total + jnp.where(slot == index, 1.0, 0.0)
                bias_ref[place : place + capacity, start : start + lanes] = jnp.log2(total)
    for c in later:
        c.wait()


def query_body(points_ref, skip_ref, w_query_ref, w_skip_ref, after_ref, q_ref, side_ref):
    del after_ref
    scale = math.log2(math.e) / math.sqrt(q_ref.shape[0] // HEADS)
    query = dot(points_ref[...], w_query_ref[...]) * scale
    q_ref[...] = query.T.astype(BF16)
    side_ref[...] = dot(skip_ref[...], w_skip_ref[...])


def attend(keys, values_t, q_ref, bias_ref, score_ref, weight_ref, att_ref, first):
    table, width = keys.shape
    count = att_ref.shape[1]
    part = slice(first, first + count)
    head_width = width // HEADS
    lanes = 128
    for head in range(HEADS):
        low, high = head * head_width, (head + 1) * head_width
        score_ref[head] = dot(keys[:, low:high], q_ref[low:high, part]) + bias_ref[:, part]
    for head in range(HEADS):
        for start in range(0, count, lanes):
            x = score_ref[head, :, start : start + lanes]
            top = jnp.max(jnp.max(x.reshape(table // 64, 8, 8, lanes), axis=0), axis=0)
            top = jnp.max(top, axis=0, keepdims=True)
            weight_ref[head, :, start : start + lanes] = jnp.exp2(x - top).astype(BF16)
    ones = jnp.ones((16, table), BF16)
    for head in range(HEADS):
        low, high = head * head_width, (head + 1) * head_width
        lhs = jnp.concatenate([values_t[low:high, :], ones], axis=0)
        mixed = dot(lhs, weight_ref[head])
        scale = 1.0 / mixed[head_width : head_width + 1]
        att_ref[low:high, :] = (mixed[:head_width] * scale).astype(BF16)


def join(points_ref, side_ref, att_ref, w_out_ref, w_hid_ref, w_down_ref, first, sizes):
    c1 = math.sqrt(2.0 / math.pi)
    residuals, pres, out = [], [], []
    starts = [sum(sizes[:k]) for k in range(len(sizes))]
    for start, size in zip(starts, sizes):
        rows = slice(first + start, first + start + size)
        mixed = att_ref[:, start : start + size]
        residuals.append(
            points_ref[rows].astype(F32) + dot(mixed, w_out_ref[...], ((0,), (0,)))
        )
    for start, size, residual in zip(starts, sizes, residuals):
        rows = slice(first + start, first + start + size)
        pres.append(dot(rms(residual).astype(BF16), w_hid_ref[...]) + side_ref[rows])
    for residual, pre in zip(residuals, pres):
        half = 0.5 * pre
        inner = half + half * jnp.tanh(pre * (c1 + (c1 * 0.044715) * (pre * pre)))
        out.append(residual + dot(inner.astype(BF16), w_down_ref[...]))
    return out


def ends_body(az_ref, *refs, pieces):
    (
        w_key_ref,
        w_value_ref,
        q_ref,
        bias_ref,
        points_ref,
        side_ref,
        w_out_ref,
        w_hid_ref,
        w_down_ref,
        joined_ref,
        block_ref,
        inner_edge_ref,
        outer_edge_ref,
        keys_ref,
        values_ref,
        score_ref,
        weight_ref,
        att_ref,
    ) = refs[pieces:]
    received = jnp.concatenate([r[...] for r in refs[:pieces]], axis=0)
    keys = dot(received, w_key_ref[...]).astype(BF16)
    normed_tokens = rms(received.astype(F32)).astype(BF16)
    values_t = dot(w_value_ref[...], normed_tokens, ((0,), (1,))).astype(BF16)
    keys_ref[...], values_ref[...] = keys, values_t
    half = block_ref.shape[1]
    first = 2 * half
    attend(keys, values_t, q_ref, bias_ref, score_ref, weight_ref, att_ref, first)
    joined = join(
        points_ref, side_ref, att_ref, w_out_ref, w_hid_ref, w_down_ref, first, (half, half)
    )
    blocks = [rms(x) for x in joined]
    for at in range(2):
        joined_ref[at] = joined[at]
        block_ref[at] = blocks[at].astype(BF16)
    turn = half // 2
    left = jnp.concatenate([x[turn : turn + 1] for x in blocks], axis=0)
    right = jnp.concatenate([x[turn - 1 : turn] for x in blocks], axis=0)
    odd = lax.rem(az_ref[0], 2) == 1
    inner_edge_ref[...] = jnp.where(odd, left, right).astype(BF16)
    outer_edge_ref[...] = jnp.where(odd, right, left).astype(BF16)


def middle_body(
    keys_ref,
    values_ref,
    joined_ends_ref,
    block_ref,
    q_ref,
    bias_ref,
    points_ref,
    side_ref,
    w_out_ref,
    w_hid_ref,
    w_down_ref,
    joined_ref,
    near_ref,
    far_ref,
    score_ref,
    weight_ref,
    att_ref,
):
    attend(
        keys_ref[...], values_ref[...], q_ref, bias_ref, score_ref, weight_ref, att_ref, 0
    )
    half = block_ref.shape[1]
    turn = half // 2
    joined = join(
        points_ref, side_ref, att_ref, w_out_ref, w_hid_ref, w_down_ref, 0, (half, half)
    )
    for at, (x, ref) in enumerate(zip(joined, (near_ref, far_ref))):
        joined_ref[at, turn : turn + half] = x
        joined_ref[at, turn + half :] = joined_ends_ref[at, :turn]
        joined_ref[at, :turn] = joined_ends_ref[at, turn:]
        ref[turn : turn + half] = rms(x).astype(BF16)
        ref[turn + half : 2 * half] = block_ref[at, :turn]
        ref[:turn] = block_ref[at, turn:]


def pack_body(az_ref, inner_ref, outer_ref, near_in, far_in, near_ref, far_ref):
    del near_in, far_in
    odd = lax.rem(az_ref[0], 2) == 1
    inner, outer = inner_ref[...].astype(F32), outer_ref[...].astype(F32)
    right = jnp.where(odd, outer, inner)
    left = jnp.where(odd, inner, outer)
    cols, width = near_ref.shape[0] - PAD, near_ref.shape[1]
    row = lax.broadcasted_iota(jnp.int32, (PAD, width), 0)
    for at, ref in enumerate((near_ref, far_ref)):
        rows = jnp.where(row == 0, right[at : at + 1], 0.0)
        rows = jnp.where(row == PAD - 1, left[at : at + 1], rows)
        ref[cols:, :] = rows.astype(BF16)


def conv_rows(pairs, cols):
    taps = []
    for dc in range(3):
        total = None
        for x, w_ref, base in pairs:
            part = dot(x, w_ref[base + dc])
            total = part if total is None else total + part
        taps.append(total)
    length = taps[0].shape[0]
    shifted = taps[1] + pltpu.roll(taps[0], 1, 0) + pltpu.roll(taps[2], length - 1, 0)
    return shifted[:cols]


def inside_body(el_ref, near_ref, far_ref, joined_ref, w_ref, out_ref):
    odd = lax.rem(el_ref[0], 2)
    cols = joined_ref.shape[1]
    near, far = near_ref[...], far_ref[...]
    out_ref[0] = joined_ref[0] + conv_rows([(near, w_ref, 3), (far, w_ref, 6 * odd)], cols)
    out_ref[1] = joined_ref[1] + conv_rows([(far, w_ref, 3), (near, w_ref, 6 - 6 * odd)], cols)


def near_border_body(el_ref, near_ref, part_ref, w_ref, out_ref):
    odd = lax.rem(el_ref[0], 2)
    near = part_ref[0] + conv_rows([(near_ref[...], w_ref, 6 - 6 * odd)], part_ref.shape[1])
    out_ref[...] = near.astype(BF16)


def far_border_body(el_ref, near_ref, far_ref, part_ref, w_ref, out_hbm, row_ref, sems, *, last):
    el = el_ref[0]
    odd = lax.rem(el, 2)
    first = pltpu.make_async_copy(near_ref, out_hbm.at[1 - odd], sems.at[0])
    first.start()
    far = conv_rows([(far_ref[...], w_ref, 6 * odd)], part_ref.shape[1])
    ends = jnp.logical_or(el == 0, el == last)
    row_ref[...] = (part_ref[1] + jnp.where(ends, 0.0, far)).astype(BF16)
    second = pltpu.make_async_copy(row_ref, out_hbm.at[odd], sems.at[1])
    second.start()
    first.wait()
    second.wait()


def per_device(
    points,
    skip,
    tokens,
    send_slots,
    recv_idx,
    w_query,
    w_key,
    w_value,
    w_out,
    w_hid,
    w_skip,
    w_down,
    w_conv,
):
    rows, cols, width = points.shape
    count = rows * cols
    own_tokens = tokens[0, 0]
    slots = send_slots[0, 0]
    offsets, groups, capacity = slots.shape
    table = offsets * groups * capacity
    el = lax.axis_index("el").astype(jnp.int32).reshape(1)
    az = lax.axis_index("az").astype(jnp.int32).reshape(1)
    shape = jax.ShapeDtypeStruct
    dma = pltpu.SemaphoreType.DMA
    sent = call(
        gather_body,
        [shape((offsets, capacity, width), BF16)] * groups,
        [el, az, own_tokens, slots],
        "gather",
        (2 * table * own_tokens.shape[0] * width, 0),
        [SMEM, SMEM, HBM, HBM],
        [VMEM(own_tokens.shape, BF16), VMEM(slots.shape, jnp.int32), dma((2,))],
    )
    got = []
    for block, step in zip(sent, swap_order(groups)):
        got.append(swap(block, "el", lambda i, n, step=step: i ^ step) if step else block)
    pieces = []
    for piece in range(offsets):
        bundle = jnp.concatenate([block[piece] for block in got], axis=0)
        pieces.append(swap(bundle, "az", MATCHES[piece]) if piece else bundle)
    held = [w_query, w_skip, w_key, w_value, w_out, w_hid, w_down, w_conv]
    idx = jnp.swapaxes(recv_idx, 1, 2)
    bias, points_v, skip_v, *held = call(
        functools.partial(load_body, groups=groups, capacity=capacity, held=len(held)),
        [
            shape((table, count), F32),
            shape((count, width), BF16),
            shape((count, width), BF16),
        ]
        + [shape(w.shape, BF16) for w in held],
        [el, az, points, skip, idx] + held,
        "load",
        (table * count * 48, table * count),
        [SMEM, SMEM] + [HBM] * (3 + len(held)),
        [VMEM(idx.shape, jnp.int32), dma((14 + len(held),))],
    )
    query_t, side = call(
        query_body,
        [shape((width, count), BF16), shape((count, w_skip.shape[1]), F32)],
        [points_v, skip_v, held[0], held[1], pieces[0]],
        "query",
        (2 * count * width * 5 * width, 0),
    )
    w_key, w_value, w_out, w_hid, w_down, w_conv = held[2:]
    half = cols // 2
    work = (10 * table * cols * width + 18 * cols * width * width, table * cols * HEADS)
    room = [
        VMEM((HEADS, table, cols), F32),
        VMEM((HEADS, table, cols), BF16),
        VMEM((width, cols), BF16),
    ]
    shared = [query_t, bias, points_v, side, w_out, w_hid, w_down]
    joined_ends, blocks, inner_edge, outer_edge, keys, values = call(
        functools.partial(ends_body, pieces=len(pieces)),
        [
            shape((rows, half, width), F32),
            shape((rows, half, width), BF16),
            shape((2, width), BF16),
            shape((2, width), BF16),
            shape((table, width), BF16),
            shape((width, table), BF16),
        ],
        [az] + pieces + [w_key, w_value] + shared,
        "ends",
        work,
        [SMEM] + [VMEM] * (len(pieces) + 2 + len(shared)),
        room,
    )
    outer_got = swap(outer_edge, "az", next_chip)
    inner_got = swap(inner_edge, "az", same_chip)
    joined, near, far = call(
        middle_body,
        [
            shape((rows, cols, width), F32),
            shape((cols + PAD, width), BF16),
            shape((cols + PAD, width), BF16),
        ],
        [keys, values, joined_ends, blocks] + shared,
        "middle",
        work,
        None,
        room,
    )
    near, far = call(
        pack_body,
        [shape((cols + PAD, width), BF16)] * 2,
        [az, inner_got, outer_got, near, far],
        "pack",
        (4 * PAD * width, 0),
        [SMEM] + [VMEM] * 4,
        (),
        {3: 0, 4: 1},
    )
    far_got = swap(far, "el", next_chip)
    near_got = swap(near, "el", same_chip)
    (partial,) = call(
        inside_body,
        [shape((rows, cols, width), F32)],
        [el, near, far, joined, w_conv],
        "inside",
        (2 * count * width * width * 6, 0),
        [SMEM] + [VMEM] * 4,
    )
    (near_row,) = call(
        near_border_body,
        [shape((cols, width), BF16)],
        [el, near_got, partial, w_conv],
        "near_border",
        (cols * width * width * 6, 0),
        [SMEM] + [VMEM] * 3,
    )
    (out,) = call(
        functools.partial(far_border_body, last=lax.axis_size("el") - 1),
        [shape((rows, cols, width), BF16)],
        [el, near_row, far_got, partial, w_conv],
        "far_border",
        (cols * width * width * 6, 0),
        [SMEM] + [VMEM] * 4,
        [VMEM((cols, width), BF16), dma((2,))],
        out_space=HBM,
    )
    return out


def solution(mesh):
    return jax.shard_map(
        per_device,
        mesh=mesh,
        in_specs=(
            P("el", "az", None),
            P("el", "az", None),
            P("az", "el", None, None),
            P("az", "el", None, None, None),
            P("el", "az", None),
            P(),
            P(),
            P(),
            P(),
            P(),
            P(),
            P(),
            P(),
        ),
        out_specs=P("el", "az", None),
        check_vma=False,
    )
```

```python
import functools
import math

import jax
import jax.numpy as jnp
from jax import lax
from jax.experimental import pallas as pl
from jax.experimental.pallas import tpu as pltpu
from jax.sharding import PartitionSpec as P

HEADS = 8
REACH = 2
PAD = 16
BF16 = jnp.bfloat16
F32 = jnp.float32
VMEM = pltpu.VMEM
SMEM = pltpu.SMEM
HBM = pltpu.HBM


def same_chip(i, n):
    return i ^ 1


def next_chip(i, n):
    return (i + 1 if i % 2 else i - 1) % n


def two_on(i, n):
    return (i + 2 if i // 2 % 2 == 0 else i - 2) % n


def two_back(i, n):
    return (i - 2 if i // 2 % 2 == 0 else i + 2) % n


def swap(x, axis, partner):
    n = lax.axis_size(axis)
    return lax.ppermute(x, axis, [(i, partner(i, n)) for i in range(n)])


def swap_inner(x):
    columns, count = lax.axis_size("az"), lax.axis_size("el")
    pairs = []
    for az in range(columns):
        for el in range(count):
            if el in (0, count - 1):
                to = same_chip(az, columns) * count + el
            else:
                to = az * count + next_chip(el, count)
            pairs.append((az * count + el, to))
    return lax.ppermute(x, ("az", "el"), pairs)


def sent_offset(az, piece):
    odd, odd_chip = lax.rem(az, 2), lax.rem(lax.div(az, 2), 2)
    return (REACH, 4 * odd_chip, 1 + 2 * odd, 4 - 4 * odd_chip, 3 - 2 * odd)[piece]


MATCHES = (None, two_back, next_chip, two_on, same_chip)


def dot(a, b, contract=((1,), (0,))):
    return lax.dot_general(a, b, (contract, ((), ())), preferred_element_type=F32)


def rms(x):
    return x * lax.rsqrt(jnp.mean(x * x, axis=-1, keepdims=True) + 1e-06)


def call(body, outs, ins, name, cost, spaces=None, scratch=(), aliases=None, out_space=VMEM):
    spaces = spaces or [VMEM] * len(ins)
    flops, transcendentals = cost
    moved = sum(x.size * x.dtype.itemsize for x in list(ins) + list(outs))
    ins = [
        pltpu.with_memory_space_constraint(x, HBM) if s == HBM else x
        for x, s in zip(ins, spaces)
    ]
    return pl.pallas_call(
        body,
        out_shape=outs,
        in_specs=[pl.BlockSpec(memory_space=s) for s in spaces],
        out_specs=[pl.BlockSpec(memory_space=out_space) for _ in outs],
        scratch_shapes=list(scratch),
        input_output_aliases=aliases or {},
        compiler_params=pltpu.CompilerParams(vmem_limit_bytes=32 * 1024 * 1024),
        cost_estimate=pl.CostEstimate(
            flops=flops, bytes_accessed=moved, transcendentals=transcendentals
        ),
        name=name,
    )(*ins)


def swap_order(groups):
    return sorted(range(groups), key=lambda s: (s > 0, -s.bit_count(), s))


def gather_body(el_ref, az_ref, tokens_hbm, slots_hbm, *refs):
    out_refs, (tokens_ref, slots_ref, sems) = refs[:-3], refs[-3:]
    copies = [
        pltpu.make_async_copy(tokens_hbm, tokens_ref, sems.at[0]),
        pltpu.make_async_copy(slots_hbm, slots_ref, sems.at[1]),
    ]
    for c in copies:
        c.start()
    offsets, groups, capacity = slots_ref.shape
    rows = tokens_ref.shape[0]
    el, az = el_ref[0], az_ref[0]
    eye = lax.broadcasted_iota(jnp.int32, (capacity, capacity), 0) == lax.broadcasted_iota(
        jnp.int32, (capacity, capacity), 1
    )
    lane = lax.broadcasted_iota(jnp.int32, (capacity, rows), 1).astype(F32)
    for c in copies:
        c.wait()
    tokens = tokens_ref[...]
    for place, step in enumerate(swap_order(groups)):
        target = lax.bitwise_xor(el, step)
        picks = []
        for piece in range(offsets):
            row = slots_ref[sent_offset(az, piece), pl.ds(target, 1), :].astype(F32)
            spread = jnp.broadcast_to(row, (capacity, capacity))
            column = jnp.sum(jnp.where(eye, spread, 0.0), axis=-1, keepdims=True)
            picks.append(jnp.where(column == lane, 1.0, 0.0))
        one_hot = jnp.concatenate(picks, axis=0).astype(BF16)
        chosen = dot(one_hot, tokens).astype(BF16)
        out_refs[place][...] = chosen.reshape(out_refs[place].shape)


def load_body(*refs, groups, capacity, held):
    el_ref, az_ref, points_hbm, skip_hbm, idx_hbm = refs[:5]
    held_hbm = refs[5 : 5 + held]
    bias_ref, points_ref, skip_ref = refs[5 + held : 8 + held]
    held_refs = refs[8 + held : 8 + 2 * held]
    idx_ref, sems = refs[8 + 2 * held :]
    el, az = el_ref[0], az_ref[0]
    even = 1 - lax.rem(el, 2)
    cols = points_ref.shape[0] // 2
    count = 2 * cols
    first, later = [], []
    turn, half = cols // 4, cols // 2
    spans = []
    for r, at in enumerate((even, 1 - even)):
        spans.append((at, turn, r * half, half))
        spans.append((at, 3 * turn, (2 + r) * half, turn))
        spans.append((at, 0, (2 + r) * half + turn, turn))
    for r, at in enumerate((even, 1 - even)):
        first.append(pltpu.make_async_copy(idx_hbm.at[at], idx_ref.at[r], sems.at[r]))
    for r, (at, low, to, size) in enumerate(spans):
        rows, place = pl.ds(low, size), pl.ds(to, size)
        later.append(
            pltpu.make_async_copy(points_hbm.at[at, rows], points_ref.at[place], sems.at[2 + r])
        )
        later.append(
            pltpu.make_async_copy(skip_hbm.at[at, rows], skip_ref.at[place], sems.at[8 + r])
        )
    for k in range(held):
        later.append(pltpu.make_async_copy(held_hbm[k], held_refs[k], sems.at[14 + k]))
    for c in first + later:
        c.start()
    for c in first:
        c.wait()
    for r in range(2):
        idx_ref[r] = pltpu.roll(idx_ref[r], cols - turn, 1)
    near = idx_ref.shape[1]
    lanes = half
    for piece in range(bias_ref.shape[0] // (groups * capacity)):
        offset = 2 * REACH - sent_offset(az, piece)
        for block, step in enumerate(swap_order(groups)):
            source = lax.bitwise_xor(el, step)
            low = (offset * groups + source) * capacity
            slot = low + lax.broadcasted_iota(jnp.int32, (capacity, lanes), 0)
            place = (piece * groups + block) * capacity
            for start in range(0, count, lanes):
                row, col = start // half % 2, start // cols * half
                total = jnp.zeros((capacity, lanes), F32)
                for n in range(near):
                    index = idx_ref[row, n : n + 1, col : col + lanes]
                    total = total + jnp.where(slot == index, 1.0, 0.0)
                bias_ref[place : place + capacity, start : start + lanes] = jnp.log2(total)
    for c in later:
        c.wait()


def query_body(points_ref, skip_ref, w_query_ref, w_skip_ref, after_ref, q_ref, side_ref):
    del after_ref
    scale = math.log2(math.e) / math.sqrt(q_ref.shape[0] // HEADS)
    query = dot(points_ref[...], w_query_ref[...]) * scale
    q_ref[...] = query.T.astype(BF16)
    side_ref[...] = dot(skip_ref[...], w_skip_ref[...])


def attend(keys, values_t, q_ref, bias_ref, score_ref, weight_ref, att_ref, first):
    table, width = keys.shape
    count = att_ref.shape[1]
    part = slice(first, first + count)
    head_width = width // HEADS
    lanes = 128
    for head in range(HEADS):
        low, high = head * head_width, (head + 1) * head_width
        score_ref[head] = dot(keys[:, low:high], q_ref[low:high, part]) + bias_ref[:, part]
    for head in range(HEADS):
        for start in range(0, count, lanes):
            x = score_ref[head, :, start : start + lanes]
            top = jnp.max(jnp.max(x.reshape(table // 64, 8, 8, lanes), axis=0), axis=0)
            top = jnp.max(top, axis=0, keepdims=True)
            weight_ref[head, :, start : start + lanes] = jnp.exp2(x - top).astype(BF16)
    ones = jnp.ones((16, table), BF16)
    for head in range(HEADS):
        low, high = head * head_width, (head + 1) * head_width
        lhs = jnp.concatenate([values_t[low:high, :], ones], axis=0)
        mixed = dot(lhs, weight_ref[head])
        scale = 1.0 / mixed[head_width : head_width + 1]
        att_ref[low:high, :] = (mixed[:head_width] * scale).astype(BF16)


def join(points_ref, side_ref, att_ref, w_out_ref, w_hid_ref, w_down_ref, first, sizes):
    c1 = math.sqrt(2.0 / math.pi)
    residuals, pres, out = [], [], []
    starts = [sum(sizes[:k]) for k in range(len(sizes))]
    for start, size in zip(starts, sizes):
        rows = slice(first + start, first + start + size)
        mixed = att_ref[:, start : start + size]
        residuals.append(
            points_ref[rows].astype(F32) + dot(mixed, w_out_ref[...], ((0,), (0,)))
        )
    for start, size, residual in zip(starts, sizes, residuals):
        rows = slice(first + start, first + start + size)
        pres.append(dot(rms(residual).astype(BF16), w_hid_ref[...]) + side_ref[rows])
    for residual, pre in zip(residuals, pres):
        half = 0.5 * pre
        inner = half + half * jnp.tanh(pre * (c1 + (c1 * 0.044715) * (pre * pre)))
        out.append(residual + dot(inner.astype(BF16), w_down_ref[...]))
    return out


def ends_body(az_ref, *refs, pieces):
    (
        w_key_ref,
        w_value_ref,
        q_ref,
        bias_ref,
        points_ref,
        side_ref,
        w_out_ref,
        w_hid_ref,
        w_down_ref,
        joined_ref,
        block_ref,
        inner_edge_ref,
        outer_edge_ref,
        keys_ref,
        values_ref,
        score_ref,
        weight_ref,
        att_ref,
    ) = refs[pieces:]
    received = jnp.concatenate([r[...] for r in refs[:pieces]], axis=0)
    keys = dot(received, w_key_ref[...]).astype(BF16)
    normed_tokens = rms(received.astype(F32)).astype(BF16)
    values_t = dot(w_value_ref[...], normed_tokens, ((0,), (1,))).astype(BF16)
    keys_ref[...], values_ref[...] = keys, values_t
    half = block_ref.shape[1]
    first = 2 * half
    attend(keys, values_t, q_ref, bias_ref, score_ref, weight_ref, att_ref, first)
    joined = join(
        points_ref, side_ref, att_ref, w_out_ref, w_hid_ref, w_down_ref, first, (half, half)
    )
    blocks = [rms(x) for x in joined]
    for at in range(2):
        joined_ref[at] = joined[at]
        block_ref[at] = blocks[at].astype(BF16)
    turn = half // 2
    left = jnp.concatenate([x[turn : turn + 1] for x in blocks], axis=0)
    right = jnp.concatenate([x[turn - 1 : turn] for x in blocks], axis=0)
    odd = lax.rem(az_ref[0], 2) == 1
    inner_edge_ref[...] = jnp.where(odd, left, right).astype(BF16)
    outer_edge_ref[...] = jnp.where(odd, right, left).astype(BF16)


def middle_body(
    keys_ref,
    values_ref,
    joined_ends_ref,
    block_ref,
    q_ref,
    bias_ref,
    points_ref,
    side_ref,
    w_out_ref,
    w_hid_ref,
    w_down_ref,
    joined_ref,
    near_ref,
    far_ref,
    score_ref,
    weight_ref,
    att_ref,
):
    attend(
        keys_ref[...], values_ref[...], q_ref, bias_ref, score_ref, weight_ref, att_ref, 0
    )
    half = block_ref.shape[1]
    turn = half // 2
    joined = join(
        points_ref, side_ref, att_ref, w_out_ref, w_hid_ref, w_down_ref, 0, (half, half)
    )
    for at, (x, ref) in enumerate(zip(joined, (near_ref, far_ref))):
        joined_ref[at, turn : turn + half] = x
        joined_ref[at, turn + half :] = joined_ends_ref[at, :turn]
        joined_ref[at, :turn] = joined_ends_ref[at, turn:]
        ref[turn : turn + half] = rms(x).astype(BF16)
        ref[turn + half : 2 * half] = block_ref[at, :turn]
        ref[:turn] = block_ref[at, turn:]


def pack_body(az_ref, inner_ref, outer_ref, near_in, far_in, near_ref, far_ref):
    del near_in, far_in
    odd = lax.rem(az_ref[0], 2) == 1
    inner, outer = inner_ref[...].astype(F32), outer_ref[...].astype(F32)
    right = jnp.where(odd, outer, inner)
    left = jnp.where(odd, inner, outer)
    cols, width = near_ref.shape[0] - PAD, near_ref.shape[1]
    row = lax.broadcasted_iota(jnp.int32, (PAD, width), 0)
    for at, ref in enumerate((near_ref, far_ref)):
        rows = jnp.where(row == 0, right[at : at + 1], 0.0)
        rows = jnp.where(row == PAD - 1, left[at : at + 1], rows)
        ref[cols:, :] = rows.astype(BF16)


def conv_rows(pairs, cols):
    taps = []
    for dc in range(3):
        total = None
        for x, w_ref, base in pairs:
            part = dot(x, w_ref[base + dc])
            total = part if total is None else total + part
        taps.append(total)
    length = taps[0].shape[0]
    shifted = taps[1] + pltpu.roll(taps[0], 1, 0) + pltpu.roll(taps[2], length - 1, 0)
    return shifted[:cols]


def inside_body(el_ref, near_ref, far_ref, joined_ref, w_ref, out_ref):
    odd = lax.rem(el_ref[0], 2)
    cols = joined_ref.shape[1]
    near, far = near_ref[...], far_ref[...]
    out_ref[0] = joined_ref[0] + conv_rows([(near, w_ref, 3), (far, w_ref, 6 * odd)], cols)
    out_ref[1] = joined_ref[1] + conv_rows([(far, w_ref, 3), (near, w_ref, 6 - 6 * odd)], cols)


def near_border_body(el_ref, near_ref, part_ref, w_ref, out_ref):
    odd = lax.rem(el_ref[0], 2)
    near = part_ref[0] + conv_rows([(near_ref[...], w_ref, 6 - 6 * odd)], part_ref.shape[1])
    out_ref[...] = near.astype(BF16)


def far_border_body(el_ref, near_ref, far_ref, part_ref, w_ref, out_hbm, row_ref, sems, *, last):
    el = el_ref[0]
    odd = lax.rem(el, 2)
    first = pltpu.make_async_copy(near_ref, out_hbm.at[1 - odd], sems.at[0])
    first.start()
    far = conv_rows([(far_ref[...], w_ref, 6 * odd)], part_ref.shape[1])
    ends = jnp.logical_or(el == 0, el == last)
    row_ref[...] = (part_ref[1] + jnp.where(ends, 0.0, far)).astype(BF16)
    second = pltpu.make_async_copy(row_ref, out_hbm.at[odd], sems.at[1])
    second.start()
    first.wait()
    second.wait()


def per_device(
    points,
    skip,
    tokens,
    send_slots,
    recv_idx,
    w_query,
    w_key,
    w_value,
    w_out,
    w_hid,
    w_skip,
    w_down,
    w_conv,
):
    rows, cols, width = points.shape
    count = rows * cols
    own_tokens = tokens[0, 0]
    slots = send_slots[0, 0]
    offsets, groups, capacity = slots.shape
    table = offsets * groups * capacity
    el = lax.axis_index("el").astype(jnp.int32).reshape(1)
    az = lax.axis_index("az").astype(jnp.int32).reshape(1)
    shape = jax.ShapeDtypeStruct
    dma = pltpu.SemaphoreType.DMA
    sent = call(
        gather_body,
        [shape((offsets, capacity, width), BF16)] * groups,
        [el, az, own_tokens, slots],
        "gather",
        (2 * table * own_tokens.shape[0] * width, 0),
        [SMEM, SMEM, HBM, HBM],
        [VMEM(own_tokens.shape, BF16), VMEM(slots.shape, jnp.int32), dma((2,))],
    )
    got = []
    for block, step in zip(sent, swap_order(groups)):
        got.append(swap(block, "el", lambda i, n, step=step: i ^ step) if step else block)
    pieces = []
    for piece in range(offsets):
        bundle = jnp.concatenate([block[piece] for block in got], axis=0)
        pieces.append(swap(bundle, "az", MATCHES[piece]) if piece else bundle)
    held = [w_query, w_skip, w_key, w_value, w_out, w_hid, w_down, w_conv]
    idx = jnp.swapaxes(recv_idx, 1, 2)
    bias, points_v, skip_v, *held = call(
        functools.partial(load_body, groups=groups, capacity=capacity, held=len(held)),
        [
            shape((table, count), F32),
            shape((count, width), BF16),
            shape((count, width), BF16),
        ]
        + [shape(w.shape, BF16) for w in held],
        [el, az, points, skip, idx] + held,
        "load",
        (table * count * 48, table * count),
        [SMEM, SMEM] + [HBM] * (3 + len(held)),
        [VMEM(idx.shape, jnp.int32), dma((14 + len(held),))],
    )
    query_t, side = call(
        query_body,
        [shape((width, count), BF16), shape((count, w_skip.shape[1]), F32)],
        [points_v, skip_v, held[0], held[1], pieces[0]],
        "query",
        (2 * count * width * 5 * width, 0),
    )
    w_key, w_value, w_out, w_hid, w_down, w_conv = held[2:]
    half = cols // 2
    work = (10 * table * cols * width + 18 * cols * width * width, table * cols * HEADS)
    room = [
        VMEM((HEADS, table, cols), F32),
        VMEM((HEADS, table, cols), BF16),
        VMEM((width, cols), BF16),
    ]
    shared = [query_t, bias, points_v, side, w_out, w_hid, w_down]
    joined_ends, blocks, inner_edge, outer_edge, keys, values = call(
        functools.partial(ends_body, pieces=len(pieces)),
        [
            shape((rows, half, width), F32),
            shape((rows, half, width), BF16),
            shape((2, width), BF16),
            shape((2, width), BF16),
            shape((table, width), BF16),
            shape((width, table), BF16),
        ],
        [az] + pieces + [w_key, w_value] + shared,
        "ends",
        work,
        [SMEM] + [VMEM] * (len(pieces) + 2 + len(shared)),
        room,
    )
    outer_got = swap(outer_edge, "az", next_chip)
    inner_got = swap(inner_edge, "az", same_chip)
    joined, near, far = call(
        middle_body,
        [
            shape((rows, cols, width), F32),
            shape((cols + PAD, width), BF16),
            shape((cols + PAD, width), BF16),
        ],
        [keys, values, joined_ends, blocks] + shared,
        "middle",
        work,
        None,
        room,
    )
    near, far = call(
        pack_body,
        [shape((cols + PAD, width), BF16)] * 2,
        [az, inner_got, outer_got, near, far],
        "pack",
        (4 * PAD * width, 0),
        [SMEM] + [VMEM] * 4,
        (),
        {3: 0, 4: 1},
    )
    far_got = swap_inner(far)
    near_got = swap(near, "el", same_chip)
    (partial,) = call(
        inside_body,
        [shape((rows, cols, width), F32)],
        [el, near, far, joined, w_conv],
        "inside",
        (2 * count * width * width * 6, 0),
        [SMEM] + [VMEM] * 4,
    )
    (near_row,) = call(
        near_border_body,
        [shape((cols, width), BF16)],
        [el, near_got, partial, w_conv],
        "near_border",
        (cols * width * width * 6, 0),
        [SMEM] + [VMEM] * 3,
    )
    (out,) = call(
        functools.partial(far_border_body, last=lax.axis_size("el") - 1),
        [shape((rows, cols, width), BF16)],
        [el, near_row, far_got, partial, w_conv],
        "far_border",
        (cols * width * width * 6, 0),
        [SMEM] + [VMEM] * 4,
        [VMEM((cols, width), BF16), dma((2,))],
        out_space=HBM,
    )
    return out


def solution(mesh):
    return jax.shard_map(
        per_device,
        mesh=mesh,
        in_specs=(
            P("el", "az", None),
            P("el", "az", None),
            P("az", "el", None, None),
            P("az", "el", None, None, None),
            P("el", "az", None),
            P(),
            P(),
            P(),
            P(),
            P(),
            P(),
            P(),
            P(),
        ),
        out_specs=P("el", "az", None),
        check_vma=False,
    )
```

```python
import functools
import math

import jax
import jax.numpy as jnp
from jax import lax
from jax.experimental import pallas as pl
from jax.experimental.pallas import tpu as pltpu
from jax.sharding import PartitionSpec as P

HEADS = 8
REACH = 2
PAD = 16
BF16 = jnp.bfloat16
F32 = jnp.float32
VMEM = pltpu.VMEM
SMEM = pltpu.SMEM
HBM = pltpu.HBM


def same_chip(i, n):
    return i ^ 1


def next_chip(i, n):
    return (i + 1 if i % 2 else i - 1) % n


def two_on(i, n):
    return (i + 2 if i // 2 % 2 == 0 else i - 2) % n


def two_back(i, n):
    return (i - 2 if i // 2 % 2 == 0 else i + 2) % n


def swap(x, axis, partner):
    n = lax.axis_size(axis)
    return lax.ppermute(x, axis, [(i, partner(i, n)) for i in range(n)])


def swap_inner(x):
    columns, count = lax.axis_size("az"), lax.axis_size("el")
    pairs = []
    for az in range(columns):
        for el in range(count):
            if el in (0, count - 1):
                to = same_chip(az, columns) * count + el
            else:
                to = az * count + next_chip(el, count)
            pairs.append((az * count + el, to))
    return lax.ppermute(x, ("az", "el"), pairs)


def sent_offset(az, piece):
    odd, odd_chip = lax.rem(az, 2), lax.rem(lax.div(az, 2), 2)
    return (REACH, 1 + 2 * odd, 4 * odd_chip, 4 - 4 * odd_chip, 3 - 2 * odd)[piece]


MATCHES = (None, next_chip, two_back, two_on, same_chip)


def dot(a, b, contract=((1,), (0,))):
    return lax.dot_general(a, b, (contract, ((), ())), preferred_element_type=F32)


def rms(x):
    return x * lax.rsqrt(jnp.mean(x * x, axis=-1, keepdims=True) + 1e-06)


def call(body, outs, ins, name, cost, spaces=None, scratch=(), aliases=None, out_space=VMEM):
    spaces = spaces or [VMEM] * len(ins)
    flops, transcendentals = cost
    moved = sum(x.size * x.dtype.itemsize for x in list(ins) + list(outs))
    ins = [
        pltpu.with_memory_space_constraint(x, HBM) if s == HBM else x
        for x, s in zip(ins, spaces)
    ]
    return pl.pallas_call(
        body,
        out_shape=outs,
        in_specs=[pl.BlockSpec(memory_space=s) for s in spaces],
        out_specs=[pl.BlockSpec(memory_space=out_space) for _ in outs],
        scratch_shapes=list(scratch),
        input_output_aliases=aliases or {},
        compiler_params=pltpu.CompilerParams(vmem_limit_bytes=32 * 1024 * 1024),
        cost_estimate=pl.CostEstimate(
            flops=flops, bytes_accessed=moved, transcendentals=transcendentals
        ),
        name=name,
    )(*ins)


def swap_order(groups):
    return sorted(range(groups), key=lambda s: (s > 0, -s.bit_count(), s))


def gather_body(el_ref, az_ref, tokens_hbm, slots_hbm, *refs):
    out_refs, (tokens_ref, slots_ref, sems) = refs[:-3], refs[-3:]
    copies = [
        pltpu.make_async_copy(tokens_hbm, tokens_ref, sems.at[0]),
        pltpu.make_async_copy(slots_hbm, slots_ref, sems.at[1]),
    ]
    for c in copies:
        c.start()
    offsets, groups, capacity = slots_ref.shape
    rows = tokens_ref.shape[0]
    el, az = el_ref[0], az_ref[0]
    eye = lax.broadcasted_iota(jnp.int32, (capacity, capacity), 0) == lax.broadcasted_iota(
        jnp.int32, (capacity, capacity), 1
    )
    lane = lax.broadcasted_iota(jnp.int32, (capacity, rows), 1).astype(F32)
    for c in copies:
        c.wait()
    tokens = tokens_ref[...]
    for place, step in enumerate(swap_order(groups)):
        target = lax.bitwise_xor(el, step)
        picks = []
        for piece in range(offsets):
            row = slots_ref[sent_offset(az, piece), pl.ds(target, 1), :].astype(F32)
            spread = jnp.broadcast_to(row, (capacity, capacity))
            column = jnp.sum(jnp.where(eye, spread, 0.0), axis=-1, keepdims=True)
            picks.append(jnp.where(column == lane, 1.0, 0.0))
        one_hot = jnp.concatenate(picks, axis=0).astype(BF16)
        chosen = dot(one_hot, tokens).astype(BF16)
        out_refs[place][...] = chosen.reshape(out_refs[place].shape)


def load_body(*refs, groups, capacity, held):
    el_ref, az_ref, points_hbm, skip_hbm, idx_hbm = refs[:5]
    held_hbm = refs[5 : 5 + held]
    bias_ref, points_ref, skip_ref = refs[5 + held : 8 + held]
    held_refs = refs[8 + held : 8 + 2 * held]
    idx_ref, sems = refs[8 + 2 * held :]
    el, az = el_ref[0], az_ref[0]
    even = 1 - lax.rem(el, 2)
    cols = points_ref.shape[0] // 2
    count = 2 * cols
    first, later = [], []
    turn, half = cols // 4, cols // 2
    spans = []
    for r, at in enumerate((even, 1 - even)):
        spans.append((at, turn, r * half, half))
        spans.append((at, 3 * turn, (2 + r) * half, turn))
        spans.append((at, 0, (2 + r) * half + turn, turn))
    for r, at in enumerate((even, 1 - even)):
        first.append(pltpu.make_async_copy(idx_hbm.at[at], idx_ref.at[r], sems.at[r]))
    for r, (at, low, to, size) in enumerate(spans):
        rows, place = pl.ds(low, size), pl.ds(to, size)
        later.append(
            pltpu.make_async_copy(points_hbm.at[at, rows], points_ref.at[place], sems.at[2 + r])
        )
        later.append(
            pltpu.make_async_copy(skip_hbm.at[at, rows], skip_ref.at[place], sems.at[8 + r])
        )
    for k in range(held):
        later.append(pltpu.make_async_copy(held_hbm[k], held_refs[k], sems.at[14 + k]))
    for c in first + later:
        c.start()
    for c in first:
        c.wait()
    for r in range(2):
        idx_ref[r] = pltpu.roll(idx_ref[r], cols - turn, 1)
    near = idx_ref.shape[1]
    lanes = half
    for piece in range(bias_ref.shape[0] // (groups * capacity)):
        offset = 2 * REACH - sent_offset(az, piece)
        for block, step in enumerate(swap_order(groups)):
            source = lax.bitwise_xor(el, step)
            low = (offset * groups + source) * capacity
            slot = low + lax.broadcasted_iota(jnp.int32, (capacity, lanes), 0)
            place = (piece * groups + block) * capacity
            for start in range(0, count, lanes):
                row, col = start // half % 2, start // cols * half
                total = jnp.zeros((capacity, lanes), F32)
                for n in range(near):
                    index = idx_ref[row, n : n + 1, col : col + lanes]
                    total = total + jnp.where(slot == index, 1.0, 0.0)
                bias_ref[place : place + capacity, start : start + lanes] = jnp.log2(total)
    for c in later:
        c.wait()


def query_body(points_ref, skip_ref, w_query_ref, w_skip_ref, after_ref, q_ref, side_ref):
    del after_ref
    scale = math.log2(math.e) / math.sqrt(q_ref.shape[0] // HEADS)
    query = dot(points_ref[...], w_query_ref[...]) * scale
    q_ref[...] = query.T.astype(BF16)
    side_ref[...] = dot(skip_ref[...], w_skip_ref[...])


def attend(keys, values_t, q_ref, bias_ref, score_ref, weight_ref, att_ref, first):
    table, width = keys.shape
    count = att_ref.shape[1]
    part = slice(first, first + count)
    head_width = width // HEADS
    lanes = 128
    for head in range(HEADS):
        low, high = head * head_width, (head + 1) * head_width
        score_ref[head] = dot(keys[:, low:high], q_ref[low:high, part]) + bias_ref[:, part]
    for head in range(HEADS):
        for start in range(0, count, lanes):
            x = score_ref[head, :, start : start + lanes]
            top = jnp.max(jnp.max(x.reshape(table // 64, 8, 8, lanes), axis=0), axis=0)
            top = jnp.max(top, axis=0, keepdims=True)
            weight_ref[head, :, start : start + lanes] = jnp.exp2(x - top).astype(BF16)
    ones = jnp.ones((16, table), BF16)
    for head in range(HEADS):
        low, high = head * head_width, (head + 1) * head_width
        lhs = jnp.concatenate([values_t[low:high, :], ones], axis=0)
        mixed = dot(lhs, weight_ref[head])
        scale = 1.0 / mixed[head_width : head_width + 1]
        att_ref[low:high, :] = (mixed[:head_width] * scale).astype(BF16)


def join(points_ref, side_ref, att_ref, w_out_ref, w_hid_ref, w_down_ref, first, sizes):
    c1 = math.sqrt(2.0 / math.pi)
    residuals, pres, out = [], [], []
    starts = [sum(sizes[:k]) for k in range(len(sizes))]
    for start, size in zip(starts, sizes):
        rows = slice(first + start, first + start + size)
        mixed = att_ref[:, start : start + size]
        residuals.append(
            points_ref[rows].astype(F32) + dot(mixed, w_out_ref[...], ((0,), (0,)))
        )
    for start, size, residual in zip(starts, sizes, residuals):
        rows = slice(first + start, first + start + size)
        pres.append(dot(rms(residual).astype(BF16), w_hid_ref[...]) + side_ref[rows])
    for residual, pre in zip(residuals, pres):
        half = 0.5 * pre
        inner = half + half * jnp.tanh(pre * (c1 + (c1 * 0.044715) * (pre * pre)))
        out.append(residual + dot(inner.astype(BF16), w_down_ref[...]))
    return out


def ends_body(az_ref, *refs, pieces):
    (
        w_key_ref,
        w_value_ref,
        q_ref,
        bias_ref,
        points_ref,
        side_ref,
        w_out_ref,
        w_hid_ref,
        w_down_ref,
        joined_ref,
        block_ref,
        inner_edge_ref,
        outer_edge_ref,
        keys_ref,
        values_ref,
        score_ref,
        weight_ref,
        att_ref,
    ) = refs[pieces:]
    received = jnp.concatenate([r[...] for r in refs[:pieces]], axis=0)
    keys = dot(received, w_key_ref[...]).astype(BF16)
    normed_tokens = rms(received.astype(F32)).astype(BF16)
    values_t = dot(w_value_ref[...], normed_tokens, ((0,), (1,))).astype(BF16)
    keys_ref[...], values_ref[...] = keys, values_t
    half = block_ref.shape[1]
    first = 2 * half
    attend(keys, values_t, q_ref, bias_ref, score_ref, weight_ref, att_ref, first)
    joined = join(
        points_ref, side_ref, att_ref, w_out_ref, w_hid_ref, w_down_ref, first, (half, half)
    )
    blocks = [rms(x) for x in joined]
    for at in range(2):
        joined_ref[at] = joined[at]
        block_ref[at] = blocks[at].astype(BF16)
    turn = half // 2
    left = jnp.concatenate([x[turn : turn + 1] for x in blocks], axis=0)
    right = jnp.concatenate([x[turn - 1 : turn] for x in blocks], axis=0)
    odd = lax.rem(az_ref[0], 2) == 1
    inner_edge_ref[...] = jnp.where(odd, left, right).astype(BF16)
    outer_edge_ref[...] = jnp.where(odd, right, left).astype(BF16)


def middle_body(
    keys_ref,
    values_ref,
    joined_ends_ref,
    block_ref,
    q_ref,
    bias_ref,
    points_ref,
    side_ref,
    w_out_ref,
    w_hid_ref,
    w_down_ref,
    joined_ref,
    near_ref,
    far_ref,
    score_ref,
    weight_ref,
    att_ref,
):
    attend(
        keys_ref[...], values_ref[...], q_ref, bias_ref, score_ref, weight_ref, att_ref, 0
    )
    half = block_ref.shape[1]
    turn = half // 2
    joined = join(
        points_ref, side_ref, att_ref, w_out_ref, w_hid_ref, w_down_ref, 0, (half, half)
    )
    for at, (x, ref) in enumerate(zip(joined, (near_ref, far_ref))):
        joined_ref[at, turn : turn + half] = x
        joined_ref[at, turn + half :] = joined_ends_ref[at, :turn]
        joined_ref[at, :turn] = joined_ends_ref[at, turn:]
        ref[turn : turn + half] = rms(x).astype(BF16)
        ref[turn + half : 2 * half] = block_ref[at, :turn]
        ref[:turn] = block_ref[at, turn:]


def pack_body(az_ref, inner_ref, outer_ref, near_in, far_in, near_ref, far_ref):
    del near_in, far_in
    odd = lax.rem(az_ref[0], 2) == 1
    inner, outer = inner_ref[...].astype(F32), outer_ref[...].astype(F32)
    right = jnp.where(odd, outer, inner)
    left = jnp.where(odd, inner, outer)
    cols, width = near_ref.shape[0] - PAD, near_ref.shape[1]
    row = lax.broadcasted_iota(jnp.int32, (PAD, width), 0)
    for at, ref in enumerate((near_ref, far_ref)):
        rows = jnp.where(row == 0, right[at : at + 1], 0.0)
        rows = jnp.where(row == PAD - 1, left[at : at + 1], rows)
        ref[cols:, :] = rows.astype(BF16)


def conv_rows(pairs, cols):
    taps = []
    for dc in range(3):
        total = None
        for x, w_ref, base in pairs:
            part = dot(x, w_ref[base + dc])
            total = part if total is None else total + part
        taps.append(total)
    length = taps[0].shape[0]
    shifted = taps[1] + pltpu.roll(taps[0], 1, 0) + pltpu.roll(taps[2], length - 1, 0)
    return shifted[:cols]


def inside_body(el_ref, near_ref, far_ref, joined_ref, w_ref, out_ref):
    odd = lax.rem(el_ref[0], 2)
    cols = joined_ref.shape[1]
    near, far = near_ref[...], far_ref[...]
    out_ref[0] = joined_ref[0] + conv_rows([(near, w_ref, 3), (far, w_ref, 6 * odd)], cols)
    out_ref[1] = joined_ref[1] + conv_rows([(far, w_ref, 3), (near, w_ref, 6 - 6 * odd)], cols)


def near_border_body(el_ref, near_ref, part_ref, w_ref, out_ref):
    odd = lax.rem(el_ref[0], 2)
    near = part_ref[0] + conv_rows([(near_ref[...], w_ref, 6 - 6 * odd)], part_ref.shape[1])
    out_ref[...] = near.astype(BF16)


def far_border_body(el_ref, near_ref, far_ref, part_ref, w_ref, out_hbm, row_ref, sems, *, last):
    el = el_ref[0]
    odd = lax.rem(el, 2)
    first = pltpu.make_async_copy(near_ref, out_hbm.at[1 - odd], sems.at[0])
    first.start()
    far = conv_rows([(far_ref[...], w_ref, 6 * odd)], part_ref.shape[1])
    ends = jnp.logical_or(el == 0, el == last)
    row_ref[...] = (part_ref[1] + jnp.where(ends, 0.0, far)).astype(BF16)
    second = pltpu.make_async_copy(row_ref, out_hbm.at[odd], sems.at[1])
    second.start()
    first.wait()
    second.wait()


def per_device(
    points,
    skip,
    tokens,
    send_slots,
    recv_idx,
    w_query,
    w_key,
    w_value,
    w_out,
    w_hid,
    w_skip,
    w_down,
    w_conv,
):
    rows, cols, width = points.shape
    count = rows * cols
    own_tokens = tokens[0, 0]
    slots = send_slots[0, 0]
    offsets, groups, capacity = slots.shape
    table = offsets * groups * capacity
    el = lax.axis_index("el").astype(jnp.int32).reshape(1)
    az = lax.axis_index("az").astype(jnp.int32).reshape(1)
    shape = jax.ShapeDtypeStruct
    dma = pltpu.SemaphoreType.DMA
    sent = call(
        gather_body,
        [shape((offsets, capacity, width), BF16)] * groups,
        [el, az, own_tokens, slots],
        "gather",
        (2 * table * own_tokens.shape[0] * width, 0),
        [SMEM, SMEM, HBM, HBM],
        [VMEM(own_tokens.shape, BF16), VMEM(slots.shape, jnp.int32), dma((2,))],
    )
    got = []
    for block, step in zip(sent, swap_order(groups)):
        got.append(swap(block, "el", lambda i, n, step=step: i ^ step) if step else block)
    pieces = []
    for piece in range(offsets):
        bundle = jnp.concatenate([block[piece] for block in got], axis=0)
        pieces.append(swap(bundle, "az", MATCHES[piece]) if piece else bundle)
    held = [w_query, w_skip, w_key, w_value, w_out, w_hid, w_down, w_conv]
    idx = jnp.swapaxes(recv_idx, 1, 2)
    bias, points_v, skip_v, *held = call(
        functools.partial(load_body, groups=groups, capacity=capacity, held=len(held)),
        [
            shape((table, count), F32),
            shape((count, width), BF16),
            shape((count, width), BF16),
        ]
        + [shape(w.shape, BF16) for w in held],
        [el, az, points, skip, idx] + held,
        "load",
        (table * count * 48, table * count),
        [SMEM, SMEM] + [HBM] * (3 + len(held)),
        [VMEM(idx.shape, jnp.int32), dma((14 + len(held),))],
    )
    query_t, side = call(
        query_body,
        [shape((width, count), BF16), shape((count, w_skip.shape[1]), F32)],
        [points_v, skip_v, held[0], held[1], pieces[0]],
        "query",
        (2 * count * width * 5 * width, 0),
    )
    w_key, w_value, w_out, w_hid, w_down, w_conv = held[2:]
    half = cols // 2
    work = (10 * table * cols * width + 18 * cols * width * width, table * cols * HEADS)
    room = [
        VMEM((HEADS, table, cols), F32),
        VMEM((HEADS, table, cols), BF16),
        VMEM((width, cols), BF16),
    ]
    shared = [query_t, bias, points_v, side, w_out, w_hid, w_down]
    joined_ends, blocks, inner_edge, outer_edge, keys, values = call(
        functools.partial(ends_body, pieces=len(pieces)),
        [
            shape((rows, half, width), F32),
            shape((rows, half, width), BF16),
            shape((2, width), BF16),
            shape((2, width), BF16),
            shape((table, width), BF16),
            shape((width, table), BF16),
        ],
        [az] + pieces + [w_key, w_value] + shared,
        "ends",
        work,
        [SMEM] + [VMEM] * (len(pieces) + 2 + len(shared)),
        room,
    )
    outer_got = swap(outer_edge, "az", next_chip)
    inner_got = swap(inner_edge, "az", same_chip)
    joined, near, far = call(
        middle_body,
        [
            shape((rows, cols, width), F32),
            shape((cols + PAD, width), BF16),
            shape((cols + PAD, width), BF16),
        ],
        [keys, values, joined_ends, blocks] + shared,
        "middle",
        work,
        None,
        room,
    )
    near, far = call(
        pack_body,
        [shape((cols + PAD, width), BF16)] * 2,
        [az, inner_got, outer_got, near, far],
        "pack",
        (4 * PAD * width, 0),
        [SMEM] + [VMEM] * 4,
        (),
        {3: 0, 4: 1},
    )
    far_got = swap_inner(far)
    near_got = swap(near, "el", same_chip)
    (partial,) = call(
        inside_body,
        [shape((rows, cols, width), F32)],
        [el, near, far, joined, w_conv],
        "inside",
        (2 * count * width * width * 6, 0),
        [SMEM] + [VMEM] * 4,
    )
    (near_row,) = call(
        near_border_body,
        [shape((cols, width), BF16)],
        [el, near_got, partial, w_conv],
        "near_border",
        (cols * width * width * 6, 0),
        [SMEM] + [VMEM] * 3,
    )
    (out,) = call(
        functools.partial(far_border_body, last=lax.axis_size("el") - 1),
        [shape((rows, cols, width), BF16)],
        [el, near_row, far_got, partial, w_conv],
        "far_border",
        (cols * width * width * 6, 0),
        [SMEM] + [VMEM] * 4,
        [VMEM((cols, width), BF16), dma((2,))],
        out_space=HBM,
    )
    return out


def solution(mesh):
    return jax.shard_map(
        per_device,
        mesh=mesh,
        in_specs=(
            P("el", "az", None),
            P("el", "az", None),
            P("az", "el", None, None),
            P("az", "el", None, None, None),
            P("el", "az", None),
            P(),
            P(),
            P(),
            P(),
            P(),
            P(),
            P(),
            P(),
        ),
        out_specs=P("el", "az", None),
        check_vma=False,
    )
```
